512 devices in a mesh: grid: 128 (over z, x, core), layer: 4 (over y).
Axes of the slice: x: 4, y: 4, z: 16, core: 2. Of those that a mesh axis runs over, the one named last changes fastest.
Arguments:
- lower_inverse: bfloat16 [4, 256, 128, 128], P('layer', 'grid'), as said below
- upper_inverse: bfloat16 [4, 256, 128, 128], P('layer', 'grid'), as said below
- lower_link: bfloat16 [4, 256, 128, 128], P('layer', 'grid'), may hold values from -1 to 1
- upper_link: bfloat16 [4, 256, 128, 128], P('layer', 'grid'), may hold values from -1 to 1
- lower_root: bfloat16 [4, 256, 512, 128], P('layer', 'grid'), may hold values from -0.03125 to 0.03125
- upper_root: bfloat16 [4, 256, 128, 512], P('layer', 'grid'), may hold values from -0.125 to 0.125
- rhs_blocks: bfloat16 [4, 256, 128, 128], P('layer', 'grid'), may hold values from -0.29882812 to 0.29882812
- rhs_root: bfloat16 [512, 128], replicated, may hold values from -3 to 3
- root_lower_inverse: bfloat16 [512, 512], replicated, as said below
- root_upper_inverse: bfloat16 [512, 512], replicated, as said below
- live_counts: int32 [4, 128], P('layer', 'grid'), may hold values from 1 to 2
Outputs:
- solution: float32 [4, 256, 128, 128], P('layer', 'grid')
- root_solution: float32 [512, 128], P(None, 'grid')
The draws below stay inside these ranges and needn't reach their ends.
Inputs may be any that keep to these rules, and one draw needn't show every extreme that they name: `lower_inverse`: unit lower triangular. `upper_inverse`: upper triangular with diagonal entries between 0.5 and 1.5. `root_lower_inverse`: unit lower triangular. `root_upper_inverse`: upper triangular with diagonal entries between 0.5 and 1.5.
All inputs are finite; a program needn't handle non-finite values.
Results may differ from the reference program's by a relative error of at most 0.0003.
Values sent between devices are 32-bit elements; how exact they have to be, the bound alone decides.
No kernel may reach another device: no remote copies, remote signals or barrier semaphores. Data moves between devices by JAX's collectives and lax.ppermute only.
A program may use at most 128 MiB of HBM per device.

```python
import math
import jax
import jax.numpy as jnp
from jax import lax

W = 128
WR = 512
NRHS = 128
SND = 2
LAYERS = 4
SUPER = 256
N_GRID = 128


def chain_scale(keep, spread):
    live_steps = SUPER * (SND + 1) / (2.0 * SND)
    return keep ** (1.0 / live_steps) * math.exp(0.5 / W) / math.sqrt(spread * W)


def draw_lower_inverse(key, part):
    key = jax.random.fold_in(key, 11)
    shape = (LAYERS, SUPER, W, W)
    noise = jax.random.normal(key, shape, jnp.float32)
    strict = jnp.tril(noise, -1) * (0.5 / W ** 0.5)
    return (strict + jnp.eye(W, dtype=jnp.float32)).astype(jnp.bfloat16)


def draw_upper_inverse(key, part):
    key = jax.random.fold_in(key, 12)
    first, second = jax.random.split(key)
    shape = (LAYERS, SUPER, W, W)
    noise = jax.random.normal(first, shape, jnp.float32)
    diagonal = jax.random.uniform(second, (LAYERS, SUPER, W), jnp.float32, 0.5, 1.5)
    strict = jnp.triu(noise, 1) * (0.5 / W ** 0.5)
    return (strict + diagonal[..., None] * jnp.eye(W, dtype=jnp.float32)).astype(jnp.bfloat16)


def draw_lower_link(key, part):
    key = jax.random.fold_in(key, 15)
    shape = (LAYERS, SUPER, W, W)
    noise = jnp.clip(jax.random.normal(key, shape, jnp.float32), -4.0, 4.0)
    factor = chain_scale(0.1, 1.125)
    return (noise * factor).astype(jnp.bfloat16)


def draw_upper_link(key, part):
    key = jax.random.fold_in(key, 16)
    shape = (LAYERS, SUPER, W, W)
    noise = jnp.clip(jax.random.normal(key, shape, jnp.float32), -4.0, 4.0)
    factor = chain_scale(0.1, 1.208)
    return (noise * factor).astype(jnp.bfloat16)


def draw_root_lower_inverse(key, part):
    key = jax.random.fold_in(key, 13)
    noise = jax.random.normal(key, (WR, WR), jnp.float32)
    return (jnp.tril(noise, -1) * (0.5 / WR ** 0.5) + jnp.eye(WR, dtype=jnp.float32)).astype(jnp.bfloat16)


def draw_root_upper_inverse(key, part):
    key = jax.random.fold_in(key, 14)
    first, second = jax.random.split(key)
    noise = jax.random.normal(first, (WR, WR), jnp.float32)
    diagonal = jax.random.uniform(second, (WR,), jnp.float32, 0.5, 1.5)
    return (jnp.triu(noise, 1) * (0.5 / WR ** 0.5) + jnp.diag(diagonal)).astype(jnp.bfloat16)


def with_ends(result, own_key, smallest, largest):
    longest = result.shape.index(max(result.shape))
    spots = []
    for shift in (0, 1):
        where = [jax.random.randint(jax.random.fold_in(own_key, axis), (), 0, length) for axis, length in enumerate(result.shape)]
        where[longest] = (where[longest] + shift) % result.shape[longest]
        spots.append(tuple(where))
    return result.at[spots[0]].set(smallest).at[spots[1]].set(largest)


def shard_levels(stream_key, dims, shards, least, top_value):
    def one(position, blocks):
        draws = jax.random.uniform(jax.random.fold_in(jax.random.fold_in(stream_key, 6), position), (blocks,), jnp.float32, least / len(shards), top_value / len(shards))
        return jnp.repeat(jnp.exp(draws), dims[position] // blocks).reshape((-1,) + (1,) * (len(dims) - position - 1))

    gain = one(*shards[0])
    for cut in shards[1:]:
        gain = gain * one(*cut)
    return gain


def bell_draw(stream_key, extent, scale, limit, shards=(), kind=jnp.bfloat16):
    values = scale * jax.random.normal(stream_key, extent, jnp.float32)
    if shards:
        values = values * shard_levels(stream_key, extent, shards, -0.22, 0.18)
    return jnp.clip(values, -limit, limit).astype(kind)


def setup_inputs(seed: int = 0) -> dict:
    seeds = jax.random.split(jax.random.key(seed), 12)
    lower_inverse = draw_lower_inverse(jax.random.fold_in(seeds[11], 71), 0)
    upper_inverse = draw_upper_inverse(jax.random.fold_in(seeds[11], 71), 0)
    lower_link = draw_lower_link(jax.random.fold_in(seeds[11], 71), 0)
    upper_link = draw_upper_link(jax.random.fold_in(seeds[11], 71), 0)
    lower_root = bell_draw(seeds[4], (LAYERS, SUPER, WR, W), (W * SUPER * LAYERS // 4) ** -0.5, 0.03125, ((0, 4), (1, 128)))
    upper_root = bell_draw(seeds[5], (LAYERS, SUPER, W, WR), (4 * WR) ** -0.5, 0.125, ((0, 4), (1, 128)))
    rhs_blocks = bell_draw(seeds[6], (LAYERS, SUPER, W, NRHS), 0.05, 0.29882812, ((0, 4), (1, 128)))
    rhs_root = bell_draw(seeds[7], (WR, NRHS), 0.5, 3.0)
    root_lower_inverse = draw_root_lower_inverse(jax.random.fold_in(seeds[11], 71), 0)
    root_upper_inverse = draw_root_upper_inverse(jax.random.fold_in(seeds[11], 71), 0)
    live_counts = with_ends(jax.random.randint(seeds[10], (LAYERS, N_GRID), 1, SND + 1), jax.random.fold_in(seeds[10], 1), 1, SND).astype(jnp.int32)
    return dict(lower_inverse=lower_inverse, upper_inverse=upper_inverse, lower_link=lower_link, upper_link=upper_link, lower_root=lower_root, upper_root=upper_root, rhs_blocks=rhs_blocks, rhs_root=rhs_root, root_lower_inverse=root_lower_inverse, root_upper_inverse=root_upper_inverse, live_counts=live_counts)


def product(left, right):
    return jnp.matmul(left.astype(jnp.float32), right.astype(jnp.float32), precision=lax.Precision.HIGHEST)


def reference(lower_inverse, upper_inverse, lower_link, upper_link, lower_root, upper_root, rhs_blocks, rhs_root, root_lower_inverse, root_upper_inverse, live_counts):
    slots = jnp.arange(SUPER) % SND
    live = slots[None, :] < jnp.repeat(live_counts, SND, axis=1)
    root_term = jnp.zeros((WR, NRHS), jnp.float32)
    forward_all = []
    for layer_index in range(LAYERS):
        def forward(carried, pieces):
            inverse, coupling, right_side, alive = pieces
            solved = product(inverse, right_side.astype(jnp.float32) - product(coupling, carried))
            solved = jnp.where(alive, solved, jnp.float32(0.0))
            return jnp.where(alive, solved, carried), solved

        start = jnp.zeros((W, NRHS), jnp.float32)
        _, solved = lax.scan(forward, start, (lower_inverse[layer_index], lower_link[layer_index], rhs_blocks[layer_index], live[layer_index]))
        forward_all.append(solved)
        root_term = root_term + jnp.einsum("kaw,kwn->an", lower_root[layer_index].astype(jnp.float32), solved, precision=lax.Precision.HIGHEST)
    root_rhs = rhs_root.astype(jnp.float32) - root_term
    root_solution = product(root_upper_inverse, product(root_lower_inverse, root_rhs))
    results = []
    for layer_index in range(LAYERS):
        def backward(carried, pieces):
            inverse, coupling, root_link, solved, alive = pieces
            inner = solved - product(coupling, carried) - product(root_link, root_solution)
            answer = jnp.where(alive, product(inverse, inner), jnp.float32(0.0))
            return jnp.where(alive, answer, carried), answer

        start = jnp.zeros((W, NRHS), jnp.float32)
        _, answers = lax.scan(backward, start, (upper_inverse[layer_index], upper_link[layer_index], upper_root[layer_index], forward_all[layer_index], live[layer_index]), reverse=True)
        results.append(answers)
    return jnp.stack(results), root_solution
```

```python
import jax
import jax.numpy as jnp
from jax import lax
from jax.experimental import pallas as pl
from jax.experimental.pallas import tpu as pltpu
from jax.sharding import Mesh
from jax.sharding import PartitionSpec as P

W = 128
F32 = jnp.float32
BF16 = jnp.bfloat16
CHAIN = ("zh", "zl", "x", "c")


def dot(left, right):
    return jnp.dot(left, right, preferred_element_type=F32)


def halves(value):
    high = value.astype(BF16)
    return high, (value - high.astype(F32)).astype(BF16)


def mul2(exact, right):
    high, low = halves(right)
    return dot(exact, high) + dot(exact, low)


def mul3(left, right):
    left_high, left_low = halves(left)
    right_high, right_low = halves(right)
    return dot(
        jnp.concatenate([left_high, left_low, left_high], 1),
        jnp.concatenate([right_high, right_high, right_low], 0),
    )


def shift(offset):
    return jnp.concatenate([jnp.zeros_like(offset), offset], 1)


def pack(square):
    return jnp.concatenate([square[: W // 2], square[W // 2 :]], 1)


def unpack(packed):
    return jnp.concatenate([packed[:, :W], packed[:, W:]], 0)


def eye():
    rows = lax.broadcasted_iota(jnp.int32, (W, W), 0)
    cols = lax.broadcasted_iota(jnp.int32, (W, W), 1)
    return jnp.where(rows == cols, F32(1), F32(0))


def slots_kernel(where, linv, llink, rhs, uinv, ulink, lroot, own, keep, send):
    core, both = where[3], where[5] == 2
    maps = []
    for slot in range(2):
        made = dot(linv[0, slot], jnp.concatenate([llink[0, slot], rhs[0, slot]], 1))
        maps.append(jnp.concatenate([-made[:, :W], made[:, W:]], 1))
    chain = mul3(maps[1][:, :W], maps[0]) + shift(maps[1][:, W:])
    chain = jnp.where(both, chain, maps[0])
    back = [-dot(uinv[0, slot], ulink[0, slot]) for slot in range(2)]
    back = jnp.where(both, mul3(back[0], back[1]), back[0])
    own[:W] = chain
    own[W:] = pack(back)
    send[:W] = chain
    send[W : W + W // 2] = pack(back)
    for half, target, at in ((core, keep, 0), (1 - core, send, W + W // 2)):
        rows = pl.ds(pl.multiple_of(half * 256, 256), 256)
        second = jnp.where(both, mul2(lroot[0, 1, rows], chain), F32(0))
        target[at : at + 256] = mul2(lroot[0, 0, rows], maps[0]) + second


def chip_kernel(where, own, keep, send, out, early, back):
    first = where[3] == 0
    mine, theirs = own[:W], send[:W]
    head = jnp.where(first, mine, theirs)
    tail = jnp.where(first, theirs, mine)
    chain = mul3(tail[:, :W], head) + shift(tail[:, W:])
    back_mine, back_theirs = unpack(own[W:]), unpack(send[W : W + W // 2])
    back_head = jnp.where(first, back_mine, back_theirs)
    back_tail = jnp.where(first, back_theirs, back_mine)
    both = pack(mul3(back_head, back_tail))
    root_mine, root_theirs = keep[...], send[W + W // 2 :]
    root_head = jnp.where(first, root_mine, root_theirs)
    root_tail = jnp.where(first, root_theirs, root_mine)
    root = root_head + mul3(root_tail[:, :W], head) + shift(root_tail[:, W:])
    early[...] = head
    back[0] = back_head
    back[1] = back_tail
    for other in range(4):
        out[other, :W] = chain
        out[other, W : W + W // 2] = both
        out[other, W + W // 2 :] = root[64 * other : 64 * other + 64]


def later_weights(place, b1, b2, b12):
    one, none = eye(), jnp.zeros((W, W), F32)
    return [
        jnp.where(place == 0, one, none),
        jnp.where(place == 0, b1, jnp.where(place == 1, one, none)),
        jnp.where(place == 0, b12, jnp.where(place == 1, b2, jnp.where(place == 2, one, none))),
    ]


def level_kernel(axis, where, parts, out, before, behind, weights):
    place = where[axis]
    maps = [parts[k, :W] for k in range(4)]
    backs = [unpack(parts[k, W : W + W // 2]) for k in range(4)]
    roots = [parts[k, W + W // 2 :] for k in range(4)]
    prefix = maps[0]
    prefixes = [prefix]
    root = roots[0]
    for k in range(1, 4):
        stacked = mul3(jnp.concatenate([maps[k][:, :W], roots[k][:, :W]], 0), prefix)
        prefix = stacked[:W] + shift(maps[k][:, W:])
        root = root + stacked[W:] + shift(roots[k][:, W:])
        prefixes.append(prefix)
    start = jnp.concatenate([eye(), jnp.zeros((W, W), F32)], 1)
    before[...] = jnp.where(
        place == 0,
        start,
        jnp.where(place == 1, prefixes[0], jnp.where(place == 2, prefixes[1], prefixes[2])),
    )
    b01 = mul3(backs[0], backs[1])
    b12 = mul3(backs[1], backs[2])
    b23 = mul3(backs[2], backs[3])
    b012 = mul3(b01, backs[2])
    b123 = mul3(backs[1], b23)
    behind[...] = jnp.where(
        place == 0, b123, jnp.where(place == 1, b23, jnp.where(place == 2, backs[3], eye()))
    )
    out[:W] = prefix
    out[W : W + W // 2] = pack(mul3(b01, b23))
    out[W + W // 2 :] = root
    weights[:W] = jnp.concatenate([backs[0], b01, b012], 1)
    weights[W:] = jnp.concatenate(later_weights(place, backs[1], backs[2], b12), 1)


def top_kernel(where, parts, root, carry, weights):
    place = where[0]
    maps = [parts[k, :W] for k in range(4)]
    backs = [unpack(parts[k, W : W + W // 2]) for k in range(1, 3)]
    roots = [parts[k, W + W // 2 :] for k in range(4)]
    total = roots[0][:, W:]
    state = maps[0][:, W:]
    states = [jnp.zeros((W, W), F32), state]
    for k in range(1, 4):
        stacked = mul3(jnp.concatenate([maps[k][:, :W], roots[k][:, :W]], 0), state)
        total = total + stacked[W:] + roots[k][:, W:]
        state = stacked[:W] + maps[k][:, W:]
        states.append(state)
    carry[...] = jnp.where(
        place == 0,
        states[0],
        jnp.where(place == 1, states[1], jnp.where(place == 2, states[2], states[3])),
    )
    for other in range(4):
        root[other] = total
    weights[...] = jnp.concatenate(
        later_weights(place, backs[0], backs[1], mul3(backs[0], backs[1])), 1
    )


def sum_kernel(parts, out):
    total = (parts[0] + parts[1]) + (parts[2] + parts[3])
    for other in range(8):
        out[other] = total


def root_kernel(
    where, sums, rhs_root, root_lower, root_upper, carry, before_low, before_x, early,
    linv, llink, rhs, uinv, ulink, uroot, own_root, plain, offset,
):
    core, both = where[3], where[5] == 2
    summed = jnp.concatenate([sums[2 * (k % 4) + k // 4] for k in range(8)], 0)
    inner = mul2(root_lower[...], rhs_root[...].astype(F32) - summed)
    root = mul2(root_upper[...], inner)
    lanes = lax.broadcasted_iota(jnp.int32, (512, W), 1)
    own_root[...] = jnp.sum(jnp.where(lanes == where[4], root, F32(0)), 1, keepdims=True)
    state = carry[...]
    for ref in (before_low, before_x):
        state = mul3(ref[:, :W], state) + ref[:, W:]
    state = jnp.where(core == 0, state, mul3(early[:, :W], state) + early[:, W:])
    root_high, root_low = halves(root)
    offsets = []
    for slot in range(2):
        state = mul2(
            linv[0, slot], rhs[0, slot].astype(F32) - mul2(llink[0, slot], state)
        )
        inner = state - (dot(uroot[0, slot], root_high) + dot(uroot[0, slot], root_low))
        offsets.append(mul2(uinv[0, slot], inner))
    link = -dot(uinv[0, 0], ulink[0, 0])
    plain[0] = offsets[0]
    plain[1] = offsets[1]
    offset[...] = jnp.where(both, offsets[0] + mul3(link, offsets[1]), offsets[0])


def pair_kernel(back, parts, out):
    out[...] = parts[0] + mul3(back[0], parts[1])


def offsets_kernel(parts, weights, out, behind):
    later = jnp.concatenate([parts[1], parts[2], parts[3]], 0)
    made = mul3(weights[...], later)
    out[...] = parts[0] + made[:W]
    behind[...] = made[W:]


def answer_kernel(
    where, parts, weights, maps_low, behind_low, maps_x, behind_x, back, pair, plain,
    uinv, ulink, out,
):
    core, both = where[3], where[5] == 2
    state = mul3(weights[...], jnp.concatenate([parts[1], parts[2], parts[3]], 0))
    state = mul3(maps_low[...], state) + behind_low[...]
    state = mul3(maps_x[...], state) + behind_x[...]
    state = jnp.where(core == 0, mul3(back[1], state) + pair[1], state)
    links = [-dot(uinv[0, slot], ulink[0, slot]) for slot in range(2)]
    last = mul3(links[1], state) + plain[1]
    state = jnp.where(both, last, state)
    out[0, 1] = jnp.where(both, last, F32(0))
    out[0, 0] = mul3(links[0], state) + plain[0]


def call(kernel, inputs, shapes):
    vmem = pl.BlockSpec(memory_space=pltpu.VMEM)
    smem = pl.BlockSpec(memory_space=pltpu.SMEM)
    outs = [jax.ShapeDtypeStruct(shape, F32) for shape in shapes]
    return pl.pallas_call(
        kernel,
        out_shape=outs,
        in_specs=[smem if a.dtype == jnp.int32 else vmem for a in inputs],
        out_specs=[vmem] * len(outs),
        compiler_params=pltpu.CompilerParams(vmem_limit_bytes=32 * 1024 * 1024),
    )(*inputs)


def on_device(
    lower_inverse,
    upper_inverse,
    lower_link,
    upper_link,
    lower_root,
    upper_root,
    rhs_blocks,
    rhs_root,
    root_lower_inverse,
    root_upper_inverse,
    live_counts,
):
    places = [lax.axis_index(name) for name in CHAIN]
    column = ((places[0] * 4 + places[1]) * 4 + places[2]) * 2 + places[3]
    where = jnp.stack(places + [column, live_counts[0, 0]]).astype(jnp.int32)
    square, wide, message = (W, W), (W, 2 * W), (2 * W, 2 * W)

    own, keep, send = call(
        slots_kernel,
        [where, lower_inverse, lower_link, rhs_blocks, upper_inverse, upper_link, lower_root],
        [(192, 256), (256, 256), (448, 256)],
    )
    send = lax.ppermute(send, "c", [(0, 1), (1, 0)])
    out, early, back = call(
        chip_kernel, [where, own, keep, send], [(4,) + message, wide, (2,) + square]
    )
    parts = lax.all_to_all(out, "x", 0, 0, tiled=True)

    def level(axis, parts):
        return call(
            lambda *refs: level_kernel(axis, *refs),
            [where, parts],
            [message, wide, square, (2 * W, 3 * W)],
        )

    out, before_x, maps_x, weights_x = level(2, parts)
    parts = lax.all_gather(out, "zl")
    out, before_low, maps_low, weights_low = level(1, parts)
    parts = lax.all_gather(out, "zh")
    root, carry, weights_high = call(
        top_kernel, [where, parts], [(4, 64, W), square, (W, 3 * W)]
    )
    parts = lax.all_to_all(root, "y", 0, 0, tiled=True)
    (root,) = call(sum_kernel, [parts], [(8, 64, W)])
    sums = lax.all_to_all(root, ("x", "c"), 0, 0, tiled=True)
    own_root, plain, offset = call(
        root_kernel,
        [
            where, sums, rhs_root, root_lower_inverse, root_upper_inverse, carry, before_low,
            before_x, early, lower_inverse, lower_link, rhs_blocks, upper_inverse, upper_link,
            upper_root,
        ],
        [(512, 1), (2,) + square, square],
    )
    pair = lax.all_gather(offset, "c")
    (offset,) = call(pair_kernel, [back, pair], [square])
    parts = lax.all_gather(offset, "x")
    offset, behind_x = call(offsets_kernel, [parts, weights_x], [square, square])
    parts = lax.all_gather(offset, "zl")
    offset, behind_low = call(offsets_kernel, [parts, weights_low], [square, square])
    parts = lax.all_gather(offset, "zh")
    (answers,) = call(
        answer_kernel,
        [
            where, parts, weights_high, maps_low, behind_low, maps_x, behind_x, back, pair,
            plain, upper_inverse, upper_link,
        ],
        [(1, 2, W, W)],
    )
    return answers, own_root


def solution(mesh):
    fine = Mesh(mesh.devices.reshape(4, 4, 4, 2, 4), CHAIN + ("y",))
    split = P("y", CHAIN)
    return jax.shard_map(
        on_device,
        mesh=fine,
        in_specs=(split,) * 7 + (P(), P(), P(), split),
        out_specs=(split, P(None, CHAIN)),
        check_vma=False,
    )
```

```python
import jax
import jax.numpy as jnp
from jax import lax
from jax.experimental import pallas as pl
from jax.experimental.pallas import tpu as pltpu
from jax.sharding import Mesh
from jax.sharding import PartitionSpec as P

W = 128
F32 = jnp.float32
BF16 = jnp.bfloat16
CHAIN = ("zh", "zl", "x", "c")


def dot(left, right):
    return jnp.dot(left, right, preferred_element_type=F32)


def halves(value):
    high = value.astype(BF16)
    return high, (value - high.astype(F32)).astype(BF16)


def mul2(exact, right):
    high, low = halves(right)
    return dot(exact, high) + dot(exact, low)


def mul3(left, right):
    left_high, left_low = halves(left)
    right_high, right_low = halves(right)
    return dot(
        jnp.concatenate([left_high, left_low, left_high], 1),
        jnp.concatenate([right_high, right_high, right_low], 0),
    )


def shift(offset):
    return jnp.concatenate([jnp.zeros_like(offset), offset], 1)


def pack(square):
    return jnp.concatenate([square[: W // 2], square[W // 2 :]], 1)


def unpack(packed):
    return jnp.concatenate([packed[:, :W], packed[:, W:]], 0)


def eye():
    rows = lax.broadcasted_iota(jnp.int32, (W, W), 0)
    cols = lax.broadcasted_iota(jnp.int32, (W, W), 1)
    return jnp.where(rows == cols, F32(1), F32(0))


def copy_all(pairs, sems):
    copies = [
        pltpu.make_async_copy(source, target, sems.at[k])
        for k, (source, target) in enumerate(pairs)
    ]
    for copy in copies:
        copy.start()
    for copy in copies:
        copy.wait()


def slots_kernel(
    where, linv_in, llink_in, rhs_in, uinv_in, ulink_in, lroot_in, own, keep, send,
    linv, llink, rhs, uinv, ulink, lroot, sems,
):
    sources = (linv_in, llink_in, rhs_in, uinv_in, ulink_in, lroot_in)
    copy_all(list(zip(sources, (linv, llink, rhs, uinv, ulink, lroot))), sems)
    core, both = where[3], where[5] == 2
    maps = []
    for slot in range(2):
        made = dot(linv[0, slot], jnp.concatenate([llink[0, slot], rhs[0, slot]], 1))
        maps.append(jnp.concatenate([-made[:, :W], made[:, W:]], 1))
    chain = mul3(maps[1][:, :W], maps[0]) + shift(maps[1][:, W:])
    chain = jnp.where(both, chain, maps[0])
    back = [-dot(uinv[0, slot], ulink[0, slot]) for slot in range(2)]
    back = pack(jnp.where(both, mul3(back[0], back[1]), back[0]).T)
    own[:W] = chain
    own[W:] = back
    send[:W] = chain
    send[W : W + W // 2] = back
    for half, target, at in ((core, keep, 0), (1 - core, send, W + W // 2)):
        rows = pl.ds(pl.multiple_of(half * 256, 256), 256)
        second = jnp.where(both, mul2(lroot[0, 1, rows], chain), F32(0))
        target[at : at + 256] = mul2(lroot[0, 0, rows], maps[0]) + second


def chip_kernel(where, own, keep, send, out, early):
    first = where[3] == 0
    mine, theirs = own[:W], send[:W]
    head = jnp.where(first, mine, theirs)
    tail = jnp.where(first, theirs, mine)
    chain = mul3(tail[:, :W], head) + shift(tail[:, W:])
    back_mine, back_theirs = own[W:], send[W : W + W // 2]
    back_head = jnp.where(first, back_mine, back_theirs)
    back_tail = jnp.where(first, back_theirs, back_mine)
    root_mine, root_theirs = keep[...], send[W + W // 2 :]
    root_head = jnp.where(first, root_mine, root_theirs)
    root_tail = jnp.where(first, root_theirs, root_mine)
    root = root_head + mul3(root_tail[:, :W], head) + shift(root_tail[:, W:])
    early[...] = head
    for other in range(4):
        out[other, :128] = chain
        out[other, 128:192] = back_head
        out[other, 192:256] = back_tail
        out[other, 256:] = root[64 * other : 64 * other + 64]


def compose(place, maps, roots):
    prefix = maps[0]
    prefixes = [prefix]
    root = roots[0]
    for k in range(1, 4):
        stacked = mul3(jnp.concatenate([maps[k][:, :W], roots[k][:, :W]], 0), prefix)
        prefix = stacked[:W] + shift(maps[k][:, W:])
        root = root + stacked[W:] + shift(roots[k][:, W:])
        prefixes.append(prefix)
    start = jnp.concatenate([eye(), jnp.zeros((W, W), F32)], 1)
    before = jnp.where(
        place == 0,
        start,
        jnp.where(place == 1, prefixes[0], jnp.where(place == 2, prefixes[1], prefixes[2])),
    )
    return prefix, root, before


def plane_kernel(where, parts, out, before, backs, back):
    maps = [parts[k, :128] for k in range(4)]
    roots = [parts[k, 256:] for k in range(4)]
    chain, root, prefix = compose(where[2], maps, roots)
    before[...] = prefix
    out[:64] = jnp.where(where[3] == 0, chain[:64], chain[64:])
    out[64:] = root
    every = []
    for k in range(4):
        every += [unpack(parts[k, 128:192]), unpack(parts[k, 192:256])]
    for k in range(8):
        backs[k] = every[k]
    while len(every) > 1:
        every = [mul3(every[k + 1], every[k]) for k in range(0, len(every), 2)]
    back[...] = every[0]


def group_kernel(where, parts, pieces, out, before):
    maps = [jnp.concatenate([pieces[0, k], pieces[1, k]], 0) for k in range(4)]
    roots = [parts[k, 64:] for k in range(4)]
    chain, root, prefix = compose(where[1], maps, roots)
    before[...] = prefix
    out[:64] = jnp.where(where[3] == 0, chain[:64], chain[64:])
    out[64:] = root


def top_kernel(where, parts, pieces, root, carry):
    place = where[0]
    maps = [jnp.concatenate([pieces[0, k], pieces[1, k]], 0) for k in range(4)]
    roots = [parts[k, 64:] for k in range(4)]
    total = roots[0][:, W:]
    state = maps[0][:, W:]
    states = [jnp.zeros((W, W), F32), state]
    for k in range(1, 4):
        stacked = mul3(jnp.concatenate([maps[k][:, :W], roots[k][:, :W]], 0), state)
        total = total + stacked[W:] + roots[k][:, W:]
        state = stacked[:W] + maps[k][:, W:]
        states.append(state)
    carry[...] = jnp.where(
        place == 0,
        states[0],
        jnp.where(place == 1, states[1], jnp.where(place == 2, states[2], states[3])),
    )
    for other in range(4):
        root[other] = total


def sum_kernel(parts, out):
    total = (parts[0] + parts[1]) + (parts[2] + parts[3])
    for other in range(8):
        out[other] = total


def root_kernel(
    where, sums, rhs_root, root_lower, root_upper, carry, before_low, before_x, early,
    linv, llink, rhs, uinv, ulink, uroot, own_root, plain, offset,
):
    core, both = where[3], where[5] == 2
    summed = jnp.concatenate([sums[2 * (k % 4) + k // 4] for k in range(8)], 0)
    inner = mul2(root_lower[...], rhs_root[...].astype(F32) - summed)
    root = mul2(root_upper[...], inner)
    lanes = lax.broadcasted_iota(jnp.int32, (512, W), 1)
    own_root[...] = jnp.sum(jnp.where(lanes == where[4], root, F32(0)), 1, keepdims=True)
    state = carry[...]
    for ref in (before_low, before_x):
        state = mul3(ref[:, :W], state) + ref[:, W:]
    state = jnp.where(core == 0, state, mul3(early[:, :W], state) + early[:, W:])
    root_high, root_low = halves(root)
    offsets = []
    for slot in range(2):
        state = mul2(
            linv[0, slot], rhs[0, slot].astype(F32) - mul2(llink[0, slot], state)
        )
        inner = state - (dot(uroot[0, slot], root_high) + dot(uroot[0, slot], root_low))
        offsets.append(mul2(uinv[0, slot], inner))
    link = -dot(uinv[0, 0], ulink[0, 0])
    plain[0] = offsets[0]
    plain[1] = offsets[1]
    turned = jnp.where(both, offsets[0] + mul3(link, offsets[1]), offsets[0]).T
    for other in range(8):
        offset[other] = turned[16 * other : 16 * other + 16]


def plane_offset_kernel(parts, backs, out):
    state = parts[7]
    for k in reversed(range(7)):
        state = parts[k] + mul3(state, backs[k])
    for other in range(16):
        out[other] = state


def carry_kernel(where, planes, plane_backs, parts, backs, out):
    place = where[0] * 4 + where[1]
    state = jnp.zeros((16, W), F32)
    for k in reversed(range(1, 16)):
        state = jnp.where(place < k, planes[k] + mul3(state, plane_backs[k]), state)
    for k in reversed(range(8)):
        out[k] = state
        if k:
            state = parts[k] + mul3(state, backs[k])


def answer_kernel(where, parts, plain, uinv, ulink, out):
    both = where[5] == 2
    state = jnp.concatenate([parts[k] for k in range(8)], 0).T
    links = [-dot(uinv[0, slot], ulink[0, slot]) for slot in range(2)]
    last = mul3(links[1], state) + plain[1]
    state = jnp.where(both, last, state)
    out[0, 1] = jnp.where(both, last, F32(0))
    out[0, 0] = mul3(links[0], state) + plain[0]


def call(kernel, inputs, shapes, fetched=False):
    vmem = pl.BlockSpec(memory_space=pltpu.VMEM)
    smem = pl.BlockSpec(memory_space=pltpu.SMEM)
    block = pl.BlockSpec(memory_space=pltpu.HBM) if fetched else vmem
    scratch = []
    if fetched:
        scratch = [pltpu.VMEM(a.shape, a.dtype) for a in inputs if a.dtype == BF16]
        scratch.append(pltpu.SemaphoreType.DMA((len(scratch),)))
    return pl.pallas_call(
        kernel,
        out_shape=[jax.ShapeDtypeStruct(shape, F32) for shape in shapes],
        in_specs=[
            smem if a.dtype == jnp.int32 else block if a.dtype == BF16 else vmem for a in inputs
        ],
        out_specs=[vmem] * len(shapes),
        scratch_shapes=scratch,
        compiler_params=pltpu.CompilerParams(vmem_limit_bytes=32 * 1024 * 1024),
    )(*inputs)


def on_device(
    lower_inverse,
    upper_inverse,
    lower_link,
    upper_link,
    lower_root,
    upper_root,
    rhs_blocks,
    rhs_root,
    root_lower_inverse,
    root_upper_inverse,
    live_counts,
):
    places = [lax.axis_index(name) for name in CHAIN]
    column = ((places[0] * 4 + places[1]) * 4 + places[2]) * 2 + places[3]
    where = jnp.stack(places + [column, live_counts[0, 0]]).astype(jnp.int32)
    square, wide = (W, W), (W, 2 * W)

    own, keep, send = call(
        slots_kernel,
        [where, lower_inverse, lower_link, rhs_blocks, upper_inverse, upper_link, lower_root],
        [(192, 256), (256, 256), (448, 256)],
        fetched=True,
    )
    send = lax.ppermute(send, "c", [(0, 1), (1, 0)])
    out, early = call(chip_kernel, [where, own, keep, send], [(4, 320, 256), wide])
    parts = lax.all_to_all(out, "x", 0, 0, tiled=True)
    out, before_x, backs, back = call(
        plane_kernel, [where, parts], [(128, 256), wide, (8,) + square, square]
    )
    plane_backs = lax.all_gather(back, ("zh", "zl"))
    parts = lax.all_gather(out, "zl")
    pieces = lax.all_gather(parts[:, :64], "c")
    out, before_low = call(group_kernel, [where, parts, pieces], [(128, 256), wide])
    parts = lax.all_gather(out, "zh")
    pieces = lax.all_gather(parts[:, :64], "c")
    root, carry = call(top_kernel, [where, parts, pieces], [(4, 64, W), square])
    parts = lax.all_to_all(root, "y", 0, 0, tiled=True)
    (root,) = call(sum_kernel, [parts], [(8, 64, W)])
    sums = lax.all_to_all(root, ("x", "c"), 0, 0, tiled=True)
    own_root, plain, offset = call(
        root_kernel,
        [
            where, sums, rhs_root, root_lower_inverse, root_upper_inverse, carry, before_low,
            before_x, early, lower_inverse, lower_link, rhs_blocks, upper_inverse, upper_link,
            upper_root,
        ],
        [(512, 1), (2,) + square, (8, 16, W)],
    )
    parts = lax.all_to_all(offset, ("x", "c"), 0, 0, tiled=True)
    (offset,) = call(plane_offset_kernel, [parts, backs], [(16, 16, W)])
    planes = lax.all_to_all(offset, ("zh", "zl"), 0, 0, tiled=True)
    (states,) = call(
        carry_kernel, [where, planes, plane_backs, parts, backs], [(8, 16, W)]
    )
    states = lax.all_to_all(states, ("x", "c"), 0, 0, tiled=True)
    (answers,) = call(
        answer_kernel, [where, states, plain, upper_inverse, upper_link], [(1, 2, W, W)]
    )
    return answers, own_root


def solution(mesh):
    fine = Mesh(mesh.devices.reshape(4, 4, 4, 2, 4), CHAIN + ("y",))
    split = P("y", CHAIN)
    return jax.shard_map(
        on_device,
        mesh=fine,
        in_specs=(split,) * 7 + (P(), P(), P(), split),
        out_specs=(split, P(None, CHAIN)),
        check_vma=False,
    )
```

```python
import jax
import jax.numpy as jnp
from jax import lax
from jax.experimental import pallas as pl
from jax.experimental.pallas import tpu as pltpu
from jax.sharding import Mesh
from jax.sharding import PartitionSpec as P

W = 128
F32 = jnp.float32
BF16 = jnp.bfloat16
CHAIN = ("zh", "zl", "x", "c")


def dot(left, right):
    return jnp.dot(left, right, preferred_element_type=F32)


def halves(value):
    high = value.astype(BF16)
    return high, (value - high.astype(F32)).astype(BF16)


def mul2(exact, right):
    high, low = halves(right)
    return dot(exact, high) + dot(exact, low)


def mul3(left, right):
    left_high, left_low = halves(left)
    right_high, right_low = halves(right)
    return dot(
        jnp.concatenate([left_high, left_low, left_high], 1),
        jnp.concatenate([right_high, right_high, right_low], 0),
    )


def shift(offset):
    return jnp.concatenate([jnp.zeros_like(offset), offset], 1)


def pack(square):
    return jnp.concatenate([square[: W // 2], square[W // 2 :]], 1)


def unpack(packed):
    return jnp.concatenate([packed[:, :W], packed[:, W:]], 0)


def eye():
    rows = lax.broadcasted_iota(jnp.int32, (W, W), 0)
    cols = lax.broadcasted_iota(jnp.int32, (W, W), 1)
    return jnp.where(rows == cols, F32(1), F32(0))


def copy_all(pairs, sems):
    copies = [
        pltpu.make_async_copy(source, target, sems.at[k])
        for k, (source, target) in enumerate(pairs)
    ]
    for copy in copies:
        copy.start()
    for copy in copies:
        copy.wait()


def slots_kernel(
    where, linv_in, llink_in, rhs_in, uinv_in, ulink_in, lroot_in, own, keep, send,
    linv, llink, rhs, uinv, ulink, lroot, sems,
):
    sources = (linv_in, llink_in, rhs_in, uinv_in, ulink_in, lroot_in)
    copy_all(list(zip(sources, (linv, llink, rhs, uinv, ulink, lroot))), sems)
    core, both = where[3], where[5] == 2
    maps = []
    for slot in range(2):
        made = dot(linv[0, slot], jnp.concatenate([llink[0, slot], rhs[0, slot]], 1))
        maps.append(jnp.concatenate([-made[:, :W], made[:, W:]], 1))
    chain = mul3(maps[1][:, :W], maps[0]) + shift(maps[1][:, W:])
    chain = jnp.where(both, chain, maps[0])
    back = [-dot(uinv[0, slot], ulink[0, slot]) for slot in range(2)]
    back = pack(jnp.where(both, mul3(back[0], back[1]), back[0]).T)
    own[:W] = chain
    own[W:] = back
    send[:W] = chain
    send[W : W + W // 2] = back
    for half, target, at in ((core, keep, 0), (1 - core, send, W + W // 2)):
        rows = pl.ds(pl.multiple_of(half * 256, 256), 256)
        second = jnp.where(both, mul2(lroot[0, 1, rows], chain), F32(0))
        target[at : at + 256] = mul2(lroot[0, 0, rows], maps[0]) + second


def chip_kernel(where, own, keep, send, out, early):
    first = where[3] == 0
    mine, theirs = own[:W], send[:W]
    head = jnp.where(first, mine, theirs)
    tail = jnp.where(first, theirs, mine)
    chain = mul3(tail[:, :W], head) + shift(tail[:, W:])
    back_mine, back_theirs = own[W:], send[W : W + W // 2]
    back_head = jnp.where(first, back_mine, back_theirs)
    back_tail = jnp.where(first, back_theirs, back_mine)
    root_mine, root_theirs = keep[...], send[W + W // 2 :]
    root_head = jnp.where(first, root_mine, root_theirs)
    root_tail = jnp.where(first, root_theirs, root_mine)
    root = root_head + mul3(root_tail[:, :W], head) + shift(root_tail[:, W:])
    early[...] = head
    for other in range(4):
        out[other, :128] = chain
        out[other, 128:192] = back_head
        out[other, 192:256] = back_tail
        out[other, 256:] = root[64 * other : 64 * other + 64]


def compose(place, maps, roots):
    prefix = maps[0]
    prefixes = [prefix]
    root = roots[0]
    for k in range(1, 4):
        stacked = mul3(jnp.concatenate([maps[k][:, :W], roots[k][:, :W]], 0), prefix)
        prefix = stacked[:W] + shift(maps[k][:, W:])
        root = root + stacked[W:] + shift(roots[k][:, W:])
        prefixes.append(prefix)
    start = jnp.concatenate([eye(), jnp.zeros((W, W), F32)], 1)
    before = jnp.where(
        place == 0,
        start,
        jnp.where(place == 1, prefixes[0], jnp.where(place == 2, prefixes[1], prefixes[2])),
    )
    return prefix, root, before


def half(core, rows):
    middle = rows.shape[0] // 2
    return jnp.where(core == 0, rows[:middle], rows[middle:])


def plane_kernel(where, parts, out, before, backs):
    maps = [parts[k, :128] for k in range(4)]
    roots = [parts[k, 256:] for k in range(4)]
    chain, root, prefix = compose(where[2], maps, roots)
    before[...] = prefix
    every = []
    for k in range(4):
        every += [unpack(parts[k, 128:192]), unpack(parts[k, 192:256])]
    for k in range(8):
        backs[k] = every[k]
    while len(every) > 1:
        every = [mul3(every[k + 1], every[k]) for k in range(0, len(every), 2)]
    out[:64] = half(where[3], chain)
    out[64:96] = half(where[3], pack(every[0]))
    out[96:] = root


def joined(pieces):
    maps = [jnp.concatenate([pieces[0, k, :64], pieces[1, k, :64]], 0) for k in range(4)]
    backs = [jnp.concatenate([pieces[0, k, 64:], pieces[1, k, 64:]], 0) for k in range(4)]
    return maps, [unpack(packed) for packed in backs]


def group_kernel(where, parts, pieces, out, before, backs):
    maps, every = joined(pieces)
    roots = [parts[k, 96:] for k in range(4)]
    chain, root, prefix = compose(where[1], maps, roots)
    before[...] = prefix
    for k in range(4):
        backs[k] = every[k]
    back = mul3(mul3(every[3], every[2]), mul3(every[1], every[0]))
    out[:64] = half(where[3], chain)
    out[64:96] = half(where[3], pack(back))
    out[96:] = root


def top_kernel(where, parts, pieces, root, carry, backs):
    place = where[0]
    maps, every = joined(pieces)
    roots = [parts[k, 96:] for k in range(4)]
    total = roots[0][:, W:]
    state = maps[0][:, W:]
    states = [jnp.zeros((W, W), F32), state]
    for k in range(1, 4):
        stacked = mul3(jnp.concatenate([maps[k][:, :W], roots[k][:, :W]], 0), state)
        total = total + stacked[W:] + roots[k][:, W:]
        state = stacked[:W] + maps[k][:, W:]
        states.append(state)
    carry[...] = jnp.where(
        place == 0,
        states[0],
        jnp.where(place == 1, states[1], jnp.where(place == 2, states[2], states[3])),
    )
    for other in range(4):
        root[other] = total
        backs[other] = every[other]


def sum_kernel(parts, out):
    total = (parts[0] + parts[1]) + (parts[2] + parts[3])
    for other in range(8):
        out[other] = total


def root_kernel(
    where, sums, rhs_root, root_lower, root_upper, carry, before_low, before_x, early,
    linv, llink, rhs, uinv, ulink, uroot, own_root, plain, offset,
):
    core, both = where[3], where[5] == 2
    summed = jnp.concatenate([sums[2 * (k % 4) + k // 4] for k in range(8)], 0)
    inner = mul2(root_lower[...], rhs_root[...].astype(F32) - summed)
    root = mul2(root_upper[...], inner)
    columns = lax.broadcasted_iota(jnp.int32, (W, 512), 0)
    own_root[...] = jnp.sum(jnp.where(columns == where[4], root.T, F32(0)), 0, keepdims=True)
    state = carry[...]
    for ref in (before_low, before_x):
        state = mul3(ref[:, :W], state) + ref[:, W:]
    state = jnp.where(core == 0, state, mul3(early[:, :W], state) + early[:, W:])
    root_high, root_low = halves(root)
    offsets = []
    for slot in range(2):
        state = mul2(
            linv[0, slot], rhs[0, slot].astype(F32) - mul2(llink[0, slot], state)
        )
        inner = state - (dot(uroot[0, slot], root_high) + dot(uroot[0, slot], root_low))
        offsets.append(mul2(uinv[0, slot], inner))
    link = -dot(uinv[0, 0], ulink[0, 0])
    plain[0] = offsets[0]
    plain[1] = offsets[1]
    turned = jnp.where(both, offsets[0] + mul3(link, offsets[1]), offsets[0]).T
    for other in range(8):
        offset[other] = turned[16 * other : 16 * other + 16]


def offset_kernel(where, parts, backs, plane_backs, group_backs, out):
    group, place = where[0], where[1]
    state = parts[7]
    for k in reversed(range(7)):
        state = parts[k] + mul3(state, backs[k])
    sent = state
    for k in reversed(range(3)):
        sent = jnp.where(place > k, mul3(sent, plane_backs[k]), sent)
    for other in reversed(range(4)):
        for k in range(4):
            out[4 * other + k] = jnp.where(group == other, state, sent)
        if other:
            sent = jnp.where(group > other, mul3(sent, group_backs[other]), sent)


def carry_kernel(where, planes, plane_backs, parts, backs, out):
    group, place = where[0], where[1]
    state = jnp.zeros((16, W), F32)
    for k in range(4, 16):
        state = state + jnp.where(k // 4 > group, planes[k], F32(0))
    for k in reversed(range(1, 4)):
        state = jnp.where(
            place < k, planes[4 * group + k] + mul3(state, plane_backs[k]), state
        )
    for k in reversed(range(8)):
        out[k] = state
        if k:
            state = parts[k] + mul3(state, backs[k])


def answer_kernel(where, parts, plain, uinv, ulink, out):
    both = where[5] == 2
    state = jnp.concatenate([parts[k] for k in range(8)], 0).T
    links = [-dot(uinv[0, slot], ulink[0, slot]) for slot in range(2)]
    last = mul3(links[1], state) + plain[1]
    state = jnp.where(both, last, state)
    out[0, 1] = jnp.where(both, last, F32(0))
    out[0, 0] = mul3(links[0], state) + plain[0]


def call(kernel, inputs, shapes, fetched=False):
    vmem = pl.BlockSpec(memory_space=pltpu.VMEM)
    smem = pl.BlockSpec(memory_space=pltpu.SMEM)
    block = pl.BlockSpec(memory_space=pltpu.HBM) if fetched else vmem
    scratch = []
    if fetched:
        scratch = [pltpu.VMEM(a.shape, a.dtype) for a in inputs if a.dtype == BF16]
        scratch.append(pltpu.SemaphoreType.DMA((len(scratch),)))
    if fetched:
        inputs = [
            pltpu.with_memory_space_constraint(a, pltpu.HBM) if a.dtype == BF16 else a
            for a in inputs
        ]
    return pl.pallas_call(
        kernel,
        out_shape=[jax.ShapeDtypeStruct(shape, F32) for shape in shapes],
        in_specs=[
            smem if a.dtype == jnp.int32 else block if a.dtype == BF16 else vmem for a in inputs
        ],
        out_specs=[vmem] * len(shapes),
        scratch_shapes=scratch,
        compiler_params=pltpu.CompilerParams(vmem_limit_bytes=32 * 1024 * 1024),
    )(*inputs)


def on_device(
    lower_inverse,
    upper_inverse,
    lower_link,
    upper_link,
    lower_root,
    upper_root,
    rhs_blocks,
    rhs_root,
    root_lower_inverse,
    root_upper_inverse,
    live_counts,
):
    places = [lax.axis_index(name) for name in CHAIN]
    column = ((places[0] * 4 + places[1]) * 4 + places[2]) * 2 + places[3]
    where = jnp.stack(places + [column, live_counts[0, 0]]).astype(jnp.int32)
    square, wide = (W, W), (W, 2 * W)

    own, keep, send = call(
        slots_kernel,
        [where, lower_inverse, lower_link, rhs_blocks, upper_inverse, upper_link, lower_root],
        [(192, 256), (256, 256), (448, 256)],
        fetched=True,
    )
    send = lax.ppermute(send, "c", [(0, 1), (1, 0)])
    out, early = call(chip_kernel, [where, own, keep, send], [(4, 320, 256), wide])
    parts = lax.all_to_all(out, "x", 0, 0, tiled=True)
    out, before_x, backs = call(
        plane_kernel, [where, parts], [(160, 256), wide, (8,) + square]
    )
    parts = lax.all_gather(out, "zl")
    pieces = lax.all_gather(parts[:, :96], "c")
    out, before_low, low_backs = call(
        group_kernel, [where, parts, pieces], [(160, 256), wide, (4,) + square]
    )
    parts = lax.all_gather(out, "zh")
    pieces = lax.all_gather(parts[:, :96], "c")
    root, carry, high_backs = call(
        top_kernel, [where, parts, pieces], [(4, 64, W), square, (4,) + square]
    )
    parts = lax.all_to_all(root, "y", 0, 0, tiled=True)
    (root,) = call(sum_kernel, [parts], [(8, 64, W)])
    sums = lax.all_to_all(root, ("x", "c"), 0, 0, tiled=True)
    own_root, plain, offset = call(
        root_kernel,
        [
            where, sums, rhs_root, root_lower_inverse, root_upper_inverse, carry, before_low,
            before_x, early, lower_inverse, lower_link, rhs_blocks, upper_inverse, upper_link,
            upper_root,
        ],
        [(1, 512), (2,) + square, (8, 16, W)],
    )
    parts = lax.all_to_all(offset, ("x", "c"), 0, 0, tiled=True)
    (offset,) = call(
        offset_kernel, [where, parts, backs, low_backs, high_backs], [(16, 16, W)]
    )
    planes = lax.all_to_all(offset, ("zh", "zl"), 0, 0, tiled=True)
    (states,) = call(carry_kernel, [where, planes, low_backs, parts, backs], [(8, 16, W)])
    states = lax.all_to_all(states, ("x", "c"), 0, 0, tiled=True)
    (answers,) = call(
        answer_kernel, [where, states, plain, upper_inverse, upper_link], [(1, 2, W, W)]
    )
    return answers, own_root.reshape(512, 1)


def solution(mesh):
    fine = Mesh(mesh.devices.reshape(4, 4, 4, 2, 4), CHAIN + ("y",))
    split = P("y", CHAIN)
    return jax.shard_map(
        on_device,
        mesh=fine,
        in_specs=(split,) * 7 + (P(), P(), P(), split),
        out_specs=(split, P(None, CHAIN)),
        check_vma=False,
    )
```

```python
from functools import partial

import jax
import jax.numpy as jnp
from jax import lax
from jax.experimental import pallas as pl
from jax.experimental.pallas import tpu as pltpu
from jax.sharding import Mesh
from jax.sharding import PartitionSpec as P

W = 128
F32 = jnp.float32
BF16 = jnp.bfloat16
CHAIN = ("zh", "zl", "x", "c")


def dot(left, right):
    return jnp.dot(left, right, preferred_element_type=F32)


def halves(value):
    high = value.astype(BF16)
    return high, (value - high.astype(F32)).astype(BF16)


def mul2(exact, right):
    high, low = halves(right)
    return dot(exact, high) + dot(exact, low)


def mul3(left, right):
    left_high, left_low = halves(left)
    right_high, right_low = halves(right)
    return dot(
        jnp.concatenate([left_high, left_low, left_high], 1),
        jnp.concatenate([right_high, right_high, right_low], 0),
    )


def shift(offset):
    return jnp.concatenate([jnp.zeros_like(offset), offset], 1)


def pack(square):
    return jnp.concatenate([square[: W // 2], square[W // 2 :]], 1)


def unpack(packed):
    return jnp.concatenate([packed[:, :W], packed[:, W:]], 0)


def eye():
    rows = lax.broadcasted_iota(jnp.int32, (W, W), 0)
    cols = lax.broadcasted_iota(jnp.int32, (W, W), 1)
    return jnp.where(rows == cols, F32(1), F32(0))


def slots_kernel(
    where, linv_in, llink_in, rhs_in, uinv_in, ulink_in, lroot_in, keep, send,
    linv, llink, rhs, uinv, ulink, lroot, sems,
):
    sources = (linv_in, llink_in, rhs_in, uinv_in, ulink_in, lroot_in)
    targets = (linv, llink, rhs, uinv, ulink, lroot)
    copies = [
        pltpu.make_async_copy(source, target, sems.at[k])
        for k, (source, target) in enumerate(zip(sources, targets))
    ]
    for copy in copies:
        copy.start()
    core, both = where[3], where[5] == 2
    for copy in copies[:3]:
        copy.wait()
    maps = []
    for slot in range(2):
        made = dot(linv[0, slot], jnp.concatenate([llink[0, slot], rhs[0, slot]], 1))
        maps.append(jnp.concatenate([-made[:, :W], made[:, W:]], 1))
    chain = mul3(maps[1][:, :W], maps[0]) + shift(maps[1][:, W:])
    chain = jnp.where(both, chain, maps[0])
    send[:W] = chain
    for copy in copies[3:]:
        copy.wait()
    back = [-dot(uinv[0, slot], ulink[0, slot]) for slot in range(2)]
    back = pack(jnp.where(both, mul3(back[0], back[1]), back[0]).T)
    send[W : W + W // 2] = back
    for part, target, at in ((core, keep, 0), (1 - core, send, W + W // 2)):
        rows = pl.ds(pl.multiple_of(part * 256, 256), 256)
        second = jnp.where(both, mul2(lroot[0, 1, rows], chain), F32(0))
        target[at : at + 256] = mul2(lroot[0, 0, rows], maps[0]) + second


def half(core, rows):
    middle = rows.shape[0] // 2
    return jnp.where(core == 0, rows[:middle], rows[middle:])


def chip_kernel(where, keep, pair, out, early, ends):
    core = where[3]
    first = core == 0
    head, tail = pair[0, :W], pair[1, :W]
    chain = mul3(tail[:, :W], head) + shift(tail[:, W:])
    back_head, back_tail = [unpack(pair[k, W : W + W // 2]) for k in range(2)]
    root_mine = keep[...]
    root_head = jnp.where(first, root_mine, pair[0, W + W // 2 :])
    root_tail = jnp.where(first, pair[1, W + W // 2 :], root_mine)
    root = root_head + mul3(root_tail[:, :W], head) + shift(root_tail[:, W:])
    early[...] = head
    ends[0] = back_head
    ends[1] = back_tail
    chain_half = half(core, chain)
    back_half = half(core, pack(mul3(back_tail, back_head)))
    for other in range(4):
        out[other, :64] = chain_half
        out[other, 64:96] = back_half
        out[other, 96:] = root[64 * other : 64 * other + 64]


def compose(place, maps, roots):
    prefix = maps[0]
    prefixes = [prefix]
    root = roots[0]
    for k in range(1, 4):
        stacked = mul3(jnp.concatenate([maps[k][:, :W], roots[k][:, :W]], 0), prefix)
        prefix = stacked[:W] + shift(maps[k][:, W:])
        root = root + stacked[W:] + shift(roots[k][:, W:])
        prefixes.append(prefix)
    start = jnp.concatenate([eye(), jnp.zeros((W, W), F32)], 1)
    before = jnp.where(
        place == 0,
        start,
        jnp.where(place == 1, prefixes[0], jnp.where(place == 2, prefixes[1], prefixes[2])),
    )
    return prefix, root, before


def joined(pieces):
    maps = [jnp.concatenate([pieces[0, k, :64], pieces[1, k, :64]], 0) for k in range(4)]
    backs = [jnp.concatenate([pieces[0, k, 64:], pieces[1, k, 64:]], 0) for k in range(4)]
    return maps, [unpack(packed) for packed in backs]


def level_kernel(axis, where, parts, pieces, out, before, backs):
    maps, every = joined(pieces)
    chain, root, prefix = compose(where[axis], maps, [parts[k, 96:] for k in range(4)])
    before[...] = prefix
    for k in range(4):
        backs[k] = every[k]
    back = mul3(mul3(every[3], every[2]), mul3(every[1], every[0]))
    out[:64] = half(where[3], chain)
    out[64:96] = half(where[3], pack(back))
    out[96:] = root


def top_kernel(where, parts, pieces, root, carry, backs):
    place = where[0]
    maps, every = joined(pieces)
    roots = [parts[k, 96:] for k in range(4)]
    total = roots[0][:, W:]
    state = maps[0][:, W:]
    states = [jnp.zeros((W, W), F32), state]
    for k in range(1, 4):
        stacked = mul3(jnp.concatenate([maps[k][:, :W], roots[k][:, :W]], 0), state)
        total = total + stacked[W:] + roots[k][:, W:]
        state = stacked[:W] + maps[k][:, W:]
        states.append(state)
    carry[...] = jnp.where(
        place == 0,
        states[0],
        jnp.where(place == 1, states[1], jnp.where(place == 2, states[2], states[3])),
    )
    for k in range(4):
        backs[k] = every[k]
    for other in range(4):
        root[other] = total


def sum_kernel(parts, out):
    total = (parts[0] + parts[1]) + (parts[2] + parts[3])
    for other in range(8):
        out[other] = total


def root_kernel(
    where, sums, rhs_root, root_lower, root_upper, carry, before_low, before_x, early, ends,
    linv, llink, rhs, uinv, ulink, uroot, own_root, plain, offset,
):
    core, both = where[3], where[5] == 2
    summed = jnp.concatenate([sums[2 * (k % 4) + k // 4] for k in range(8)], 0)
    inner = mul2(root_lower[...], rhs_root[...].astype(F32) - summed)
    root = mul2(root_upper[...], inner)
    state = carry[...]
    for ref in (before_low, before_x):
        state = mul3(ref[:, :W], state) + ref[:, W:]
    state = jnp.where(core == 0, state, mul3(early[:, :W], state) + early[:, W:])
    root_high, root_low = halves(root)
    offsets = []
    for slot in range(2):
        state = mul2(
            linv[0, slot], rhs[0, slot].astype(F32) - mul2(llink[0, slot], state)
        )
        inner = state - (dot(uroot[0, slot], root_high) + dot(uroot[0, slot], root_low))
        offsets.append(mul2(uinv[0, slot], inner))
    link = -dot(uinv[0, 0], ulink[0, 0])
    plain[0] = offsets[0]
    plain[1] = offsets[1]
    turned = jnp.where(both, offsets[0] + mul3(link, offsets[1]), offsets[0]).T
    carried = jnp.where(core == 0, turned, mul3(turned, ends[0]))
    for other in range(8):
        rows = slice(16 * other, 16 * other + 16)
        offset[other, :16] = carried[rows]
        offset[other, 16:] = turned[rows]
    columns = lax.broadcasted_iota(jnp.int32, (W, 512), 0)
    own_root[...] = jnp.sum(jnp.where(columns == where[4], root.T, F32(0)), 0, keepdims=True)


def offset_kernel(where, parts, backs, plane_backs, group_backs, out):
    group, place = where[0], where[1]
    chips = [parts[2 * k, :16] + parts[2 * k + 1, :16] for k in range(4)]
    state = chips[3]
    for k in reversed(range(3)):
        state = chips[k] + mul3(state, backs[k])
    sent = state
    for k in reversed(range(3)):
        sent = jnp.where(place > k, mul3(sent, plane_backs[k]), sent)
    for other in reversed(range(4)):
        for k in range(4):
            out[4 * other + k] = jnp.where(group == other, state, sent)
        if other:
            sent = jnp.where(group > other, mul3(sent, group_backs[other]), sent)


def carry_kernel(where, planes, plane_backs, parts, backs, out):
    group, place = where[0], where[1]
    state = jnp.zeros((16, W), F32)
    for k in range(4, 16):
        state = state + jnp.where(k // 4 > group, planes[k], F32(0))
    for k in reversed(range(1, 4)):
        state = jnp.where(
            place < k, planes[4 * group + k] + mul3(state, plane_backs[k]), state
        )
    for k in reversed(range(4)):
        for core in range(2):
            out[2 * k + core, :16] = state
            out[2 * k + core, 16:] = parts[2 * k + 1, 16:]
        if k:
            chip = parts[2 * k, :16] + parts[2 * k + 1, :16]
            state = chip + mul3(state, backs[k])


def answer_kernel(where, parts, ends, plain, uinv, ulink, out):
    both = where[5] == 2
    state = jnp.concatenate([parts[k, :16] for k in range(8)], 0)
    other = jnp.concatenate([parts[k, 16:] for k in range(8)], 0)
    state = jnp.where(where[3] == 0, mul3(state, ends[1]) + other, state).T
    links = [-dot(uinv[0, slot], ulink[0, slot]) for slot in range(2)]
    last = mul3(links[1], state) + plain[1]
    state = jnp.where(both, last, state)
    out[0, 1] = jnp.where(both, last, F32(0))
    out[0, 0] = mul3(links[0], state) + plain[0]


def call(kernel, inputs, shapes, fetched=False):
    vmem = pl.BlockSpec(memory_space=pltpu.VMEM)
    smem = pl.BlockSpec(memory_space=pltpu.SMEM)
    block = pl.BlockSpec(memory_space=pltpu.HBM) if fetched else vmem
    scratch = []
    if fetched:
        scratch = [pltpu.VMEM(a.shape, a.dtype) for a in inputs if a.dtype == BF16]
        scratch.append(pltpu.SemaphoreType.DMA((len(scratch),)))
    if fetched:
        inputs = [
            pltpu.with_memory_space_constraint(a, pltpu.HBM) if a.dtype == BF16 else a
            for a in inputs
        ]
    return pl.pallas_call(
        kernel,
        out_shape=[jax.ShapeDtypeStruct(shape, F32) for shape in shapes],
        in_specs=[
            smem if a.dtype == jnp.int32 else block if a.dtype == BF16 else vmem for a in inputs
        ],
        out_specs=[vmem] * len(shapes),
        scratch_shapes=scratch,
        compiler_params=pltpu.CompilerParams(vmem_limit_bytes=32 * 1024 * 1024),
    )(*inputs)


def on_device(
    lower_inverse,
    upper_inverse,
    lower_link,
    upper_link,
    lower_root,
    upper_root,
    rhs_blocks,
    rhs_root,
    root_lower_inverse,
    root_upper_inverse,
    live_counts,
):
    places = [lax.axis_index(name) for name in CHAIN]
    column = ((places[0] * 4 + places[1]) * 4 + places[2]) * 2 + places[3]
    where = jnp.stack(places + [column, live_counts[0, 0]]).astype(jnp.int32)
    square, wide = (W, W), (W, 2 * W)

    keep, send = call(
        slots_kernel,
        [where, lower_inverse, lower_link, rhs_blocks, upper_inverse, upper_link, lower_root],
        [(256, 256), (448, 256)],
        fetched=True,
    )
    pair = lax.all_gather(send, "c")
    out, early, ends = call(
        chip_kernel, [where, keep, pair], [(4, 160, 256), wide, (2,) + square]
    )

    def level(axis, parts):
        pieces = lax.all_gather(parts[:, :96], "c")
        return call(
            partial(level_kernel, axis),
            [where, parts, pieces],
            [(160, 256), wide, (4,) + square],
        )

    parts = lax.all_to_all(out, "x", 0, 0, tiled=True)
    out, before_x, chip_backs = level(2, parts)
    parts = lax.all_gather(out, "zl")
    out, before_low, low_backs = level(1, parts)
    parts = lax.all_gather(out, "zh")
    pieces = lax.all_gather(parts[:, :96], "c")
    root, carry, high_backs = call(
        top_kernel, [where, parts, pieces], [(4, 64, W), square, (4,) + square]
    )
    parts = lax.all_to_all(root, "y", 0, 0, tiled=True)
    (root,) = call(sum_kernel, [parts], [(8, 64, W)])
    sums = lax.all_to_all(root, ("x", "c"), 0, 0, tiled=True)
    own_root, plain, offset = call(
        root_kernel,
        [
            where, sums, rhs_root, root_lower_inverse, root_upper_inverse, carry, before_low,
            before_x, early, ends, lower_inverse, lower_link, rhs_blocks, upper_inverse,
            upper_link, upper_root,
        ],
        [(1, 512), (2,) + square, (8, 32, W)],
    )
    parts = lax.all_to_all(offset, ("x", "c"), 0, 0, tiled=True)
    (offset,) = call(
        offset_kernel, [where, parts, chip_backs, low_backs, high_backs], [(16, 16, W)]
    )
    planes = lax.all_to_all(offset, ("zh", "zl"), 0, 0, tiled=True)
    (states,) = call(
        carry_kernel, [where, planes, low_backs, parts, chip_backs], [(8, 32, W)]
    )
    states = lax.all_to_all(states, ("x", "c"), 0, 0, tiled=True)
    (answers,) = call(
        answer_kernel, [where, states, ends, plain, upper_inverse, upper_link], [(1, 2, W, W)]
    )
    return answers, own_root.reshape(512, 1)


def solution(mesh):
    fine = Mesh(mesh.devices.reshape(4, 4, 4, 2, 4), CHAIN + ("y",))
    split = P("y", CHAIN)
    return jax.shard_map(
        on_device,
        mesh=fine,
        in_specs=(split,) * 7 + (P(), P(), P(), split),
        out_specs=(split, P(None, CHAIN)),
        check_vma=False,
    )
```

```python
import jax
import jax.numpy as jnp
from jax import lax
from jax.experimental import pallas as pl
from jax.experimental.pallas import tpu as pltpu
from jax.sharding import Mesh
from jax.sharding import PartitionSpec as P

W = 128
F32 = jnp.float32
BF16 = jnp.bfloat16
CHAIN = ("zh", "zl", "x", "c")


def dot(left, right):
    return jnp.dot(left, right, preferred_element_type=F32)


def halves(value):
    high = value.astype(BF16)
    return high, (value - high.astype(F32)).astype(BF16)


def mul2(exact, right):
    high, low = halves(right)
    return dot(exact, high) + dot(exact, low)


def mul3(left, right):
    left_high, left_low = halves(left)
    right_high, right_low = halves(right)
    return dot(
        jnp.concatenate([left_high, left_low, left_high], 1),
        jnp.concatenate([right_high, right_high, right_low], 0),
    )


def shift(offset):
    return jnp.concatenate([jnp.zeros_like(offset), offset], 1)


def pack(square):
    return jnp.concatenate([square[: W // 2], square[W // 2 :]], 1)


def unpack(packed):
    return jnp.concatenate([packed[:, :W], packed[:, W:]], 0)


def eye():
    rows = lax.broadcasted_iota(jnp.int32, (W, W), 0)
    cols = lax.broadcasted_iota(jnp.int32, (W, W), 1)
    return jnp.where(rows == cols, F32(1), F32(0))


def slots_kernel(
    where, linv_in, llink_in, rhs_in, uinv_in, ulink_in, lroot_in, keep, send, ahead,
    linv, llink, rhs, uinv, ulink, lroot, sems,
):
    sources = (linv_in, llink_in, rhs_in, uinv_in, ulink_in, lroot_in)
    targets = (linv, llink, rhs, uinv, ulink, lroot)
    copies = [
        pltpu.make_async_copy(source, target, sems.at[k])
        for k, (source, target) in enumerate(zip(sources, targets))
    ]
    for copy in copies:
        copy.start()
    core, both = where[3], where[5] == 2
    for copy in copies[:3]:
        copy.wait()
    maps = []
    for slot in range(2):
        made = dot(linv[0, slot], jnp.concatenate([llink[0, slot], rhs[0, slot]], 1))
        maps.append(jnp.concatenate([-made[:, :W], made[:, W:]], 1))
    chain = mul3(maps[1][:, :W], maps[0]) + shift(maps[1][:, W:])
    chain = jnp.where(both, chain, maps[0])
    send[:W] = chain
    for copy in copies[3:]:
        copy.wait()
    links = [-dot(uinv[0, slot], ulink[0, slot]) for slot in range(2)]
    back = jnp.where(both, mul3(links[0], links[1]), links[0])
    send[W : W + W // 2] = pack(back.T)
    ahead[:W] = maps[0]
    ahead[W:] = jnp.concatenate([back, links[1]], 1)
    for part, target, at in ((core, keep, 0), (1 - core, send, W + W // 2)):
        rows = pl.ds(pl.multiple_of(part * 256, 256), 256)
        second = jnp.where(both, mul2(lroot[0, 1, rows], chain), F32(0))
        target[at : at + 256] = mul2(lroot[0, 0, rows], maps[0]) + second


def half(core, rows):
    middle = rows.shape[0] // 2
    return jnp.where(core == 0, rows[:middle], rows[middle:])


def after(map_rows, ahead):
    return mul3(map_rows[:, :W], ahead) + shift(map_rows[:, W:])


def chip_kernel(where, keep, pair, ahead, out, solve, ends, last):
    core = where[3]
    first = core == 0
    head, tail = pair[0, :W], pair[1, :W]
    root_mine = keep[...]
    root_head = jnp.where(first, root_mine, pair[0, W + W // 2 :])
    root_tail = jnp.where(first, pair[1, W + W // 2 :], root_mine)
    slot = ahead[:W]
    made = after(jnp.concatenate([tail, slot, root_tail], 0), head)
    chain, root = made[:W], root_head + made[2 * W :]
    solve[:W] = jnp.where(first, slot, made[W : 2 * W])
    solve[W:] = jnp.where(first, head, chain)
    back_head, back_tail = [unpack(pair[k, W : W + W // 2]) for k in range(2)]
    chain_half = half(core, chain)
    back_half = half(core, pack(mul3(back_tail, back_head)))
    for other in range(4):
        out[other, :64] = chain_half
        out[other, 64:96] = back_half
        out[other, 96:] = root[64 * other : 64 * other + 64]
    ends[...] = back_head.T
    answer = jnp.concatenate([ahead[W:, :W], ahead[W:, W:]], 0)
    last[:, :W] = jnp.where(first, mul3(answer, back_tail.T), answer)
    last[:, W:] = jnp.where(first, answer, F32(0))


def compose(place, maps, roots):
    one = after(jnp.concatenate([maps[1], roots[1]], 0), maps[0])
    two = after(jnp.concatenate([maps[3], roots[3]], 0), maps[2])
    root_one, root_two = roots[0] + one[W:], roots[2] + two[W:]
    one, two = one[:W], two[:W]
    made = after(jnp.concatenate([maps[2], two, root_two], 0), one)
    start = jnp.concatenate([eye(), jnp.zeros((W, W), F32)], 1)
    before = jnp.where(
        place == 0,
        start,
        jnp.where(place == 1, maps[0], jnp.where(place == 2, one, made[:W])),
    )
    return made[W : 2 * W], root_one + made[2 * W :], before


def products(backs):
    p10, p21, p32 = [mul3(backs[k + 1], backs[k]) for k in range(3)]
    return p10, p21, p32, mul3(backs[2], p10), mul3(backs[3], p21), mul3(p32, p10)


def joined(pieces):
    maps = [jnp.concatenate([pieces[0, k, :64], pieces[1, k, :64]], 0) for k in range(4)]
    backs = [jnp.concatenate([pieces[0, k, 64:], pieces[1, k, 64:]], 0) for k in range(4)]
    return maps, [unpack(packed) for packed in backs]


def plane_kernel(where, parts, pieces, out, before, gather, spread):
    core = where[3]
    maps, backs = joined(pieces)
    chain, root, prefix = compose(where[2], maps, [parts[k, 96:] for k in range(4)])
    before[...] = prefix
    p10, p21, p32, p210, p321, total = products(backs)
    out[:64] = half(core, chain)
    out[64:96] = half(core, pack(total))
    out[96:] = root
    for k, value in enumerate((eye(), backs[0], p10, p210)):
        gather[W * k : W * k + W] = value
    for k, value in enumerate((p321, p32, backs[3], p21, backs[2], backs[1])):
        spread[:, W * k : W * k + W] = value


def pick(place, *values):
    chosen = values[-1]
    for k in reversed(range(len(values) - 1)):
        chosen = jnp.where(place == k, values[k], chosen)
    return chosen


def group_kernel(
    where, parts, pieces, solve, before_x, out, before, solve_out, ahead, within,
    chain_ref, back_ref, root_ref,
):
    core, place = where[3], where[1]
    maps, backs = joined(pieces)
    chain, root, prefix = compose(place, maps, [parts[k, 96:] for k in range(4)])
    before[...] = prefix
    p10, p21, p32, p210, p321, total = products(backs)
    at = 0
    for ref, value, rows, start in (
        (chain_ref, chain, 16, 64 * core + 16 * place),
        (back_ref, pack(total), 8, 32 * core + 8 * place),
        (root_ref, root, 16, 16 * place),
    ):
        ref[...] = value
        out[at : at + rows] = ref[pl.ds(pl.multiple_of(start, rows), rows)]
        at += rows
    solve_out[...] = after(solve[...], before_x[...])
    one, none = eye(), jnp.zeros((W, W), F32)
    ahead[...] = pick(place, one, backs[0], p10, p210)
    within[:W] = pick(place, p321, p32, backs[3], one)
    within[W : 2 * W] = pick(place, one, none)
    within[2 * W : 3 * W] = pick(place, backs[1], one, none)
    within[3 * W :] = pick(place, p21, backs[2], one, none)


def top_kernel(where, parts, pieces, solve, before_low, ahead, root, carry, solve_out, sent):
    place = where[0]
    maps, backs, roots = [], [], []
    for k in range(4):
        mine = [(core, 4 * k + low) for core in range(2) for low in range(4)]
        maps.append(jnp.concatenate([pieces[core, z, :16] for core, z in mine], 0))
        backs.append(unpack(jnp.concatenate([pieces[core, z, 16:] for core, z in mine], 0)))
        roots.append(jnp.concatenate([parts[4 * k + low, 24:] for low in range(4)], 0))
    total = roots[0][:, W:]
    state = maps[0][:, W:]
    states = [jnp.zeros((W, W), F32), state]
    for k in range(1, 4):
        stacked = mul3(jnp.concatenate([maps[k][:, :W], roots[k][:, :W]], 0), state)
        total = total + stacked[W:] + roots[k][:, W:]
        state = stacked[:W] + maps[k][:, W:]
        states.append(state)
    carry[...] = pick(place, *states[:4])
    for other in range(4):
        root[other] = total
    solve_out[...] = after(solve[...], before_low[...])
    one = mul3(ahead[...], pick(place, backs[0], backs[0], backs[1], backs[2]))
    sent[:, :W] = ahead[...]
    sent[:, W : 2 * W] = one
    sent[:, 2 * W :] = mul3(one, pick(place, backs[0], backs[0], backs[0], backs[1]))


def sum_kernel(parts, out):
    total = (parts[0] + parts[1]) + (parts[2] + parts[3])
    for other in range(8):
        out[other] = total


def root_kernel(
    where, sums, rhs_root, root_lower, root_upper, carry, solve, ends, uinv, ulink, uroot,
    own_root, plain, offset,
):
    core, both = where[3], where[5] == 2
    summed = jnp.concatenate([sums[2 * (k % 4) + k // 4] for k in range(8)], 0)
    inner = mul2(root_lower[...], rhs_root[...].astype(F32) - summed)
    root = mul2(root_upper[...], inner)
    solved = mul3(solve[:, :W], carry[...]) + solve[:, W:]
    first, second = uinv[0, 0].astype(F32), uinv[0, 1].astype(F32)
    link = jnp.where(both, -dot(uinv[0, 0], ulink[0, 0]), F32(0))
    over = mul3(link, second)
    moved = mul3(ends[...], jnp.concatenate([first, over], 1))
    root_high, root_low = halves(root)
    inner = [
        solved[W * slot : W * slot + W]
        - (dot(uroot[0, slot], root_high) + dot(uroot[0, slot], root_low))
        for slot in range(2)
    ]
    on_first = mul3(jnp.concatenate([first, moved[:, :W]], 0), inner[0])
    on_second = mul3(jnp.concatenate([over, moved[:, W:], second], 0), inner[1])
    whole = on_first + on_second[: 2 * W]
    plain[:W] = whole[:W]
    plain[W:] = on_second[2 * W :]
    turned = whole[:W].T
    carried = jnp.where(core == 0, whole[:W], whole[W:]).T
    for other in range(8):
        rows = slice(16 * other, 16 * other + 16)
        offset[other, :16] = carried[rows]
        offset[other, 16:] = turned[rows]
    columns = lax.broadcasted_iota(jnp.int32, (W, 512), 0)
    own_root[...] = jnp.sum(jnp.where(columns == where[4], root.T, F32(0)), 0, keepdims=True)


def chip_offsets(parts):
    return [parts[2 * k, :16] + parts[2 * k + 1, :16] for k in range(4)]


def offset_kernel(where, parts, gather, sent, out):
    state = mul3(jnp.concatenate(chip_offsets(parts), 1), gather[...])
    moved = mul3(state, sent[...])
    values = [state, moved[:, :W], moved[:, W : 2 * W], moved[:, 2 * W :]]
    for other in range(4):
        value = pick(where[0] - other, *values)
        for k in range(4):
            out[4 * other + k] = value


def carry_kernel(where, planes, within, parts, spread, out):
    group = where[0]
    state = jnp.zeros((16, W), F32)
    for k in range(4, 16):
        state = state + jnp.where(k // 4 > group, planes[k], F32(0))
    offsets = [planes[4 * group + k] for k in range(1, 4)]
    state = mul3(jnp.concatenate([state] + offsets, 1), within[...])
    chips = chip_offsets(parts)
    moved = mul3(chips[3], spread[:, 3 * W : 5 * W])
    plain = [
        chips[1] + mul3(chips[2], spread[:, 5 * W :]) + moved[:, :W],
        chips[2] + moved[:, W:],
        chips[3],
    ]
    moved = mul3(state, spread[:, : 3 * W])
    states = [plain[k] + moved[:, W * k : W * k + W] for k in range(3)] + [state]
    for k in range(4):
        for core in range(2):
            out[2 * k + core, :16] = states[k]
            out[2 * k + core, 16:] = parts[2 * k + 1, 16:]


def answer_kernel(where, parts, last, plain, out):
    state = jnp.concatenate([parts[k, :16] for k in range(8)], 0).T
    other = jnp.concatenate([parts[k, 16:] for k in range(8)], 0).T
    made = mul3(last[...], jnp.concatenate([state, other], 0)) + plain[...]
    out[0, 0] = made[:W]
    out[0, 1] = jnp.where(where[5] == 2, made[W:], F32(0))


def call(kernel, inputs, shapes, fetched=False, scratch=()):
    vmem = pl.BlockSpec(memory_space=pltpu.VMEM)
    smem = pl.BlockSpec(memory_space=pltpu.SMEM)
    block = pl.BlockSpec(memory_space=pltpu.HBM) if fetched else vmem
    scratch = [pltpu.VMEM(shape, F32) for shape in scratch]
    if fetched:
        scratch = [pltpu.VMEM(a.shape, a.dtype) for a in inputs if a.dtype == BF16]
        scratch.append(pltpu.SemaphoreType.DMA((len(scratch),)))
    if fetched:
        inputs = [
            pltpu.with_memory_space_constraint(a, pltpu.HBM) if a.dtype == BF16 else a
            for a in inputs
        ]
    return pl.pallas_call(
        kernel,
        out_shape=[jax.ShapeDtypeStruct(shape, F32) for shape in shapes],
        in_specs=[
            smem if a.dtype == jnp.int32 else block if a.dtype == BF16 else vmem for a in inputs
        ],
        out_specs=[vmem] * len(shapes),
        scratch_shapes=scratch,
        compiler_params=pltpu.CompilerParams(vmem_limit_bytes=32 * 1024 * 1024),
    )(*inputs)


def on_device(
    lower_inverse,
    upper_inverse,
    lower_link,
    upper_link,
    lower_root,
    upper_root,
    rhs_blocks,
    rhs_root,
    root_lower_inverse,
    root_upper_inverse,
    live_counts,
):
    places = [lax.axis_index(name) for name in CHAIN]
    column = ((places[0] * 4 + places[1]) * 4 + places[2]) * 2 + places[3]
    where = jnp.stack(places + [column, live_counts[0, 0]]).astype(jnp.int32)
    square, wide = (W, W), (W, 2 * W)

    keep, send, ahead = call(
        slots_kernel,
        [where, lower_inverse, lower_link, rhs_blocks, upper_inverse, upper_link, lower_root],
        [(256, 256), (448, 256), (256, 256)],
        fetched=True,
    )
    pair = lax.all_gather(send, "c")
    out, solve, ends, last = call(
        chip_kernel,
        [where, keep, pair, ahead],
        [(4, 160, 256), (256, 256), square, (256, 256)],
    )
    parts = lax.all_to_all(out, "x", 0, 0, tiled=True)
    pieces = lax.all_gather(parts[:, :96], "c")
    out, before_x, gather, spread = call(
        plane_kernel, [where, parts, pieces], [(160, 256), wide, (4 * W, W), (W, 6 * W)]
    )
    parts = lax.all_gather(out, "zl")
    pieces = lax.all_gather(parts[:, :96], "c")
    out, before_low, solve, ahead, within = call(
        group_kernel,
        [where, parts, pieces, solve, before_x],
        [(40, 256), wide, (256, 256), square, (4 * W, W)],
        scratch=[wide, (64, 256), (64, 256)],
    )
    parts = lax.all_gather(out, ("zh", "zl"))
    pieces = lax.all_gather(parts[:, :24], "c")
    root, carry, solve, sent = call(
        top_kernel,
        [where, parts, pieces, solve, before_low, ahead],
        [(4, 64, W), square, (256, 256), (W, 3 * W)],
    )
    parts = lax.all_to_all(root, "y", 0, 0, tiled=True)
    (root,) = call(sum_kernel, [parts], [(8, 64, W)])
    sums = lax.all_to_all(root, ("x", "c"), 0, 0, tiled=True)
    own_root, plain, offset = call(
        root_kernel,
        [
            where, sums, rhs_root, root_lower_inverse, root_upper_inverse, carry, solve, ends,
            upper_inverse, upper_link, upper_root,
        ],
        [(1, 512), (256, W), (8, 32, W)],
    )
    parts = lax.all_to_all(offset, ("x", "c"), 0, 0, tiled=True)
    (offset,) = call(offset_kernel, [where, parts, gather, sent], [(16, 16, W)])
    planes = lax.all_to_all(offset, ("zh", "zl"), 0, 0, tiled=True)
    (states,) = call(carry_kernel, [where, planes, within, parts, spread], [(8, 32, W)])
    states = lax.all_to_all(states, ("x", "c"), 0, 0, tiled=True)
    (answers,) = call(answer_kernel, [where, states, last, plain], [(1, 2, W, W)])
    return answers, own_root.reshape(512, 1)


def solution(mesh):
    fine = Mesh(mesh.devices.reshape(4, 4, 4, 2, 4), CHAIN + ("y",))
    split = P("y", CHAIN)
    return jax.shard_map(
        on_device,
        mesh=fine,
        in_specs=(split,) * 7 + (P(), P(), P(), split),
        out_specs=(split, P(None, CHAIN)),
        check_vma=False,
    )
```

```python
import jax
import jax.numpy as jnp
from jax import lax
from jax.experimental import pallas as pl
from jax.experimental.pallas import tpu as pltpu
from jax.sharding import Mesh
from jax.sharding import PartitionSpec as P

W = 128
F32 = jnp.float32
BF16 = jnp.bfloat16
CHAIN = ("zh", "za", "zb", "x", "c")
LOW = ("za", "zb")
SHARE = ("zb",)
SHARES = 2
ROWS = 64 // SHARES


def dot(left, right):
    return jnp.dot(left, right, preferred_element_type=F32)


def halves(value):
    high = value.astype(BF16)
    return high, (value - high.astype(F32)).astype(BF16)


def mul2(exact, right):
    high, low = halves(right)
    return dot(exact, high) + dot(exact, low)


def mul3(left, right):
    left_high, left_low = halves(left)
    right_high, right_low = halves(right)
    return dot(
        jnp.concatenate([left_high, left_low, left_high], 1),
        jnp.concatenate([right_high, right_high, right_low], 0),
    )


def shift(offset):
    return jnp.concatenate([jnp.zeros_like(offset), offset], 1)


def pack(square):
    return jnp.concatenate([square[: W // 2], square[W // 2 :]], 1)


def unpack(packed):
    return jnp.concatenate([packed[:, :W], packed[:, W:]], 0)


def eye():
    rows = lax.broadcasted_iota(jnp.int32, (W, W), 0)
    cols = lax.broadcasted_iota(jnp.int32, (W, W), 1)
    return jnp.where(rows == cols, F32(1), F32(0))


def slots_kernel(
    where, linv_in, llink_in, rhs_in, uinv_in, ulink_in, lroot_in, keep, send, ahead,
    linv, llink, rhs, uinv, ulink, lroot, sems,
):
    sources = (linv_in, llink_in, rhs_in, uinv_in, ulink_in, lroot_in)
    targets = (linv, llink, rhs, uinv, ulink, lroot)
    copies = [
        pltpu.make_async_copy(source, target, sems.at[k])
        for k, (source, target) in enumerate(zip(sources, targets))
    ]
    for copy in copies:
        copy.start()
    core, both = where[3], where[5] == 2
    for copy in copies[:3]:
        copy.wait()
    maps = []
    for slot in range(2):
        made = dot(linv[0, slot], jnp.concatenate([llink[0, slot], rhs[0, slot]], 1))
        maps.append(jnp.concatenate([-made[:, :W], made[:, W:]], 1))
    chain = mul3(maps[1][:, :W], maps[0]) + shift(maps[1][:, W:])
    chain = jnp.where(both, chain, maps[0])
    send[:W] = chain
    for copy in copies[3:]:
        copy.wait()
    links = [-dot(uinv[0, slot], ulink[0, slot]) for slot in range(2)]
    back = jnp.where(both, mul3(links[0], links[1]), links[0])
    send[W : W + W // 2] = pack(back.T)
    ahead[:W] = maps[0]
    ahead[W:] = jnp.concatenate([back, links[1]], 1)
    for part, target, at in ((core, keep, 0), (1 - core, send, W + W // 2)):
        rows = pl.ds(pl.multiple_of(part * 256, 256), 256)
        second = jnp.where(both, mul2(lroot[0, 1, rows], chain), F32(0))
        target[at : at + 256] = mul2(lroot[0, 0, rows], maps[0]) + second


def half(core, rows):
    middle = rows.shape[0] // 2
    return jnp.where(core == 0, rows[:middle], rows[middle:])


def after(map_rows, ahead):
    return mul3(map_rows[:, :W], ahead) + shift(map_rows[:, W:])


def chip_kernel(where, keep, pair, ahead, out, solve, ends, last):
    core = where[3]
    first = core == 0
    head, tail = pair[0, :W], pair[1, :W]
    root_mine = keep[...]
    root_head = jnp.where(first, root_mine, pair[0, W + W // 2 :])
    root_tail = jnp.where(first, pair[1, W + W // 2 :], root_mine)
    slot = ahead[:W]
    made = after(jnp.concatenate([tail, slot, root_tail], 0), head)
    chain, root = made[:W], root_head + made[2 * W :]
    solve[:W] = jnp.where(first, slot, made[W : 2 * W])
    solve[W:] = jnp.where(first, head, chain)
    back_head, back_tail = [unpack(pair[k, W : W + W // 2]) for k in range(2)]
    chain_half = half(core, chain)
    back_half = half(core, pack(mul3(back_tail, back_head)))
    for other in range(4):
        out[other, :64] = chain_half
        out[other, 64:96] = back_half
        out[other, 96:] = root[64 * other : 64 * other + 64]
    ends[...] = back_head.T
    answer = jnp.concatenate([ahead[W:, :W], ahead[W:, W:]], 0)
    last[:, :W] = jnp.where(first, mul3(answer, back_tail.T), answer)
    last[:, W:] = jnp.where(first, answer, F32(0))


def compose(place, maps, roots):
    one = after(jnp.concatenate([maps[1], roots[1]], 0), maps[0])
    two = after(jnp.concatenate([maps[3], roots[3]], 0), maps[2])
    root_one, root_two = roots[0] + one[W:], roots[2] + two[W:]
    one, two = one[:W], two[:W]
    made = after(jnp.concatenate([maps[2], two, root_two], 0), one)
    start = jnp.concatenate([eye(), jnp.zeros((W, W), F32)], 1)
    before = jnp.where(
        place == 0,
        start,
        jnp.where(place == 1, maps[0], jnp.where(place == 2, one, made[:W])),
    )
    return made[W : 2 * W], root_one + made[2 * W :], before


def products(backs):
    p10, p21, p32 = [mul3(backs[k + 1], backs[k]) for k in range(3)]
    return p10, p21, p32, mul3(backs[2], p10), mul3(backs[3], p21), mul3(p32, p10)


def joined(pieces):
    maps = [jnp.concatenate([pieces[0, k, :64], pieces[1, k, :64]], 0) for k in range(4)]
    backs = [jnp.concatenate([pieces[0, k, 64:], pieces[1, k, 64:]], 0) for k in range(4)]
    return maps, [unpack(packed) for packed in backs]


def plane_kernel(where, parts, pieces, out, before, gather, spread):
    core = where[3]
    maps, backs = joined(pieces)
    chain, root, prefix = compose(where[2], maps, [parts[k, 96:] for k in range(4)])
    before[...] = prefix
    p10, p21, p32, p210, p321, total = products(backs)
    out[:64] = half(core, chain)
    out[64:96] = half(core, pack(total))
    out[96:] = root
    for k, value in enumerate((eye(), backs[0], p10, p210)):
        gather[W * k : W * k + W] = value
    for k, value in enumerate((p321, p32, backs[3], p21, backs[2], backs[1])):
        spread[:, W * k : W * k + W] = value


def pick(place, *values):
    chosen = values[-1]
    for k in reversed(range(len(values) - 1)):
        chosen = jnp.where(place == k, values[k], chosen)
    return chosen


def group_kernel(
    where, parts, pieces, solve, before_x, out, before, solve_out, ahead, within,
):
    core, place = where[3], where[1]
    share = pl.ds(pl.multiple_of(96 + lax.rem(place, SHARES) * ROWS, ROWS), ROWS)
    maps, backs = joined(pieces)
    chain, root, prefix = compose(place, maps, [parts[k, share] for k in range(4)])
    before[...] = prefix
    p10, p21, p32, p210, p321, total = products(backs)
    out[:64] = half(core, chain)
    out[64:96] = half(core, pack(total))
    out[96:] = root
    solve_out[...] = after(solve[...], before_x[...])
    one, none = eye(), jnp.zeros((W, W), F32)
    ahead[...] = pick(place, one, backs[0], p10, p210)
    within[:W] = pick(place, p321, p32, backs[3], one)
    within[W : 2 * W] = pick(place, one, none)
    within[2 * W : 3 * W] = pick(place, backs[1], one, none)
    within[3 * W :] = pick(place, p21, backs[2], one, none)


def top_kernel(where, parts, pieces, solve, before_low, ahead, root, carry, solve_out, sent):
    place = where[0]
    maps, backs = joined(pieces)
    roots = [parts[k, 96:] for k in range(4)]
    total = roots[0][:, W:]
    state = maps[0][:, W:]
    states = [jnp.zeros((W, W), F32), state]
    for k in range(1, 4):
        stacked = mul3(jnp.concatenate([maps[k][:, :W], roots[k][:, :W]], 0), state)
        total = total + stacked[W:] + roots[k][:, W:]
        state = stacked[:W] + maps[k][:, W:]
        states.append(state)
    carry[...] = pick(place, *states[:4])
    for other in range(4):
        root[other] = total
    solve_out[...] = after(solve[...], before_low[...])
    one = mul3(ahead[...], pick(place, backs[0], backs[0], backs[1], backs[2]))
    sent[:, :W] = ahead[...]
    sent[:, W : 2 * W] = one
    sent[:, 2 * W :] = mul3(one, pick(place, backs[0], backs[0], backs[0], backs[1]))


def sum_kernel(parts, out):
    total = (parts[0] + parts[1]) + (parts[2] + parts[3])
    for other in range(8 * SHARES):
        out[other] = total


def root_kernel(
    where, sums, rhs_root, root_lower, root_upper, carry, solve, ends, uinv, ulink, uroot,
    own_root, plain, offset,
):
    core, both = where[3], where[5] == 2
    order = [(k * 4 + x) * 2 + c for c in range(2) for x in range(4) for k in range(SHARES)]
    summed = jnp.concatenate([sums[k] for k in order], 0)
    inner = mul2(root_lower[...], rhs_root[...].astype(F32) - summed)
    root = mul2(root_upper[...], inner)
    solved = mul3(solve[:, :W], carry[...]) + solve[:, W:]
    first, second = uinv[0, 0].astype(F32), uinv[0, 1].astype(F32)
    link = jnp.where(both, -dot(uinv[0, 0], ulink[0, 0]), F32(0))
    over = mul3(link, second)
    moved = mul3(ends[...], jnp.concatenate([first, over], 1))
    root_high, root_low = halves(root)
    inner = [
        solved[W * slot : W * slot + W]
        - (dot(uroot[0, slot], root_high) + dot(uroot[0, slot], root_low))
        for slot in range(2)
    ]
    on_first = mul3(jnp.concatenate([first, moved[:, :W]], 0), inner[0])
    on_second = mul3(jnp.concatenate([over, moved[:, W:], second], 0), inner[1])
    whole = on_first + on_second[: 2 * W]
    plain[:W] = whole[:W]
    plain[W:] = on_second[2 * W :]
    turned = whole[:W].T
    carried = jnp.where(core == 0, whole[:W], whole[W:]).T
    for other in range(8):
        rows = slice(16 * other, 16 * other + 16)
        offset[other, :16] = carried[rows]
        offset[other, 16:] = turned[rows]
    columns = lax.broadcasted_iota(jnp.int32, (W, 512), 0)
    own_root[...] = jnp.sum(jnp.where(columns == where[4], root.T, F32(0)), 0, keepdims=True)


def chip_offsets(parts):
    return [parts[2 * k, :16] + parts[2 * k + 1, :16] for k in range(4)]


def offset_kernel(where, parts, gather, sent, out):
    state = mul3(jnp.concatenate(chip_offsets(parts), 1), gather[...])
    moved = mul3(state, sent[...])
    values = [state, moved[:, :W], moved[:, W : 2 * W], moved[:, 2 * W :]]
    for other in range(4):
        value = pick(where[0] - other, *values)
        for k in range(4):
            out[4 * other + k] = value


def carry_kernel(where, planes, within, parts, spread, out):
    group = where[0]
    state = jnp.zeros((16, W), F32)
    for k in range(4, 16):
        state = state + jnp.where(k // 4 > group, planes[k], F32(0))
    offsets = [planes[4 * group + k] for k in range(1, 4)]
    state = mul3(jnp.concatenate([state] + offsets, 1), within[...])
    chips = chip_offsets(parts)
    moved = mul3(chips[3], spread[:, 3 * W : 5 * W])
    plain = [
        chips[1] + mul3(chips[2], spread[:, 5 * W :]) + moved[:, :W],
        chips[2] + moved[:, W:],
        chips[3],
    ]
    moved = mul3(state, spread[:, : 3 * W])
    states = [plain[k] + moved[:, W * k : W * k + W] for k in range(3)] + [state]
    for k in range(4):
        for core in range(2):
            out[2 * k + core, :16] = states[k]
            out[2 * k + core, 16:] = parts[2 * k + 1, 16:]


def answer_kernel(where, parts, last, plain, out):
    state = jnp.concatenate([parts[k, :16] for k in range(8)], 0).T
    other = jnp.concatenate([parts[k, 16:] for k in range(8)], 0).T
    made = mul3(last[...], jnp.concatenate([state, other], 0)) + plain[...]
    out[0, 0] = made[:W]
    out[0, 1] = jnp.where(where[5] == 2, made[W:], F32(0))


def call(kernel, inputs, shapes, fetched=False):
    vmem = pl.BlockSpec(memory_space=pltpu.VMEM)
    smem = pl.BlockSpec(memory_space=pltpu.SMEM)
    block = pl.BlockSpec(memory_space=pltpu.HBM) if fetched else vmem
    scratch = []
    if fetched:
        scratch = [pltpu.VMEM(a.shape, a.dtype) for a in inputs if a.dtype == BF16]
        scratch.append(pltpu.SemaphoreType.DMA((len(scratch),)))
        inputs = [
            pltpu.with_memory_space_constraint(a, pltpu.HBM) if a.dtype == BF16 else a
            for a in inputs
        ]
    return pl.pallas_call(
        kernel,
        out_shape=[jax.ShapeDtypeStruct(shape, F32) for shape in shapes],
        in_specs=[
            smem if a.dtype == jnp.int32 else block if a.dtype == BF16 else vmem for a in inputs
        ],
        out_specs=[vmem] * len(shapes),
        scratch_shapes=scratch,
        compiler_params=pltpu.CompilerParams(vmem_limit_bytes=32 * 1024 * 1024),
    )(*inputs)


def on_device(
    lower_inverse,
    upper_inverse,
    lower_link,
    upper_link,
    lower_root,
    upper_root,
    rhs_blocks,
    rhs_root,
    root_lower_inverse,
    root_upper_inverse,
    live_counts,
):
    places = [lax.axis_index(axes) for axes in ("zh", LOW, "x", "c")]
    column = ((places[0] * 4 + places[1]) * 4 + places[2]) * 2 + places[3]
    where = jnp.stack(places + [column, live_counts[0, 0]]).astype(jnp.int32)
    square, wide = (W, W), (W, 2 * W)

    keep, send, ahead = call(
        slots_kernel,
        [where, lower_inverse, lower_link, rhs_blocks, upper_inverse, upper_link, lower_root],
        [(256, 256), (448, 256), (256, 256)],
        fetched=True,
    )
    pair = lax.all_gather(send, "c")
    out, solve, ends, last = call(
        chip_kernel,
        [where, keep, pair, ahead],
        [(4, 160, 256), (256, 256), square, (256, 256)],
    )
    parts = lax.all_to_all(out, "x", 0, 0, tiled=True)
    pieces = lax.all_gather(parts[:, :96], "c")
    out, before_x, gather, spread = call(
        plane_kernel, [where, parts, pieces], [(160, 256), wide, (4 * W, W), (W, 6 * W)]
    )
    parts = lax.all_gather(out, LOW)
    pieces = lax.all_gather(parts[:, :96], "c")
    out, before_low, solve, ahead, within = call(
        group_kernel,
        [where, parts, pieces, solve, before_x],
        [(96 + ROWS, 256), wide, (256, 256), square, (4 * W, W)],
    )
    parts = lax.all_gather(out, "zh")
    pieces = lax.all_gather(parts[:, :96], "c")
    root, carry, solve, sent = call(
        top_kernel,
        [where, parts, pieces, solve, before_low, ahead],
        [(4, ROWS, W), square, (256, 256), (W, 3 * W)],
    )
    parts = lax.all_to_all(root, "y", 0, 0, tiled=True)
    (root,) = call(sum_kernel, [parts], [(8 * SHARES, ROWS, W)])
    sums = lax.all_to_all(root, SHARE + ("x", "c"), 0, 0, tiled=True)
    own_root, plain, offset = call(
        root_kernel,
        [
            where, sums, rhs_root, root_lower_inverse, root_upper_inverse, carry, solve, ends,
            upper_inverse, upper_link, upper_root,
        ],
        [(1, 512), (256, W), (8, 32, W)],
    )
    parts = lax.all_to_all(offset, ("x", "c"), 0, 0, tiled=True)
    (offset,) = call(offset_kernel, [where, parts, gather, sent], [(16, 16, W)])
    planes = lax.all_to_all(offset, ("zh",) + LOW, 0, 0, tiled=True)
    (states,) = call(carry_kernel, [where, planes, within, parts, spread], [(8, 32, W)])
    states = lax.all_to_all(states, ("x", "c"), 0, 0, tiled=True)
    (answers,) = call(answer_kernel, [where, states, last, plain], [(1, 2, W, W)])
    return answers, own_root.reshape(512, 1)


def solution(mesh):
    fine = Mesh(mesh.devices.reshape(4, 2, 2, 4, 2, 4), CHAIN + ("y",))
    split = P("y", CHAIN)
    return jax.shard_map(
        on_device,
        mesh=fine,
        in_specs=(split,) * 7 + (P(), P(), P(), split),
        out_specs=(split, P(None, CHAIN)),
        check_vma=False,
    )
```

```python
import jax
import jax.numpy as jnp
from jax import lax
from jax.experimental import pallas as pl
from jax.experimental.pallas import tpu as pltpu
from jax.sharding import Mesh
from jax.sharding import PartitionSpec as P

W = 128
F32 = jnp.float32
BF16 = jnp.bfloat16
CHAIN = ("zh", "za", "zb", "x", "c")
LOW = ("za", "zb")
SHARE = ("zb",)
SHARES = 2
ROWS = 64 // SHARES


def dot(left, right):
    return jnp.dot(left, right, preferred_element_type=F32)


def halves(value):
    high = value.astype(BF16)
    return high, (value - high.astype(F32)).astype(BF16)


def mul2(exact, right):
    high, low = halves(right)
    if right.shape[1] == W:
        made = dot(exact, jnp.concatenate([high, low], 1))
        return made[:, :W] + made[:, W:]
    return dot(jnp.concatenate([exact, exact], 1), jnp.concatenate([high, low], 0))


def mul3(left, right):
    left_high, left_low = halves(left)
    right_high, right_low = halves(right)
    both = jnp.concatenate([left_high, left_low], 1)
    if right.shape[1] == W:
        upper = jnp.concatenate([right_high, right_low], 1)
        lower = jnp.concatenate([right_high, jnp.zeros_like(right_low)], 1)
        made = dot(both, jnp.concatenate([upper, lower], 0))
        return made[:, :W] + made[:, W:]
    return dot(both, jnp.concatenate([right_high, right_high], 0)) + dot(left_high, right_low)


def shift(offset):
    return jnp.concatenate([jnp.zeros_like(offset), offset], 1)


def pack(square):
    return jnp.concatenate([square[: W // 2], square[W // 2 :]], 1)


def unpack(packed):
    return jnp.concatenate([packed[:, :W], packed[:, W:]], 0)


def eye():
    rows = lax.broadcasted_iota(jnp.int32, (W, W), 0)
    cols = lax.broadcasted_iota(jnp.int32, (W, W), 1)
    return jnp.where(rows == cols, F32(1), F32(0))


def slots_kernel(
    where, linv_in, llink_in, rhs_in, uinv_in, ulink_in, lroot_in, keep, send, ahead,
    linv, llink, rhs, uinv, ulink, lroot, sems,
):
    sources = (linv_in, llink_in, rhs_in, uinv_in, ulink_in, lroot_in)
    targets = (linv, llink, rhs, uinv, ulink, lroot)
    copies = [
        pltpu.make_async_copy(source, target, sems.at[k])
        for k, (source, target) in enumerate(zip(sources, targets))
    ]
    for copy in copies:
        copy.start()
    core, both = where[3], where[5] == 2
    for copy in copies[:3]:
        copy.wait()
    maps = []
    for slot in range(2):
        made = dot(linv[0, slot], jnp.concatenate([llink[0, slot], rhs[0, slot]], 1))
        maps.append(jnp.concatenate([-made[:, :W], made[:, W:]], 1))
    chain = mul3(maps[1][:, :W], maps[0]) + shift(maps[1][:, W:])
    chain = jnp.where(both, chain, maps[0])
    send[:W] = chain
    for copy in copies[3:]:
        copy.wait()
    links = [-dot(uinv[0, slot], ulink[0, slot]) for slot in range(2)]
    back = jnp.where(both, mul3(links[0], links[1]), links[0])
    send[W : W + W // 2] = pack(back.T)
    ahead[:W] = maps[0]
    ahead[W:] = jnp.concatenate([back, links[1]], 1)
    second = jnp.where(both, chain, F32(0))
    ahead_high, ahead_low = halves(jnp.concatenate([maps[0], second], 0))
    for part, target, at in ((core, keep, 0), (1 - core, send, W + W // 2)):
        rows = pl.ds(pl.multiple_of(part * 256, 256), 256)
        blocks = jnp.concatenate([lroot[0, 0, rows], lroot[0, 1, rows]], 1)
        target[at : at + 256] = dot(blocks, ahead_high) + dot(blocks, ahead_low)


def half(core, rows):
    middle = rows.shape[0] // 2
    return jnp.where(core == 0, rows[:middle], rows[middle:])


def after(map_rows, ahead):
    return mul3(map_rows[:, :W], ahead) + shift(map_rows[:, W:])


def chip_kernel(where, keep, pair, ahead, out, solve, ends, last):
    core = where[3]
    first = core == 0
    head, tail = pair[0, :W], pair[1, :W]
    root_mine = keep[...]
    root_head = jnp.where(first, root_mine, pair[0, W + W // 2 :])
    root_tail = jnp.where(first, pair[1, W + W // 2 :], root_mine)
    slot = ahead[:W]
    made = after(jnp.concatenate([tail, slot, root_tail], 0), head)
    chain, root = made[:W], root_head + made[2 * W :]
    solve[:W] = jnp.where(first, slot, made[W : 2 * W])
    solve[W:] = jnp.where(first, head, chain)
    back_head, back_tail = [unpack(pair[k, W : W + W // 2]) for k in range(2)]
    chain_half = half(core, chain)
    back_half = half(core, pack(mul3(back_tail, back_head)))
    for other in range(4):
        out[other, :64] = chain_half
        out[other, 64:96] = back_half
        out[other, 96:] = root[64 * other : 64 * other + 64]
    ends[...] = back_head.T
    answer = jnp.concatenate([ahead[W:, :W], ahead[W:, W:]], 0)
    last[:, :W] = jnp.where(first, mul3(answer, back_tail.T), answer)
    last[:, W:] = jnp.where(first, answer, F32(0))


def compose(place, maps, roots):
    one = after(jnp.concatenate([maps[1], roots[1]], 0), maps[0])
    two = after(jnp.concatenate([maps[3], roots[3]], 0), maps[2])
    root_one, root_two = roots[0] + one[W:], roots[2] + two[W:]
    one, two = one[:W], two[:W]
    made = after(jnp.concatenate([maps[2], two, root_two], 0), one)
    start = jnp.concatenate([eye(), jnp.zeros((W, W), F32)], 1)
    before = jnp.where(
        place == 0,
        start,
        jnp.where(place == 1, maps[0], jnp.where(place == 2, one, made[:W])),
    )
    return made[W : 2 * W], root_one + made[2 * W :], before


def products(backs):
    p10, p21, p32 = [mul3(backs[k + 1], backs[k]) for k in range(3)]
    return p10, p21, p32, mul3(backs[2], p10), mul3(backs[3], p21), mul3(p32, p10)


def joined(pieces):
    maps = [jnp.concatenate([pieces[0, k, :64], pieces[1, k, :64]], 0) for k in range(4)]
    backs = [jnp.concatenate([pieces[0, k, 64:], pieces[1, k, 64:]], 0) for k in range(4)]
    return maps, [unpack(packed) for packed in backs]


def plane_kernel(where, parts, pieces, out, before, gather, spread):
    core = where[3]
    maps, backs = joined(pieces)
    chain, root, prefix = compose(where[2], maps, [parts[k, 96:] for k in range(4)])
    before[...] = prefix
    p10, p21, p32, p210, p321, total = products(backs)
    out[:64] = half(core, chain)
    out[64:96] = half(core, pack(total))
    out[96:] = root
    for k, value in enumerate((eye(), backs[0], p10, p210)):
        gather[W * k : W * k + W] = value
    for k, value in enumerate((p321, p32, backs[3], p21, backs[2], backs[1])):
        spread[:, W * k : W * k + W] = value


def pick(place, *values):
    chosen = values[-1]
    for k in reversed(range(len(values) - 1)):
        chosen = jnp.where(place == k, values[k], chosen)
    return chosen


def group_kernel(
    where, parts, pieces, solve, before_x, out, before, solve_out, ahead, within,
):
    core, place = where[3], where[1]
    share = pl.ds(pl.multiple_of(96 + lax.rem(place, SHARES) * ROWS, ROWS), ROWS)
    maps, backs = joined(pieces)
    chain, root, prefix = compose(place, maps, [parts[k, share] for k in range(4)])
    before[...] = prefix
    p10, p21, p32, p210, p321, total = products(backs)
    out[:64] = half(core, chain)
    out[64:96] = half(core, pack(total))
    out[96:] = root
    solve_out[...] = after(solve[...], before_x[...])
    one, none = eye(), jnp.zeros((W, W), F32)
    ahead[...] = pick(place, one, backs[0], p10, p210)
    within[:W] = pick(place, p321, p32, backs[3], one)
    within[W : 2 * W] = pick(place, one, none)
    within[2 * W : 3 * W] = pick(place, backs[1], one, none)
    within[3 * W :] = pick(place, p21, backs[2], one, none)


def top_kernel(where, parts, pieces, solve, before_low, ahead, root, carry, solve_out, sent):
    place = where[0]
    maps, backs = joined(pieces)
    roots = [parts[k, 96:] for k in range(4)]
    total = roots[0][:, W:]
    state = maps[0][:, W:]
    states = [jnp.zeros((W, W), F32), state]
    for k in range(1, 4):
        stacked = mul3(jnp.concatenate([maps[k][:, :W], roots[k][:, :W]], 0), state)
        total = total + stacked[W:] + roots[k][:, W:]
        state = stacked[:W] + maps[k][:, W:]
        states.append(state)
    carry[...] = pick(place, *states[:4])
    for other in range(4):
        root[other] = total
    solve_out[...] = after(solve[...], before_low[...])
    one = mul3(ahead[...], pick(place, backs[0], backs[0], backs[1], backs[2]))
    sent[:, :W] = ahead[...]
    sent[:, W : 2 * W] = one
    sent[:, 2 * W :] = mul3(one, pick(place, backs[0], backs[0], backs[0], backs[1]))


def sum_kernel(parts, out):
    total = (parts[0] + parts[1]) + (parts[2] + parts[3])
    for other in range(8 * SHARES):
        out[other] = total


def root_kernel(
    where, sums, rhs_root, root_lower, root_upper, carry, solve, ends, uinv, ulink, uroot,
    own_root, plain, offset,
):
    core, both = where[3], where[5] == 2
    order = [(k * 4 + x) * 2 + c for c in range(2) for x in range(4) for k in range(SHARES)]
    summed = jnp.concatenate([sums[k] for k in order], 0)
    inner = mul2(root_lower[...], rhs_root[...].astype(F32) - summed)
    root = mul2(root_upper[...], inner)
    solved = mul3(solve[:, :W], carry[...]) + solve[:, W:]
    first, second = uinv[0, 0].astype(F32), uinv[0, 1].astype(F32)
    link = jnp.where(both, -dot(uinv[0, 0], ulink[0, 0]), F32(0))
    over = mul3(link, second)
    moved = mul3(ends[...], jnp.concatenate([first, over], 1))
    parts = mul2(jnp.concatenate([uroot[0, 0], uroot[0, 1]], 0), root)
    inner = [(solved - parts)[W * slot : W * slot + W] for slot in range(2)]
    on_first = mul3(jnp.concatenate([first, moved[:, :W]], 0), inner[0])
    on_second = mul3(jnp.concatenate([over, moved[:, W:], second], 0), inner[1])
    whole = on_first + on_second[: 2 * W]
    plain[:W] = whole[:W]
    plain[W:] = on_second[2 * W :]
    turned = whole[:W].T
    carried = jnp.where(core == 0, whole[:W], whole[W:]).T
    for other in range(8):
        rows = slice(16 * other, 16 * other + 16)
        offset[other, :16] = carried[rows]
        offset[other, 16:] = turned[rows]
    columns = lax.broadcasted_iota(jnp.int32, (W, 512), 0)
    own_root[...] = jnp.sum(jnp.where(columns == where[4], root.T, F32(0)), 0, keepdims=True)


def chip_offsets(parts):
    return [parts[2 * k, :16] + parts[2 * k + 1, :16] for k in range(4)]


def offset_kernel(where, parts, gather, sent, out):
    state = mul3(jnp.concatenate(chip_offsets(parts), 1), gather[...])
    moved = mul3(state, sent[...])
    values = [state, moved[:, :W], moved[:, W : 2 * W], moved[:, 2 * W :]]
    for other in range(4):
        value = pick(where[0] - other, *values)
        for k in range(4):
            out[4 * other + k] = value


def carry_kernel(where, planes, within, parts, spread, out):
    group = where[0]
    state = jnp.zeros((16, W), F32)
    for k in range(4, 16):
        state = state + jnp.where(k // 4 > group, planes[k], F32(0))
    offsets = [planes[4 * group + k] for k in range(1, 4)]
    state = mul3(jnp.concatenate([state] + offsets, 1), within[...])
    chips = chip_offsets(parts)
    moved = mul3(chips[3], spread[:, 3 * W : 5 * W])
    plain = [
        chips[1] + mul3(chips[2], spread[:, 5 * W :]) + moved[:, :W],
        chips[2] + moved[:, W:],
        chips[3],
    ]
    moved = mul3(state, spread[:, : 3 * W])
    states = [plain[k] + moved[:, W * k : W * k + W] for k in range(3)] + [state]
    for k in range(4):
        for core in range(2):
            out[2 * k + core, :16] = states[k]
            out[2 * k + core, 16:] = parts[2 * k + 1, 16:]


def answer_kernel(where, parts, last, plain, out):
    state = jnp.concatenate([parts[k, :16] for k in range(8)], 0).T
    other = jnp.concatenate([parts[k, 16:] for k in range(8)], 0).T
    made = mul3(last[...], jnp.concatenate([state, other], 0)) + plain[...]
    out[0, 0] = made[:W]
    out[0, 1] = jnp.where(where[5] == 2, made[W:], F32(0))


def call(kernel, inputs, shapes, fetched=False):
    vmem = pl.BlockSpec(memory_space=pltpu.VMEM)
    smem = pl.BlockSpec(memory_space=pltpu.SMEM)
    block = pl.BlockSpec(memory_space=pltpu.HBM) if fetched else vmem
    scratch = []
    if fetched:
        scratch = [pltpu.VMEM(a.shape, a.dtype) for a in inputs if a.dtype == BF16]
        scratch.append(pltpu.SemaphoreType.DMA((len(scratch),)))
        inputs = [
            pltpu.with_memory_space_constraint(a, pltpu.HBM) if a.dtype == BF16 else a
            for a in inputs
        ]
    return pl.pallas_call(
        kernel,
        out_shape=[jax.ShapeDtypeStruct(shape, F32) for shape in shapes],
        in_specs=[
            smem if a.dtype == jnp.int32 else block if a.dtype == BF16 else vmem for a in inputs
        ],
        out_specs=[vmem] * len(shapes),
        scratch_shapes=scratch,
        compiler_params=pltpu.CompilerParams(vmem_limit_bytes=32 * 1024 * 1024),
    )(*inputs)


def on_device(
    lower_inverse,
    upper_inverse,
    lower_link,
    upper_link,
    lower_root,
    upper_root,
    rhs_blocks,
    rhs_root,
    root_lower_inverse,
    root_upper_inverse,
    live_counts,
):
    places = [lax.axis_index(axes) for axes in ("zh", LOW, "x", "c")]
    column = ((places[0] * 4 + places[1]) * 4 + places[2]) * 2 + places[3]
    where = jnp.stack(places + [column, live_counts[0, 0]]).astype(jnp.int32)
    square, wide = (W, W), (W, 2 * W)

    keep, send, ahead = call(
        slots_kernel,
        [where, lower_inverse, lower_link, rhs_blocks, upper_inverse, upper_link, lower_root],
        [(256, 256), (448, 256), (256, 256)],
        fetched=True,
    )
    pair = lax.all_gather(send, "c")
    out, solve, ends, last = call(
        chip_kernel,
        [where, keep, pair, ahead],
        [(4, 160, 256), (256, 256), square, (256, 256)],
    )
    parts = lax.all_to_all(out, "x", 0, 0, tiled=True)
    pieces = lax.all_gather(parts[:, :96], "c")
    out, before_x, gather, spread = call(
        plane_kernel, [where, parts, pieces], [(160, 256), wide, (4 * W, W), (W, 6 * W)]
    )
    parts = lax.all_gather(out, LOW)
    pieces = lax.all_gather(parts[:, :96], "c")
    out, before_low, solve, ahead, within = call(
        group_kernel,
        [where, parts, pieces, solve, before_x],
        [(96 + ROWS, 256), wide, (256, 256), square, (4 * W, W)],
    )
    parts = lax.all_gather(out, "zh")
    pieces = lax.all_gather(parts[:, :96], "c")
    root, carry, solve, sent = call(
        top_kernel,
        [where, parts, pieces, solve, before_low, ahead],
        [(4, ROWS, W), square, (256, 256), (W, 3 * W)],
    )
    parts = lax.all_to_all(root, "y", 0, 0, tiled=True)
    (root,) = call(sum_kernel, [parts], [(8 * SHARES, ROWS, W)])
    sums = lax.all_to_all(root, SHARE + ("x", "c"), 0, 0, tiled=True)
    own_root, plain, offset = call(
        root_kernel,
        [
            where, sums, rhs_root, root_lower_inverse, root_upper_inverse, carry, solve, ends,
            upper_inverse, upper_link, upper_root,
        ],
        [(1, 512), (256, W), (8, 32, W)],
    )
    parts = lax.all_to_all(offset, ("x", "c"), 0, 0, tiled=True)
    (offset,) = call(offset_kernel, [where, parts, gather, sent], [(16, 16, W)])
    planes = lax.all_to_all(offset, ("zh",) + LOW, 0, 0, tiled=True)
    (states,) = call(carry_kernel, [where, planes, within, parts, spread], [(8, 32, W)])
    states = lax.all_to_all(states, ("x", "c"), 0, 0, tiled=True)
    (answers,) = call(answer_kernel, [where, states, last, plain], [(1, 2, W, W)])
    return answers, own_root.reshape(512, 1)


def solution(mesh):
    fine = Mesh(mesh.devices.reshape(4, 2, 2, 4, 2, 4), CHAIN + ("y",))
    split = P("y", CHAIN)
    return jax.shard_map(
        on_device,
        mesh=fine,
        in_specs=(split,) * 7 + (P(), P(), P(), split),
        out_specs=(split, P(None, CHAIN)),
        check_vma=False,
    )
```

```python
import jax
import jax.numpy as jnp
from jax import lax
from jax.experimental import pallas as pl
from jax.experimental.pallas import tpu as pltpu
from jax.sharding import Mesh
from jax.sharding import PartitionSpec as P

W = 128
F32 = jnp.float32
BF16 = jnp.bfloat16
CHAIN = ("zh", "za", "zb", "x", "c")
LOW = ("za", "zb")
SHARE = ("zb",)
SHARES = 2
ROWS = 64 // SHARES


def dot(left, right):
    return jnp.dot(left, right, preferred_element_type=F32)


def halves(value):
    high = value.astype(BF16)
    return high, (value - high.astype(F32)).astype(BF16)


def mul2(exact, right):
    high, low = halves(right)
    if right.shape[1] == W:
        made = dot(exact, jnp.concatenate([high, low], 1))
        return made[:, :W] + made[:, W:]
    return dot(jnp.concatenate([exact, exact], 1), jnp.concatenate([high, low], 0))


def mul3(left, right):
    left_high, left_low = halves(left)
    right_high, right_low = halves(right)
    both = jnp.concatenate([left_high, left_low], 1)
    if right.shape[1] == W:
        upper = jnp.concatenate([right_high, right_low], 1)
        lower = jnp.concatenate([right_high, jnp.zeros_like(right_low)], 1)
        made = dot(both, jnp.concatenate([upper, lower], 0))
        return made[:, :W] + made[:, W:]
    return dot(both, jnp.concatenate([right_high, right_high], 0)) + dot(left_high, right_low)


def shift(offset):
    return jnp.concatenate([jnp.zeros_like(offset), offset], 1)


def pack(square):
    return jnp.concatenate([square[: W // 2], square[W // 2 :]], 1)


def unpack(packed):
    return jnp.concatenate([packed[:, :W], packed[:, W:]], 0)


def eye():
    rows = lax.broadcasted_iota(jnp.int32, (W, W), 0)
    cols = lax.broadcasted_iota(jnp.int32, (W, W), 1)
    return jnp.where(rows == cols, F32(1), F32(0))


def slots_kernel(
    where, linv_in, llink_in, rhs_in, uinv_in, ulink_in, lroot_in, keep, send, ahead,
    linv, llink, rhs, uinv, ulink, lroot, sems,
):
    sources = (linv_in, llink_in, rhs_in, uinv_in, ulink_in, lroot_in)
    targets = (linv, llink, rhs, uinv, ulink, lroot)
    copies = [
        pltpu.make_async_copy(source, target, sems.at[k])
        for k, (source, target) in enumerate(zip(sources, targets))
    ]
    for copy in copies:
        copy.start()
    core, both = where[3], where[5] == 2
    for copy in copies[:3]:
        copy.wait()
    maps = []
    for slot in range(2):
        made = dot(linv[0, slot], jnp.concatenate([llink[0, slot], rhs[0, slot]], 1))
        maps.append(jnp.concatenate([-made[:, :W], made[:, W:]], 1))
    chain = mul3(maps[1][:, :W], maps[0]) + shift(maps[1][:, W:])
    chain = jnp.where(both, chain, maps[0])
    send[:W] = chain
    for copy in copies[3:]:
        copy.wait()
    links = [-dot(uinv[0, slot], ulink[0, slot]) for slot in range(2)]
    back = jnp.where(both, mul3(links[0], links[1]), links[0])
    send[W : W + W // 2] = pack(back.T)
    ahead[:W] = maps[0]
    ahead[W:] = jnp.concatenate([back, links[1]], 1)
    second = jnp.where(both, chain, F32(0))
    ahead_high, ahead_low = halves(jnp.concatenate([maps[0], second], 0))
    for part, target, at in ((core, keep, 0), (1 - core, send, W + W // 2)):
        rows = pl.ds(pl.multiple_of(part * 256, 256), 256)
        blocks = jnp.concatenate([lroot[0, 0, rows], lroot[0, 1, rows]], 1)
        target[at : at + 256] = dot(blocks, ahead_high) + dot(blocks, ahead_low)


def half(core, rows):
    middle = rows.shape[0] // 2
    return jnp.where(core == 0, rows[:middle], rows[middle:])


def after(map_rows, ahead):
    return mul3(map_rows[:, :W], ahead) + shift(map_rows[:, W:])


def chip_kernel(where, keep, pair, ahead, out, solve, ends, last):
    core = where[3]
    first = core == 0
    head, tail = pair[0, :W], pair[1, :W]
    root_mine = keep[...]
    root_head = jnp.where(first, root_mine, pair[0, W + W // 2 :])
    root_tail = jnp.where(first, pair[1, W + W // 2 :], root_mine)
    slot = ahead[:W]
    made = after(jnp.concatenate([tail, slot, root_tail], 0), head)
    chain, root = made[:W], root_head + made[2 * W :]
    solve[:W] = jnp.where(first, slot, made[W : 2 * W])
    solve[W:] = jnp.where(first, head, chain)
    back_head, back_tail = [unpack(pair[k, W : W + W // 2]) for k in range(2)]
    chain_half = half(core, chain)
    back_half = half(core, pack(mul3(back_tail, back_head)))
    for other in range(4):
        out[other, :64] = chain_half
        out[other, 64:96] = back_half
        out[other, 96:] = root[64 * other : 64 * other + 64]
    ends[...] = back_head.T
    answer = jnp.concatenate([ahead[W:, :W], ahead[W:, W:]], 0)
    last[:, :W] = jnp.where(first, mul3(answer, back_tail.T), answer)
    last[:, W:] = jnp.where(first, answer, F32(0))


def compose(place, maps, roots):
    one = after(jnp.concatenate([maps[1], roots[1]], 0), maps[0])
    two = after(jnp.concatenate([maps[3], roots[3]], 0), maps[2])
    root_one, root_two = roots[0] + one[W:], roots[2] + two[W:]
    one, two = one[:W], two[:W]
    made = after(jnp.concatenate([maps[2], two, root_two], 0), one)
    start = jnp.concatenate([eye(), jnp.zeros((W, W), F32)], 1)
    before = jnp.where(
        place == 0,
        start,
        jnp.where(place == 1, maps[0], jnp.where(place == 2, one, made[:W])),
    )
    return made[W : 2 * W], root_one + made[2 * W :], before


def products(backs):
    p10, p21, p32 = [mul3(backs[k + 1], backs[k]) for k in range(3)]
    return p10, p21, p32, mul3(backs[2], p10), mul3(backs[3], p21), mul3(p32, p10)


def joined(pieces):
    maps = [jnp.concatenate([pieces[0, k, :64], pieces[1, k, :64]], 0) for k in range(4)]
    backs = [jnp.concatenate([pieces[0, k, 64:], pieces[1, k, 64:]], 0) for k in range(4)]
    return maps, [unpack(packed) for packed in backs]


def plane_kernel(where, parts, pieces, out, before, gather, spread):
    core = where[3]
    maps, backs = joined(pieces)
    chain, root, prefix = compose(where[2], maps, [parts[k, 96:] for k in range(4)])
    before[...] = prefix
    p10, p21, p32, p210, p321, total = products(backs)
    out[:64] = half(core, chain)
    out[64:96] = half(core, pack(total))
    out[96:] = root
    for k, value in enumerate((eye(), backs[0], p10, p210)):
        gather[W * k : W * k + W] = value
    for k, value in enumerate((p321, p32, backs[3], p21, backs[2], backs[1])):
        spread[:, W * k : W * k + W] = value


def pick(place, *values):
    chosen = values[-1]
    for k in reversed(range(len(values) - 1)):
        chosen = jnp.where(place == k, values[k], chosen)
    return chosen


def group_kernel(
    where, parts, pieces, solve, before_x, out, before, solve_out, ahead, within, back_ref,
):
    core, place = where[3], where[1]
    share = pl.ds(pl.multiple_of(96 + lax.rem(place, SHARES) * ROWS, ROWS), ROWS)
    maps, backs = joined(pieces)
    chain, root, prefix = compose(place, maps, [parts[k, share] for k in range(4)])
    before[...] = prefix
    p10, p21, p32, p210, p321, total = products(backs)
    out[:64] = half(core, chain)
    back_ref[...] = pack(total)
    out[64:72] = back_ref[pl.ds(pl.multiple_of(32 * core + 8 * where[2], 8), 8)]
    out[72:] = root
    solve_out[...] = after(solve[...], before_x[...])
    one, none = eye(), jnp.zeros((W, W), F32)
    ahead[...] = pick(place, one, backs[0], p10, p210)
    within[:W] = pick(place, p321, p32, backs[3], one)
    within[W : 2 * W] = pick(place, one, none)
    within[2 * W : 3 * W] = pick(place, backs[1], one, none)
    within[3 * W :] = pick(place, p21, backs[2], one, none)


def top_kernel(where, parts, pieces, solve, before_low, root, carry, solve_out):
    place = where[0]
    maps = [jnp.concatenate([pieces[0, k], pieces[1, k]], 0) for k in range(4)]
    roots = [parts[k, 72:] for k in range(4)]
    total = roots[0][:, W:]
    state = maps[0][:, W:]
    states = [jnp.zeros((W, W), F32), state]
    for k in range(1, 4):
        stacked = mul3(jnp.concatenate([maps[k][:, :W], roots[k][:, :W]], 0), state)
        total = total + stacked[W:] + roots[k][:, W:]
        state = stacked[:W] + maps[k][:, W:]
        states.append(state)
    carry[...] = pick(place, *states[:4])
    for other in range(4):
        root[other] = total
    solve_out[...] = after(solve[...], before_low[...])


def sum_kernel(parts, out):
    total = (parts[0] + parts[1]) + (parts[2] + parts[3])
    for other in range(8 * SHARES):
        out[other] = total


def root_kernel(
    where, sums, rhs_root, root_lower, root_upper, carry, solve, ends, groups, uinv, ulink,
    uroot, own_root, plain, offset,
):
    core, both = where[3], where[5] == 2
    order = [(k * 4 + x) * 2 + c for c in range(2) for x in range(4) for k in range(SHARES)]
    summed = jnp.concatenate([sums[k] for k in order], 0)
    inner = mul2(root_lower[...], rhs_root[...].astype(F32) - summed)
    root = mul2(root_upper[...], inner)
    solved = mul3(solve[:, :W], carry[...]) + solve[:, W:]
    first, second = uinv[0, 0].astype(F32), uinv[0, 1].astype(F32)
    link = jnp.where(both, -dot(uinv[0, 0], ulink[0, 0]), F32(0))
    over = mul3(link, second)
    moved = mul3(ends[...], jnp.concatenate([first, over], 1))
    parts = mul2(jnp.concatenate([uroot[0, 0], uroot[0, 1]], 0), root)
    inner = [(solved - parts)[W * slot : W * slot + W] for slot in range(2)]
    on_first = mul3(jnp.concatenate([first, moved[:, :W]], 0), inner[0])
    on_second = mul3(jnp.concatenate([over, moved[:, W:], second], 0), inner[1])
    whole = on_first + on_second[: 2 * W]
    plain[:W] = whole[:W]
    plain[W:] = on_second[2 * W :]
    turned = whole[:W].T
    carried = jnp.where(core == 0, whole[:W], whole[W:]).T
    for other in range(8):
        rows = slice(16 * other, 16 * other + 16)
        offset[other, :16] = carried[rows]
        offset[other, 16:32] = turned[rows]
        for k in range(2):
            at = 32 + 16 * k
            offset[other, at : at + 8] = groups[k + 1, 64:72, :W]
            offset[other, at + 8 : at + 16] = groups[k + 1, 64:72, W:]
    columns = lax.broadcasted_iota(jnp.int32, (W, 512), 0)
    own_root[...] = jnp.sum(jnp.where(columns == where[4], root.T, F32(0)), 0, keepdims=True)


def chip_offsets(parts):
    return [parts[2 * k, :16] + parts[2 * k + 1, :16] for k in range(4)]


def offset_kernel(where, parts, gather, ahead, out):
    backs = []
    for at in (32, 48):
        order = [2 * x + core for core in range(2) for x in range(4)]
        sides = [parts[k, at : at + 8] for k in order]
        sides += [parts[k, at + 8 : at + 16] for k in order]
        backs.append(jnp.concatenate(sides, 0))
    state = mul3(jnp.concatenate(chip_offsets(parts), 1), gather[...])
    one = mul3(state, ahead[...])
    two = mul3(one, jnp.where(where[0] == 3, backs[1], backs[0]))
    values = [state, one, two, mul3(two, backs[0])]
    for other in range(4):
        value = pick(where[0] - other, *values)
        for k in range(4):
            out[4 * other + k] = value


def carry_kernel(where, planes, within, parts, spread, out):
    group = where[0]
    state = jnp.zeros((16, W), F32)
    for k in range(4, 16):
        state = state + jnp.where(k // 4 > group, planes[k], F32(0))
    offsets = [planes[4 * group + k] for k in range(1, 4)]
    state = mul3(jnp.concatenate([state] + offsets, 1), within[...])
    chips = chip_offsets(parts)
    moved = mul3(chips[3], spread[:, 3 * W : 5 * W])
    plain = [
        chips[1] + mul3(chips[2], spread[:, 5 * W :]) + moved[:, :W],
        chips[2] + moved[:, W:],
        chips[3],
    ]
    moved = mul3(state, spread[:, : 3 * W])
    states = [plain[k] + moved[:, W * k : W * k + W] for k in range(3)] + [state]
    for k in range(4):
        for core in range(2):
            out[2 * k + core, :16] = states[k]
            out[2 * k + core, 16:] = parts[2 * k + 1, 16:32]


def answer_kernel(where, parts, last, plain, out):
    state = jnp.concatenate([parts[k, :16] for k in range(8)], 0).T
    other = jnp.concatenate([parts[k, 16:] for k in range(8)], 0).T
    made = mul3(last[...], jnp.concatenate([state, other], 0)) + plain[...]
    out[0, 0] = made[:W]
    out[0, 1] = jnp.where(where[5] == 2, made[W:], F32(0))


def call(kernel, inputs, shapes, fetched=False, scratch=()):
    vmem = pl.BlockSpec(memory_space=pltpu.VMEM)
    smem = pl.BlockSpec(memory_space=pltpu.SMEM)
    block = pl.BlockSpec(memory_space=pltpu.HBM) if fetched else vmem
    scratch = [pltpu.VMEM(shape, F32) for shape in scratch]
    if fetched:
        scratch = [pltpu.VMEM(a.shape, a.dtype) for a in inputs if a.dtype == BF16]
        scratch.append(pltpu.SemaphoreType.DMA((len(scratch),)))
        inputs = [
            pltpu.with_memory_space_constraint(a, pltpu.HBM) if a.dtype == BF16 else a
            for a in inputs
        ]
    return pl.pallas_call(
        kernel,
        out_shape=[jax.ShapeDtypeStruct(shape, F32) for shape in shapes],
        in_specs=[
            smem if a.dtype == jnp.int32 else block if a.dtype == BF16 else vmem for a in inputs
        ],
        out_specs=[vmem] * len(shapes),
        scratch_shapes=scratch,
        compiler_params=pltpu.CompilerParams(vmem_limit_bytes=32 * 1024 * 1024),
    )(*inputs)


def on_device(
    lower_inverse,
    upper_inverse,
    lower_link,
    upper_link,
    lower_root,
    upper_root,
    rhs_blocks,
    rhs_root,
    root_lower_inverse,
    root_upper_inverse,
    live_counts,
):
    places = [lax.axis_index(axes) for axes in ("zh", LOW, "x", "c")]
    column = ((places[0] * 4 + places[1]) * 4 + places[2]) * 2 + places[3]
    where = jnp.stack(places + [column, live_counts[0, 0]]).astype(jnp.int32)
    square, wide = (W, W), (W, 2 * W)

    keep, send, ahead = call(
        slots_kernel,
        [where, lower_inverse, lower_link, rhs_blocks, upper_inverse, upper_link, lower_root],
        [(256, 256), (448, 256), (256, 256)],
        fetched=True,
    )
    pair = lax.all_gather(send, "c")
    out, solve, ends, last = call(
        chip_kernel,
        [where, keep, pair, ahead],
        [(4, 160, 256), (256, 256), square, (256, 256)],
    )
    parts = lax.all_to_all(out, "x", 0, 0, tiled=True)
    pieces = lax.all_gather(parts[:, :96], "c")
    out, before_x, gather, spread = call(
        plane_kernel, [where, parts, pieces], [(160, 256), wide, (4 * W, W), (W, 6 * W)]
    )
    parts = lax.all_gather(out, LOW)
    pieces = lax.all_gather(parts[:, :96], "c")
    out, before_low, solve, ahead, within = call(
        group_kernel,
        [where, parts, pieces, solve, before_x],
        [(72 + ROWS, 256), wide, (256, 256), square, (4 * W, W)],
        scratch=[(64, 256)],
    )
    groups = lax.all_gather(out, "zh")
    pieces = lax.all_gather(groups[:, :64], "c")
    root, carry, solve = call(
        top_kernel,
        [where, groups, pieces, solve, before_low],
        [(4, ROWS, W), square, (256, 256)],
    )
    parts = lax.all_to_all(root, "y", 0, 0, tiled=True)
    (root,) = call(sum_kernel, [parts], [(8 * SHARES, ROWS, W)])
    sums = lax.all_to_all(root, SHARE + ("x", "c"), 0, 0, tiled=True)
    own_root, plain, offset = call(
        root_kernel,
        [
            where, sums, rhs_root, root_lower_inverse, root_upper_inverse, carry, solve, ends,
            groups, upper_inverse, upper_link, upper_root,
        ],
        [(1, 512), (256, W), (8, 64, W)],
    )
    parts = lax.all_to_all(offset, ("x", "c"), 0, 0, tiled=True)
    (offset,) = call(offset_kernel, [where, parts, gather, ahead], [(16, 16, W)])
    planes = lax.all_to_all(offset, ("zh",) + LOW, 0, 0, tiled=True)
    (states,) = call(carry_kernel, [where, planes, within, parts, spread], [(8, 32, W)])
    states = lax.all_to_all(states, ("x", "c"), 0, 0, tiled=True)
    (answers,) = call(answer_kernel, [where, states, last, plain], [(1, 2, W, W)])
    return answers, own_root.reshape(512, 1)


def solution(mesh):
    fine = Mesh(mesh.devices.reshape(4, 2, 2, 4, 2, 4), CHAIN + ("y",))
    split = P("y", CHAIN)
    return jax.shard_map(
        on_device,
        mesh=fine,
        in_specs=(split,) * 7 + (P(), P(), P(), split),
        out_specs=(split, P(None, CHAIN)),
        check_vma=False,
    )
```

```python
import jax
import jax.numpy as jnp
from jax import lax
from jax.experimental import pallas as pl
from jax.experimental.pallas import tpu as pltpu
from jax.sharding import Mesh
from jax.sharding import PartitionSpec as P

W = 128
F32 = jnp.float32
BF16 = jnp.bfloat16
CHAIN = ("zh", "za", "zb", "x", "c")
LOW = ("za", "zb")
SHARE = ("zb",)
SHARES = 2
ROWS = 64 // SHARES
HIGH, PLANE, CHIP, CORE, COLUMN, LIVE, ODD, PIECE = range(8)
MARKS = (8, 512)


def dot(left, right):
    return jnp.dot(left, right, preferred_element_type=F32)


def halves(value):
    high = value.astype(BF16)
    return high, (value - high.astype(F32)).astype(BF16)


def mul2(exact, right):
    high, low = halves(right)
    if right.shape[1] == W:
        made = dot(exact, jnp.concatenate([high, low], 1))
        return made[:, :W] + made[:, W:]
    return dot(jnp.concatenate([exact, exact], 1), jnp.concatenate([high, low], 0))


def mul3(left, right):
    left_high, left_low = halves(left)
    right_high, right_low = halves(right)
    both = jnp.concatenate([left_high, left_low], 1)
    if right.shape[1] == W:
        upper = jnp.concatenate([right_high, right_low], 1)
        lower = jnp.concatenate([right_high, jnp.zeros_like(right_low)], 1)
        made = dot(both, jnp.concatenate([upper, lower], 0))
        return made[:, :W] + made[:, W:]
    return dot(both, jnp.concatenate([right_high, right_high], 0)) + dot(left_high, right_low)


def shift(offset):
    return jnp.concatenate([jnp.zeros_like(offset), offset], 1)


def pack(square):
    return jnp.concatenate([square[: W // 2], square[W // 2 :]], 1)


def unpack(packed):
    return jnp.concatenate([packed[:, :W], packed[:, W:]], 0)


def choose(mark, value, one, other):
    return jnp.where(jnp.broadcast_to(mark[:, : one.shape[1]], one.shape) == value, one, other)


def pick(mark, *values):
    chosen = values[-1]
    for k in reversed(range(len(values) - 1)):
        chosen = choose(mark, k, values[k], chosen)
    return chosen


def eye():
    rows = lax.broadcasted_iota(jnp.int32, (W, W), 0)
    cols = lax.broadcasted_iota(jnp.int32, (W, W), 1)
    return jnp.where(rows == cols, F32(1), F32(0))


def slots_kernel(
    where, linv_in, llink_in, rhs_in, uinv_in, ulink_in, lroot_in, keep, send, ahead, marks,
    linv, llink, rhs, uinv, ulink, lroot, sems,
):
    sources = (linv_in, llink_in, rhs_in, uinv_in, ulink_in, lroot_in)
    targets = (linv, llink, rhs, uinv, ulink, lroot)
    copies = [
        pltpu.make_async_copy(source, target, sems.at[k])
        for k, (source, target) in enumerate(zip(sources, targets))
    ]
    for copy in copies:
        copy.start()
    core, both = where[3], where[5] == 2
    rows = lax.broadcasted_iota(jnp.int32, MARKS, 0)
    made = jnp.zeros(MARKS, jnp.int32)
    for k in range(8):
        made = jnp.where(rows == k, where[k], made)
    marks[...] = made
    for copy in copies[:3]:
        copy.wait()
    maps = []
    for slot in range(2):
        made = dot(linv[0, slot], jnp.concatenate([llink[0, slot], rhs[0, slot]], 1))
        maps.append(jnp.concatenate([-made[:, :W], made[:, W:]], 1))
    chain = mul3(maps[1][:, :W], maps[0]) + shift(maps[1][:, W:])
    chain = jnp.where(both, chain, maps[0])
    send[:W] = chain
    for copy in copies[3:]:
        copy.wait()
    links = [-dot(uinv[0, slot], ulink[0, slot]) for slot in range(2)]
    back = jnp.where(both, mul3(links[0], links[1]), links[0])
    send[W : W + W // 2] = pack(back.T)
    ahead[:W] = maps[0]
    ahead[W:] = jnp.concatenate([back, links[1]], 1)
    second = jnp.where(both, chain, F32(0))
    ahead_high, ahead_low = halves(jnp.concatenate([maps[0], second], 0))
    for part, target, at in ((core, keep, 0), (1 - core, send, W + W // 2)):
        rows = pl.ds(pl.multiple_of(part * 256, 256), 256)
        blocks = jnp.concatenate([lroot[0, 0, rows], lroot[0, 1, rows]], 1)
        target[at : at + 256] = dot(blocks, ahead_high) + dot(blocks, ahead_low)


def half(core, rows):
    middle = rows.shape[0] // 2
    return choose(core, 0, rows[:middle], rows[middle:])


def after(map_rows, ahead):
    return mul3(map_rows[:, :W], ahead) + shift(map_rows[:, W:])


def chip_kernel(marks, keep, pair, ahead, out, solve, ends, last):
    core = marks[CORE : CORE + 1]
    head, tail = pair[0, :W], pair[1, :W]
    root_mine = keep[...]
    root_head = choose(core, 0, root_mine, pair[0, W + W // 2 :])
    root_tail = choose(core, 0, pair[1, W + W // 2 :], root_mine)
    slot = ahead[:W]
    made = after(jnp.concatenate([tail, slot, root_tail], 0), head)
    chain, root = made[:W], root_head + made[2 * W :]
    solve[:W] = choose(core, 0, slot, made[W : 2 * W])
    solve[W:] = choose(core, 0, head, chain)
    back_head, back_tail = [unpack(pair[k, W : W + W // 2]) for k in range(2)]
    chain_half = half(core, chain)
    back_half = half(core, pack(mul3(back_tail, back_head)))
    for other in range(4):
        out[other, :64] = chain_half
        out[other, 64:96] = back_half
        out[other, 96:] = root[64 * other : 64 * other + 64]
    ends[...] = back_head.T
    answer = jnp.concatenate([ahead[W:, :W], ahead[W:, W:]], 0)
    last[:, :W] = choose(core, 0, mul3(answer, back_tail.T), answer)
    last[:, W:] = choose(core, 0, answer, jnp.zeros_like(answer))


def compose(place, maps, roots):
    one = after(jnp.concatenate([maps[1], roots[1]], 0), maps[0])
    two = after(jnp.concatenate([maps[3], roots[3]], 0), maps[2])
    root_one, root_two = roots[0] + one[W:], roots[2] + two[W:]
    one, two = one[:W], two[:W]
    made = after(jnp.concatenate([maps[2], two, root_two], 0), one)
    start = jnp.concatenate([eye(), jnp.zeros((W, W), F32)], 1)
    before = pick(place, start, maps[0], one, made[:W])
    return made[W : 2 * W], root_one + made[2 * W :], before


def products(backs):
    p10, p21, p32 = [mul3(backs[k + 1], backs[k]) for k in range(3)]
    return p10, p21, p32, mul3(backs[2], p10), mul3(backs[3], p21), mul3(p32, p10)


def joined(pieces):
    maps = [jnp.concatenate([pieces[0, k, :64], pieces[1, k, :64]], 0) for k in range(4)]
    backs = [jnp.concatenate([pieces[0, k, 64:], pieces[1, k, 64:]], 0) for k in range(4)]
    return maps, [unpack(packed) for packed in backs]


def plane_kernel(marks, parts, pieces, out, before, gather, spread):
    core = marks[CORE : CORE + 1]
    maps, backs = joined(pieces)
    chain, root, prefix = compose(marks[CHIP : CHIP + 1], maps, [parts[k, 96:] for k in range(4)])
    before[...] = prefix
    p10, p21, p32, p210, p321, total = products(backs)
    out[:64] = half(core, chain)
    out[64:96] = half(core, pack(total))
    out[96:] = root
    for k, value in enumerate((eye(), backs[0], p10, p210)):
        gather[W * k : W * k + W] = value
    for k, value in enumerate((p321, p32, backs[3], p21, backs[2], backs[1])):
        spread[:, W * k : W * k + W] = value


def group_kernel(
    marks, parts, pieces, solve, before_x, out, before, solve_out, ahead, within,
):
    core, place = marks[CORE : CORE + 1], marks[PLANE : PLANE + 1]
    odd = marks[ODD : ODD + 1]
    maps, backs = joined(pieces)
    roots = [choose(odd, 0, parts[k, 96 : 96 + ROWS], parts[k, 96 + ROWS :]) for k in range(4)]
    chain, root, prefix = compose(place, maps, roots)
    before[...] = prefix
    p10, p21, p32, p210, p321, total = products(backs)
    out[:64] = half(core, chain)
    packed = pack(total)
    out[64:72] = pick(marks[PIECE : PIECE + 1], *[packed[8 * k : 8 * k + 8] for k in range(8)])
    out[72:] = root
    solve_out[...] = after(solve[...], before_x[...])
    one, none = eye(), jnp.zeros((W, W), F32)
    ahead[...] = pick(place, one, backs[0], p10, p210)
    within[:W] = pick(place, p321, p32, backs[3], one)
    within[W : 2 * W] = pick(place, one, none)
    within[2 * W : 3 * W] = pick(place, backs[1], one, none)
    within[3 * W :] = pick(place, p21, backs[2], one, none)


def top_kernel(marks, parts, pieces, solve, before_low, root, carry, solve_out):
    place = marks[HIGH : HIGH + 1]
    maps = [jnp.concatenate([pieces[0, k], pieces[1, k]], 0) for k in range(4)]
    roots = [parts[k, 72:] for k in range(4)]
    total = roots[0][:, W:]
    state = maps[0][:, W:]
    states = [jnp.zeros((W, W), F32), state]
    for k in range(1, 4):
        stacked = mul3(jnp.concatenate([maps[k][:, :W], roots[k][:, :W]], 0), state)
        total = total + stacked[W:] + roots[k][:, W:]
        state = stacked[:W] + maps[k][:, W:]
        states.append(state)
    carry[...] = pick(place, *states[:4])
    for other in range(4):
        root[other] = total
    solve_out[...] = after(solve[...], before_low[...])


def sum_kernel(parts, out):
    total = (parts[0] + parts[1]) + (parts[2] + parts[3])
    for other in range(8 * SHARES):
        out[other] = total


def root_kernel(
    marks, sums, rhs_root, root_lower, root_upper, carry, solve, ends, groups, uinv, ulink,
    uroot, own_root, plain, offset,
):
    order = [(k * 4 + x) * 2 + c for c in range(2) for x in range(4) for k in range(SHARES)]
    summed = jnp.concatenate([sums[k] for k in order], 0)
    inner = mul2(root_lower[...], rhs_root[...].astype(F32) - summed)
    root = mul2(root_upper[...], inner)
    solved = mul3(solve[:, :W], carry[...]) + solve[:, W:]
    first, second = uinv[0, 0].astype(F32), uinv[0, 1].astype(F32)
    link = -dot(uinv[0, 0], ulink[0, 0])
    link = choose(marks[LIVE : LIVE + 1], 2, link, jnp.zeros_like(link))
    over = mul3(link, second)
    moved = mul3(ends[...], jnp.concatenate([first, over], 1))
    parts = mul2(jnp.concatenate([uroot[0, 0], uroot[0, 1]], 0), root)
    inner = [(solved - parts)[W * slot : W * slot + W] for slot in range(2)]
    on_first = mul3(jnp.concatenate([first, moved[:, :W]], 0), inner[0])
    on_second = mul3(jnp.concatenate([over, moved[:, W:], second], 0), inner[1])
    whole = on_first + on_second[: 2 * W]
    plain[:W] = whole[:W]
    plain[W:] = on_second[2 * W :]
    turned = whole[:W].T
    carried = choose(marks[CORE : CORE + 1], 0, whole[:W], whole[W:]).T
    for other in range(8):
        rows = slice(16 * other, 16 * other + 16)
        offset[other, :16] = carried[rows]
        offset[other, 16:32] = turned[rows]
        for k in range(2):
            at = 32 + 16 * k
            offset[other, at : at + 8] = groups[k + 1, 64:72, :W]
            offset[other, at + 8 : at + 16] = groups[k + 1, 64:72, W:]
    columns = lax.broadcasted_iota(jnp.int32, (W, 512), 0)
    own = jnp.broadcast_to(marks[COLUMN : COLUMN + 1], (W, 512)) == columns
    own_root[...] = jnp.sum(jnp.where(own, root.T, F32(0)), 0, keepdims=True)


def chip_offsets(parts):
    return [parts[2 * k, :16] + parts[2 * k + 1, :16] for k in range(4)]


def offset_kernel(marks, parts, gather, ahead, out):
    group = marks[HIGH : HIGH + 1]
    backs = []
    for at in (32, 48):
        order = [2 * x + core for core in range(2) for x in range(4)]
        sides = [parts[k, at : at + 8] for k in order]
        sides += [parts[k, at + 8 : at + 16] for k in order]
        backs.append(jnp.concatenate(sides, 0))
    state = mul3(jnp.concatenate(chip_offsets(parts), 1), gather[...])
    one = mul3(state, ahead[...])
    two = mul3(one, choose(group, 3, backs[1], backs[0]))
    values = [state, one, two, mul3(two, backs[0])]
    for other in range(4):
        value = pick(group - other, *values)
        for k in range(4):
            out[4 * other + k] = value


def carry_kernel(marks, planes, within, parts, spread, out):
    group = marks[HIGH : HIGH + 1]
    apart = jnp.broadcast_to(group[:, :W], (16, W))
    state = jnp.zeros((16, W), F32)
    for k in range(4, 16):
        state = state + jnp.where(apart < k // 4, planes[k], F32(0))
    offsets = [pick(group, *[planes[4 * g + k] for g in range(4)]) for k in range(1, 4)]
    state = mul3(jnp.concatenate([state] + offsets, 1), within[...])
    chips = chip_offsets(parts)
    moved = mul3(chips[3], spread[:, 3 * W : 5 * W])
    plain = [
        chips[1] + mul3(chips[2], spread[:, 5 * W :]) + moved[:, :W],
        chips[2] + moved[:, W:],
        chips[3],
    ]
    moved = mul3(state, spread[:, : 3 * W])
    states = [plain[k] + moved[:, W * k : W * k + W] for k in range(3)] + [state]
    for k in range(4):
        for core in range(2):
            out[2 * k + core, :16] = states[k]
            out[2 * k + core, 16:] = parts[2 * k + 1, 16:32]


def answer_kernel(marks, parts, last, plain, column, out, own_root):
    state = jnp.concatenate([parts[k, :16] for k in range(8)], 0).T
    other = jnp.concatenate([parts[k, 16:] for k in range(8)], 0).T
    made = mul3(last[...], jnp.concatenate([state, other], 0)) + plain[...]
    out[0, 0] = made[:W]
    out[0, 1] = choose(marks[LIVE : LIVE + 1], 2, made[W:], jnp.zeros_like(made[W:]))
    own_root[...] = column[...]


def call(kernel, inputs, shapes, fetched=False):
    vmem = pl.BlockSpec(memory_space=pltpu.VMEM)
    smem = pl.BlockSpec(memory_space=pltpu.SMEM)
    block = pl.BlockSpec(memory_space=pltpu.HBM) if fetched else vmem
    scratch = []
    if fetched:
        scratch = [pltpu.VMEM(a.shape, a.dtype) for a in inputs if a.dtype == BF16]
        scratch.append(pltpu.SemaphoreType.DMA((len(scratch),)))
        inputs = [
            pltpu.with_memory_space_constraint(a, pltpu.HBM) if a.dtype == BF16 else a
            for a in inputs
        ]
    return pl.pallas_call(
        kernel,
        out_shape=[
            jax.ShapeDtypeStruct(shape, jnp.int32 if shape == MARKS else F32) for shape in shapes
        ],
        in_specs=[
            smem if a.ndim == 1 else block if a.dtype == BF16 else vmem for a in inputs
        ],
        out_specs=[vmem] * len(shapes),
        scratch_shapes=scratch,
        compiler_params=pltpu.CompilerParams(vmem_limit_bytes=32 * 1024 * 1024),
    )(*inputs)


def on_device(
    lower_inverse,
    upper_inverse,
    lower_link,
    upper_link,
    lower_root,
    upper_root,
    rhs_blocks,
    rhs_root,
    root_lower_inverse,
    root_upper_inverse,
    live_counts,
):
    places = [lax.axis_index(axes) for axes in ("zh", LOW, "x", "c")]
    column = ((places[0] * 4 + places[1]) * 4 + places[2]) * 2 + places[3]
    odd, piece = lax.axis_index("zb"), 4 * places[3] + places[2]
    where = jnp.stack(places + [column, live_counts[0, 0], odd, piece]).astype(jnp.int32)
    square, wide = (W, W), (W, 2 * W)

    keep, send, ahead, marks = call(
        slots_kernel,
        [where, lower_inverse, lower_link, rhs_blocks, upper_inverse, upper_link, lower_root],
        [(256, 256), (448, 256), (256, 256), MARKS],
        fetched=True,
    )
    pair = lax.all_gather(send, "c")
    out, solve, ends, last = call(
        chip_kernel,
        [marks, keep, pair, ahead],
        [(4, 160, 256), (256, 256), square, (256, 256)],
    )
    parts = lax.all_to_all(out, "x", 0, 0, tiled=True)
    pieces = lax.all_gather(parts[:, :96], "c")
    out, before_x, gather, spread = call(
        plane_kernel, [marks, parts, pieces], [(160, 256), wide, (4 * W, W), (W, 6 * W)]
    )
    parts = lax.all_gather(out, LOW)
    pieces = lax.all_gather(parts[:, :96], "c")
    out, before_low, solve, ahead, within = call(
        group_kernel,
        [marks, parts, pieces, solve, before_x],
        [(72 + ROWS, 256), wide, (256, 256), square, (4 * W, W)],
    )
    groups = lax.all_gather(out, "zh")
    pieces = lax.all_gather(groups[:, :64], "c")
    root, carry, solve = call(
        top_kernel,
        [marks, groups, pieces, solve, before_low],
        [(4, ROWS, W), square, (256, 256)],
    )
    parts = lax.all_to_all(root, "y", 0, 0, tiled=True)
    (root,) = call(sum_kernel, [parts], [(8 * SHARES, ROWS, W)])
    sums = lax.all_to_all(root, SHARE + ("x", "c"), 0, 0, tiled=True)
    column, plain, offset = call(
        root_kernel,
        [
            marks, sums, rhs_root, root_lower_inverse, root_upper_inverse, carry, solve, ends,
            groups, upper_inverse, upper_link, upper_root,
        ],
        [(1, 512), (256, W), (8, 64, W)],
    )
    parts = lax.all_to_all(offset, ("x", "c"), 0, 0, tiled=True)
    (offset,) = call(offset_kernel, [marks, parts, gather, ahead], [(16, 16, W)])
    planes = lax.all_to_all(offset, ("zh",) + LOW, 0, 0, tiled=True)
    (states,) = call(carry_kernel, [marks, planes, within, parts, spread], [(8, 32, W)])
    states = lax.all_to_all(states, ("x", "c"), 0, 0, tiled=True)
    answers, own_root = call(
        answer_kernel, [marks, states, last, plain, column], [(1, 2, W, W), (1, 512)]
    )
    return answers, own_root.reshape(512, 1)


def solution(mesh):
    fine = Mesh(mesh.devices.reshape(4, 2, 2, 4, 2, 4), CHAIN + ("y",))
    split = P("y", CHAIN)
    return jax.shard_map(
        on_device,
        mesh=fine,
        in_specs=(split,) * 7 + (P(), P(), P(), split),
        out_specs=(split, P(None, CHAIN)),
        check_vma=False,
    )
```

```python
import jax
import jax.numpy as jnp
from jax import lax
from jax.experimental import pallas as pl
from jax.experimental.pallas import tpu as pltpu
from jax.sharding import Mesh
from jax.sharding import PartitionSpec as P

W = 128
F32 = jnp.float32
BF16 = jnp.bfloat16
CHAIN = ("zh", "za", "zb", "x", "c")
LOW = ("za", "zb")
SHARE = ("zb",)
SHARES = 2
ROWS = 64 // SHARES
HIGH, PLANE, CHIP, CORE, COLUMN, LIVE, ODD, PIECE = range(8)
MARKS = (8, 512)


def dot(left, right):
    return jnp.dot(left, right, preferred_element_type=F32)


def halves(value):
    high = value.astype(BF16)
    return high, (value - high.astype(F32)).astype(BF16)


def mul2(exact, right):
    high, low = halves(right)
    if right.shape[1] == W:
        made = dot(exact, jnp.concatenate([high, low], 1))
        return made[:, :W] + made[:, W:]
    return dot(jnp.concatenate([exact, exact], 1), jnp.concatenate([high, low], 0))


def mul3(left, right):
    left_high, left_low = halves(left)
    right_high, right_low = halves(right)
    both = jnp.concatenate([left_high, left_low], 1)
    if right.shape[1] == W:
        upper = jnp.concatenate([right_high, right_low], 1)
        lower = jnp.concatenate([right_high, jnp.zeros_like(right_low)], 1)
        made = dot(both, jnp.concatenate([upper, lower], 0))
        return made[:, :W] + made[:, W:]
    return dot(both, jnp.concatenate([right_high, right_high], 0)) + dot(left_high, right_low)


def shift(offset):
    return jnp.concatenate([jnp.zeros_like(offset), offset], 1)


def pack(square):
    return jnp.concatenate([square[: W // 2], square[W // 2 :]], 1)


def unpack(packed):
    return jnp.concatenate([packed[:, :W], packed[:, W:]], 0)


def choose(mark, value, one, other):
    return jnp.where(jnp.broadcast_to(mark[:, : one.shape[1]], one.shape) == value, one, other)


def pick(mark, *values):
    chosen = values[-1]
    for k in reversed(range(len(values) - 1)):
        chosen = choose(mark, k, values[k], chosen)
    return chosen


def eye():
    rows = lax.broadcasted_iota(jnp.int32, (W, W), 0)
    cols = lax.broadcasted_iota(jnp.int32, (W, W), 1)
    return jnp.where(rows == cols, F32(1), F32(0))


def slots_kernel(
    marks, linv_in, llink_in, rhs_in, uinv_in, ulink_in, lroot_in, keep, send, ahead,
    linv, llink, rhs, uinv, ulink, lroot, sems,
):
    sources = (linv_in, llink_in, rhs_in, uinv_in, ulink_in, lroot_in)
    targets = (linv, llink, rhs, uinv, ulink, lroot)
    copies = [
        pltpu.make_async_copy(source, target, sems.at[k])
        for k, (source, target) in enumerate(zip(sources, targets))
    ]
    for copy in copies:
        copy.start()
    core, live = marks[CORE : CORE + 1], marks[LIVE : LIVE + 1]
    for copy in copies[:3]:
        copy.wait()
    maps = []
    for slot in range(2):
        made = dot(linv[0, slot], jnp.concatenate([llink[0, slot], rhs[0, slot]], 1))
        maps.append(jnp.concatenate([-made[:, :W], made[:, W:]], 1))
    chain = mul3(maps[1][:, :W], maps[0]) + shift(maps[1][:, W:])
    chain = choose(live, 2, chain, maps[0])
    send[:W] = chain
    for copy in copies[3:]:
        copy.wait()
    links = [-dot(uinv[0, slot], ulink[0, slot]) for slot in range(2)]
    back = choose(live, 2, mul3(links[0], links[1]), links[0])
    send[W : W + W // 2] = pack(back.T)
    ahead[:W] = maps[0]
    ahead[W:] = jnp.concatenate([back, links[1]], 1)
    second = choose(live, 2, chain, jnp.zeros_like(chain))
    ahead_high, ahead_low = halves(jnp.concatenate([maps[0], second], 0))
    blocks = jnp.concatenate([lroot[0, 0], lroot[0, 1]], 1)
    made = dot(blocks, ahead_high) + dot(blocks, ahead_low)
    keep[...] = choose(core, 0, made[:256], made[256:])
    send[W + W // 2 :] = choose(core, 0, made[256:], made[:256])


def half(core, rows):
    middle = rows.shape[0] // 2
    return choose(core, 0, rows[:middle], rows[middle:])


def after(map_rows, ahead):
    return mul3(map_rows[:, :W], ahead) + shift(map_rows[:, W:])


def chip_kernel(marks, keep, pair, ahead, out, solve, ends, last):
    core = marks[CORE : CORE + 1]
    head, tail = pair[0, :W], pair[1, :W]
    root_mine = keep[...]
    root_head = choose(core, 0, root_mine, pair[0, W + W // 2 :])
    root_tail = choose(core, 0, pair[1, W + W // 2 :], root_mine)
    slot = ahead[:W]
    made = after(jnp.concatenate([tail, slot, root_tail], 0), head)
    chain, root = made[:W], root_head + made[2 * W :]
    solve[:W] = choose(core, 0, slot, made[W : 2 * W])
    solve[W:] = choose(core, 0, head, chain)
    back_head, back_tail = [unpack(pair[k, W : W + W // 2]) for k in range(2)]
    chain_half = half(core, chain)
    back_half = half(core, pack(mul3(back_tail, back_head)))
    for other in range(4):
        out[other, :64] = chain_half
        out[other, 64:96] = back_half
        out[other, 96:] = root[64 * other : 64 * other + 64]
    ends[...] = back_head.T
    answer = jnp.concatenate([ahead[W:, :W], ahead[W:, W:]], 0)
    last[:, :W] = choose(core, 0, mul3(answer, back_tail.T), answer)
    last[:, W:] = choose(core, 0, answer, jnp.zeros_like(answer))


def compose(place, maps, roots):
    one = after(jnp.concatenate([maps[1], roots[1]], 0), maps[0])
    two = after(jnp.concatenate([maps[3], roots[3]], 0), maps[2])
    root_one, root_two = roots[0] + one[W:], roots[2] + two[W:]
    one, two = one[:W], two[:W]
    made = after(jnp.concatenate([maps[2], two, root_two], 0), one)
    start = jnp.concatenate([eye(), jnp.zeros((W, W), F32)], 1)
    before = pick(place, start, maps[0], one, made[:W])
    return made[W : 2 * W], root_one + made[2 * W :], before


def products(backs):
    p10, p21, p32 = [mul3(backs[k + 1], backs[k]) for k in range(3)]
    return p10, p21, p32, mul3(backs[2], p10), mul3(backs[3], p21), mul3(p32, p10)


def joined(pieces):
    maps = [jnp.concatenate([pieces[0, k, :64], pieces[1, k, :64]], 0) for k in range(4)]
    backs = [jnp.concatenate([pieces[0, k, 64:], pieces[1, k, 64:]], 0) for k in range(4)]
    return maps, [unpack(packed) for packed in backs]


def plane_kernel(marks, parts, pieces, out, before, gather, spread):
    core = marks[CORE : CORE + 1]
    maps, backs = joined(pieces)
    chain, root, prefix = compose(marks[CHIP : CHIP + 1], maps, [parts[k, 96:] for k in range(4)])
    before[...] = prefix
    p10, p21, p32, p210, p321, total = products(backs)
    out[:64] = half(core, chain)
    out[64:96] = half(core, pack(total))
    out[96:] = root
    for k, value in enumerate((eye(), backs[0], p10, p210)):
        gather[W * k : W * k + W] = value
    for k, value in enumerate((p321, p32, backs[3], p21, backs[2], backs[1])):
        spread[:, W * k : W * k + W] = value


def group_kernel(
    marks, parts, pieces, solve, before_x, out, before, solve_out, ahead, within,
):
    core, place = marks[CORE : CORE + 1], marks[PLANE : PLANE + 1]
    odd = marks[ODD : ODD + 1]
    maps, backs = joined(pieces)
    roots = [choose(odd, 0, parts[k, 96 : 96 + ROWS], parts[k, 96 + ROWS :]) for k in range(4)]
    chain, root, prefix = compose(place, maps, roots)
    before[...] = prefix
    p10, p21, p32, p210, p321, total = products(backs)
    out[:64] = half(core, chain)
    packed = pack(total)
    out[64:72] = pick(marks[PIECE : PIECE + 1], *[packed[8 * k : 8 * k + 8] for k in range(8)])
    out[72:] = root
    solve_out[...] = after(solve[...], before_x[...])
    one, none = eye(), jnp.zeros((W, W), F32)
    ahead[...] = pick(place, one, backs[0], p10, p210)
    within[:W] = pick(place, p321, p32, backs[3], one)
    within[W : 2 * W] = pick(place, one, none)
    within[2 * W : 3 * W] = pick(place, backs[1], one, none)
    within[3 * W :] = pick(place, p21, backs[2], one, none)


def top_kernel(marks, parts, pieces, solve, before_low, root, carry, solve_out):
    place = marks[HIGH : HIGH + 1]
    maps = [jnp.concatenate([pieces[0, k], pieces[1, k]], 0) for k in range(4)]
    roots = [parts[k, 72:] for k in range(4)]
    total = roots[0][:, W:]
    state = maps[0][:, W:]
    states = [jnp.zeros((W, W), F32), state]
    for k in range(1, 4):
        stacked = mul3(jnp.concatenate([maps[k][:, :W], roots[k][:, :W]], 0), state)
        total = total + stacked[W:] + roots[k][:, W:]
        state = stacked[:W] + maps[k][:, W:]
        states.append(state)
    carry[...] = pick(place, *states[:4])
    for other in range(4):
        root[other] = total
    solve_out[...] = after(solve[...], before_low[...])


def sum_kernel(parts, out):
    total = (parts[0] + parts[1]) + (parts[2] + parts[3])
    for other in range(8 * SHARES):
        out[other] = total


def root_kernel(
    marks, sums, rhs_root, root_lower, root_upper, carry, solve, ends, groups, uinv, ulink,
    uroot, own_root, plain, offset,
):
    order = [(k * 4 + x) * 2 + c for c in range(2) for x in range(4) for k in range(SHARES)]
    summed = jnp.concatenate([sums[k] for k in order], 0)
    inner = mul2(root_lower[...], rhs_root[...].astype(F32) - summed)
    root = mul2(root_upper[...], inner)
    solved = mul3(solve[:, :W], carry[...]) + solve[:, W:]
    first, second = uinv[0, 0].astype(F32), uinv[0, 1].astype(F32)
    link = -dot(uinv[0, 0], ulink[0, 0])
    link = choose(marks[LIVE : LIVE + 1], 2, link, jnp.zeros_like(link))
    over = mul3(link, second)
    moved = mul3(ends[...], jnp.concatenate([first, over], 1))
    parts = mul2(jnp.concatenate([uroot[0, 0], uroot[0, 1]], 0), root)
    inner = [(solved - parts)[W * slot : W * slot + W] for slot in range(2)]
    on_first = mul3(jnp.concatenate([first, moved[:, :W]], 0), inner[0])
    on_second = mul3(jnp.concatenate([over, moved[:, W:], second], 0), inner[1])
    whole = on_first + on_second[: 2 * W]
    plain[:W] = whole[:W]
    plain[W:] = on_second[2 * W :]
    turned = whole[:W].T
    carried = choose(marks[CORE : CORE + 1], 0, whole[:W], whole[W:]).T
    for other in range(8):
        rows = slice(16 * other, 16 * other + 16)
        offset[other, :16] = carried[rows]
        offset[other, 16:32] = turned[rows]
        for k in range(2):
            at = 32 + 16 * k
            offset[other, at : at + 8] = groups[k + 1, 64:72, :W]
            offset[other, at + 8 : at + 16] = groups[k + 1, 64:72, W:]
    columns = lax.broadcasted_iota(jnp.int32, (W, 512), 0)
    own = jnp.broadcast_to(marks[COLUMN : COLUMN + 1], (W, 512)) == columns
    own_root[...] = jnp.sum(jnp.where(own, root.T, F32(0)), 0, keepdims=True)


def chip_offsets(parts):
    return [parts[2 * k, :16] + parts[2 * k + 1, :16] for k in range(4)]


def offset_kernel(marks, parts, gather, ahead, out):
    group = marks[HIGH : HIGH + 1]
    backs = []
    for at in (32, 48):
        order = [2 * x + core for core in range(2) for x in range(4)]
        sides = [parts[k, at : at + 8] for k in order]
        sides += [parts[k, at + 8 : at + 16] for k in order]
        backs.append(jnp.concatenate(sides, 0))
    state = mul3(jnp.concatenate(chip_offsets(parts), 1), gather[...])
    one = mul3(state, ahead[...])
    two = mul3(one, choose(group, 3, backs[1], backs[0]))
    values = [state, one, two, mul3(two, backs[0])]
    for other in range(4):
        value = pick(group - other, *values)
        for k in range(4):
            out[4 * other + k] = value


def carry_kernel(marks, planes, within, parts, spread, out):
    group = marks[HIGH : HIGH + 1]
    apart = jnp.broadcast_to(group[:, :W], (16, W))
    state = jnp.zeros((16, W), F32)
    for k in range(4, 16):
        state = state + jnp.where(apart < k // 4, planes[k], F32(0))
    offsets = [pick(group, *[planes[4 * g + k] for g in range(4)]) for k in range(1, 4)]
    state = mul3(jnp.concatenate([state] + offsets, 1), within[...])
    chips = chip_offsets(parts)
    moved = mul3(chips[3], spread[:, 3 * W : 5 * W])
    plain = [
        chips[1] + mul3(chips[2], spread[:, 5 * W :]) + moved[:, :W],
        chips[2] + moved[:, W:],
        chips[3],
    ]
    moved = mul3(state, spread[:, : 3 * W])
    states = [plain[k] + moved[:, W * k : W * k + W] for k in range(3)] + [state]
    for k in range(4):
        for core in range(2):
            out[2 * k + core, :16] = states[k]
            out[2 * k + core, 16:] = parts[2 * k + 1, 16:32]


def answer_kernel(marks, parts, last, plain, column, out, own_root):
    state = jnp.concatenate([parts[k, :16] for k in range(8)], 0).T
    other = jnp.concatenate([parts[k, 16:] for k in range(8)], 0).T
    made = mul3(last[...], jnp.concatenate([state, other], 0)) + plain[...]
    out[0, 0] = made[:W]
    out[0, 1] = choose(marks[LIVE : LIVE + 1], 2, made[W:], jnp.zeros_like(made[W:]))
    own_root[...] = column[...]


def call(kernel, inputs, shapes, fetched=False):
    vmem = pl.BlockSpec(memory_space=pltpu.VMEM)
    block = pl.BlockSpec(memory_space=pltpu.HBM) if fetched else vmem
    scratch = []
    if fetched:
        scratch = [pltpu.VMEM(a.shape, a.dtype) for a in inputs if a.dtype == BF16]
        scratch.append(pltpu.SemaphoreType.DMA((len(scratch),)))
        inputs = [
            pltpu.with_memory_space_constraint(a, pltpu.HBM) if a.dtype == BF16 else a
            for a in inputs
        ]
    return pl.pallas_call(
        kernel,
        out_shape=[jax.ShapeDtypeStruct(shape, F32) for shape in shapes],
        in_specs=[block if a.dtype == BF16 else vmem for a in inputs],
        out_specs=[vmem] * len(shapes),
        scratch_shapes=scratch,
        compiler_params=pltpu.CompilerParams(vmem_limit_bytes=32 * 1024 * 1024),
    )(*inputs)


def on_device(
    lower_inverse,
    upper_inverse,
    lower_link,
    upper_link,
    lower_root,
    upper_root,
    rhs_blocks,
    rhs_root,
    root_lower_inverse,
    root_upper_inverse,
    live_counts,
):
    places = [lax.axis_index(axes) for axes in ("zh", LOW, "x", "c")]
    column = ((places[0] * 4 + places[1]) * 4 + places[2]) * 2 + places[3]
    odd, piece = lax.axis_index("zb"), 4 * places[3] + places[2]
    marks = jnp.stack(places + [column, live_counts[0, 0], odd, piece]).astype(jnp.int32)
    marks = jnp.broadcast_to(marks[:, None], MARKS)
    square, wide = (W, W), (W, 2 * W)

    keep, send, ahead = call(
        slots_kernel,
        [marks, lower_inverse, lower_link, rhs_blocks, upper_inverse, upper_link, lower_root],
        [(256, 256), (448, 256), (256, 256)],
        fetched=True,
    )
    pair = lax.all_gather(send, "c")
    out, solve, ends, last = call(
        chip_kernel,
        [marks, keep, pair, ahead],
        [(4, 160, 256), (256, 256), square, (256, 256)],
    )
    parts = lax.all_to_all(out, "x", 0, 0, tiled=True)
    pieces = lax.all_gather(parts[:, :96], "c")
    out, before_x, gather, spread = call(
        plane_kernel, [marks, parts, pieces], [(160, 256), wide, (4 * W, W), (W, 6 * W)]
    )
    parts = lax.all_gather(out, LOW)
    pieces = lax.all_gather(parts[:, :96], "c")
    out, before_low, solve, ahead, within = call(
        group_kernel,
        [marks, parts, pieces, solve, before_x],
        [(72 + ROWS, 256), wide, (256, 256), square, (4 * W, W)],
    )
    groups = lax.all_gather(out, "zh")
    pieces = lax.all_gather(groups[:, :64], "c")
    root, carry, solve = call(
        top_kernel,
        [marks, groups, pieces, solve, before_low],
        [(4, ROWS, W), square, (256, 256)],
    )
    parts = lax.all_to_all(root, "y", 0, 0, tiled=True)
    (root,) = call(sum_kernel, [parts], [(8 * SHARES, ROWS, W)])
    sums = lax.all_to_all(root, SHARE + ("x", "c"), 0, 0, tiled=True)
    column, plain, offset = call(
        root_kernel,
        [
            marks, sums, rhs_root, root_lower_inverse, root_upper_inverse, carry, solve, ends,
            groups, upper_inverse, upper_link, upper_root,
        ],
        [(1, 512), (256, W), (8, 64, W)],
    )
    parts = lax.all_to_all(offset, ("x", "c"), 0, 0, tiled=True)
    (offset,) = call(offset_kernel, [marks, parts, gather, ahead], [(16, 16, W)])
    planes = lax.all_to_all(offset, ("zh",) + LOW, 0, 0, tiled=True)
    (states,) = call(carry_kernel, [marks, planes, within, parts, spread], [(8, 32, W)])
    states = lax.all_to_all(states, ("x", "c"), 0, 0, tiled=True)
    answers, own_root = call(
        answer_kernel, [marks, states, last, plain, column], [(1, 2, W, W), (1, 512)]
    )
    return answers, own_root.reshape(512, 1)


def solution(mesh):
    fine = Mesh(mesh.devices.reshape(4, 2, 2, 4, 2, 4), CHAIN + ("y",))
    split = P("y", CHAIN)
    return jax.shard_map(
        on_device,
        mesh=fine,
        in_specs=(split,) * 7 + (P(), P(), P(), split),
        out_specs=(split, P(None, CHAIN)),
        check_vma=False,
    )
```

```python
import jax
import jax.numpy as jnp
from jax import lax
from jax.experimental import pallas as pl
from jax.experimental.pallas import tpu as pltpu
from jax.sharding import Mesh
from jax.sharding import PartitionSpec as P

W = 128
F32 = jnp.float32
BF16 = jnp.bfloat16
CHAIN = ("zh", "za", "zb", "x", "c")
LOW = ("za", "zb")
SHARE = ("zb",)
SHARES = 2
ROWS = 64 // SHARES
HIGH, PLANE, CHIP, CORE, COLUMN, LIVE, ODD, PIECE = range(8)
MARKS = (8, 512)


def dot(left, right):
    return jnp.dot(left, right, preferred_element_type=F32)


def halves(value):
    high = value.astype(BF16)
    return high, (value - high.astype(F32)).astype(BF16)


def mul2(exact, right):
    high, low = halves(right)
    if right.shape[1] == W:
        made = dot(exact, jnp.concatenate([high, low], 1))
        return made[:, :W] + made[:, W:]
    return dot(jnp.concatenate([exact, exact], 1), jnp.concatenate([high, low], 0))


def mul3(left, right):
    left_high, left_low = halves(left)
    right_high, right_low = halves(right)
    both = jnp.concatenate([left_high, left_low], 1)
    if right.shape[1] == W:
        upper = jnp.concatenate([right_high, right_low], 1)
        lower = jnp.concatenate([right_high, jnp.zeros_like(right_low)], 1)
        made = dot(both, jnp.concatenate([upper, lower], 0))
        return made[:, :W] + made[:, W:]
    return dot(both, jnp.concatenate([right_high, right_high], 0)) + dot(left_high, right_low)


def shift(offset):
    return jnp.concatenate([jnp.zeros_like(offset), offset], 1)


def pack(square):
    return jnp.concatenate([square[: W // 2], square[W // 2 :]], 1)


def unpack(packed):
    return jnp.concatenate([packed[:, :W], packed[:, W:]], 0)


def choose(mark, value, one, other):
    return jnp.where(jnp.broadcast_to(mark[:, : one.shape[1]], one.shape) == value, one, other)


def pick(mark, *values):
    chosen = values[-1]
    for k in reversed(range(len(values) - 1)):
        chosen = choose(mark, k, values[k], chosen)
    return chosen


def eye():
    rows = lax.broadcasted_iota(jnp.int32, (W, W), 0)
    cols = lax.broadcasted_iota(jnp.int32, (W, W), 1)
    return jnp.where(rows == cols, F32(1), F32(0))


def slots_kernel(
    marks, linv_in, llink_in, rhs_in, uinv_in, ulink_in, lroot_in, keep, send, ahead,
    linv, llink, rhs, uinv, ulink, lroot, sems,
):
    sources = (linv_in, llink_in, rhs_in, uinv_in, ulink_in, lroot_in)
    targets = (linv, llink, rhs, uinv, ulink, lroot)
    copies = [
        pltpu.make_async_copy(source, target, sems.at[k])
        for k, (source, target) in enumerate(zip(sources, targets))
    ]
    for copy in copies:
        copy.start()
    core, live = marks[CORE : CORE + 1], marks[LIVE : LIVE + 1]
    for copy in copies[:3]:
        copy.wait()
    maps = []
    for slot in range(2):
        made = dot(linv[0, slot], jnp.concatenate([llink[0, slot], rhs[0, slot]], 1))
        maps.append(jnp.concatenate([-made[:, :W], made[:, W:]], 1))
    chain = mul3(maps[1][:, :W], maps[0]) + shift(maps[1][:, W:])
    chain = choose(live, 2, chain, maps[0])
    send[:W] = chain
    for copy in copies[3:]:
        copy.wait()
    links = [-dot(uinv[0, slot], ulink[0, slot]) for slot in range(2)]
    back = choose(live, 2, mul3(links[0], links[1]), links[0])
    send[W : W + W // 2] = pack(back.T)
    ahead[:W] = maps[0]
    ahead[W:] = jnp.concatenate([back, links[1]], 1)
    second = choose(live, 2, chain, jnp.zeros_like(chain))
    ahead_high, ahead_low = halves(jnp.concatenate([maps[0], second], 0))
    blocks = jnp.concatenate([lroot[0, 0], lroot[0, 1]], 1)
    made = dot(blocks, ahead_high) + dot(blocks, ahead_low)
    keep[...] = choose(core, 0, made[:256], made[256:])
    send[W + W // 2 :] = choose(core, 0, made[256:], made[:256])


def half(core, rows):
    middle = rows.shape[0] // 2
    return choose(core, 0, rows[:middle], rows[middle:])


def after(map_rows, ahead):
    return mul3(map_rows[:, :W], ahead) + shift(map_rows[:, W:])


def chip_kernel(marks, keep, pair, ahead, out, solve, ends, last):
    core = marks[CORE : CORE + 1]
    head, tail = pair[0, :W], pair[1, :W]
    root_mine = keep[...]
    root_head = choose(core, 0, root_mine, pair[0, W + W // 2 :])
    root_tail = choose(core, 0, pair[1, W + W // 2 :], root_mine)
    slot = ahead[:W]
    made = after(jnp.concatenate([tail, slot, root_tail], 0), head)
    chain, root = made[:W], root_head + made[2 * W :]
    solve[:W] = choose(core, 0, slot, made[W : 2 * W])
    solve[W:] = choose(core, 0, head, chain)
    back_head, back_tail = [unpack(pair[k, W : W + W // 2]) for k in range(2)]
    chain_half = half(core, chain)
    back_half = half(core, pack(mul3(back_tail, back_head)))
    for other in range(4):
        out[other, :64] = chain_half
        out[other, 64:96] = back_half
        out[other, 96:] = root[64 * other : 64 * other + 64]
    ends[...] = back_head.T
    answer = jnp.concatenate([ahead[W:, :W], ahead[W:, W:]], 0)
    last[:, :W] = choose(core, 0, mul3(answer, back_tail.T), answer)
    last[:, W:] = choose(core, 0, answer, jnp.zeros_like(answer))


def compose(place, maps, roots):
    one = after(jnp.concatenate([maps[1], roots[1]], 0), maps[0])
    two = after(jnp.concatenate([maps[3], roots[3]], 0), maps[2])
    root_one, root_two = roots[0] + one[W:], roots[2] + two[W:]
    one, two = one[:W], two[:W]
    made = after(jnp.concatenate([maps[2], two, root_two], 0), one)
    start = jnp.concatenate([eye(), jnp.zeros((W, W), F32)], 1)
    before = pick(place, start, maps[0], one, made[:W])
    return made[W : 2 * W], root_one + made[2 * W :], before


def products(backs):
    p10, p21, p32 = [mul3(backs[k + 1], backs[k]) for k in range(3)]
    return p10, p21, p32, mul3(backs[2], p10), mul3(backs[3], p21), mul3(p32, p10)


def joined(pieces):
    maps = [jnp.concatenate([pieces[0, k, :64], pieces[1, k, :64]], 0) for k in range(4)]
    backs = [jnp.concatenate([pieces[0, k, 64:], pieces[1, k, 64:]], 0) for k in range(4)]
    return maps, [unpack(packed) for packed in backs]


def plane_kernel(marks, parts, pieces, out, before, gather, spread):
    core = marks[CORE : CORE + 1]
    maps, backs = joined(pieces)
    chain, root, prefix = compose(marks[CHIP : CHIP + 1], maps, [parts[k, 96:] for k in range(4)])
    before[...] = prefix
    p10, p21, p32, p210, p321, total = products(backs)
    out[:64] = half(core, chain)
    out[64:96] = half(core, pack(total))
    out[96:] = root
    for k, value in enumerate((eye(), backs[0], p10, p210)):
        gather[W * k : W * k + W] = value
    for k, value in enumerate((p321, p32, backs[3], p21, backs[2], backs[1])):
        spread[:, W * k : W * k + W] = value


def group_kernel(
    marks, parts, pieces, solve, before_x, out, before, solve_out, ahead, within,
):
    core, place = marks[CORE : CORE + 1], marks[PLANE : PLANE + 1]
    odd = marks[ODD : ODD + 1]
    maps, backs = joined(pieces)
    roots = [choose(odd, 0, parts[k, 96 : 96 + ROWS], parts[k, 96 + ROWS :]) for k in range(4)]
    chain, root, prefix = compose(place, maps, roots)
    before[...] = prefix
    p10, p21, p32, p210, p321, total = products(backs)
    out[:64] = half(core, chain)
    packed = pack(total)
    out[64:72] = pick(marks[PIECE : PIECE + 1], *[packed[8 * k : 8 * k + 8] for k in range(8)])
    out[72:] = root
    solve_out[...] = after(solve[...], before_x[...])
    one, none = eye(), jnp.zeros((W, W), F32)
    ahead[...] = pick(place, one, backs[0], p10, p210)
    within[:W] = pick(place, p321, p32, backs[3], one)
    within[W : 2 * W] = pick(place, one, none)
    within[2 * W : 3 * W] = pick(place, backs[1], one, none)
    within[3 * W :] = pick(place, p21, backs[2], one, none)


def top_kernel(marks, parts, pieces, solve, before_low, root, carry, solve_out):
    place = marks[HIGH : HIGH + 1]
    maps = [jnp.concatenate([pieces[0, k], pieces[1, k]], 0) for k in range(4)]
    roots = [parts[k, 72:] for k in range(4)]
    total = roots[0][:, W:]
    state = maps[0][:, W:]
    states = [jnp.zeros((W, W), F32), state]
    for k in range(1, 4):
        stacked = mul3(jnp.concatenate([maps[k][:, :W], roots[k][:, :W]], 0), state)
        total = total + stacked[W:] + roots[k][:, W:]
        state = stacked[:W] + maps[k][:, W:]
        states.append(state)
    carry[...] = pick(place, *states[:4])
    for other in range(8):
        root[other] = total
    solve_out[...] = after(solve[...], before_low[...])


def sum_kernel(parts, out):
    rows = []
    for core in range(2):
        a, b, c, d = [parts[2 * layer + core] for layer in range(4)]
        rows.append((a + b) + (c + d))
    total = jnp.concatenate(rows, 0)
    for other in range(8):
        out[other] = total


def root_kernel(
    marks, sums, rhs_root, root_lower, root_upper, carry, solve, ends, groups, uinv, ulink,
    uroot, own_root, plain, offset,
):
    order = [(k * 4 + x, c) for c in range(2) for x in range(4) for k in range(SHARES)]
    summed = jnp.concatenate([sums[k, ROWS * c : ROWS * c + ROWS] for k, c in order], 0)
    inner = mul2(root_lower[...], rhs_root[...].astype(F32) - summed)
    root = mul2(root_upper[...], inner)
    solved = mul3(solve[:, :W], carry[...]) + solve[:, W:]
    first, second = uinv[0, 0].astype(F32), uinv[0, 1].astype(F32)
    link = -dot(uinv[0, 0], ulink[0, 0])
    link = choose(marks[LIVE : LIVE + 1], 2, link, jnp.zeros_like(link))
    over = mul3(link, second)
    moved = mul3(ends[...], jnp.concatenate([first, over], 1))
    parts = mul2(jnp.concatenate([uroot[0, 0], uroot[0, 1]], 0), root)
    inner = [(solved - parts)[W * slot : W * slot + W] for slot in range(2)]
    on_first = mul3(jnp.concatenate([first, moved[:, :W]], 0), inner[0])
    on_second = mul3(jnp.concatenate([over, moved[:, W:], second], 0), inner[1])
    whole = on_first + on_second[: 2 * W]
    plain[:W] = whole[:W]
    plain[W:] = on_second[2 * W :]
    turned = whole[:W].T
    carried = choose(marks[CORE : CORE + 1], 0, whole[:W], whole[W:]).T
    for other in range(8):
        rows = slice(16 * other, 16 * other + 16)
        offset[other, :16] = carried[rows]
        offset[other, 16:32] = turned[rows]
        for k in range(2):
            at = 32 + 16 * k
            offset[other, at : at + 8] = groups[k + 1, 64:72, :W]
            offset[other, at + 8 : at + 16] = groups[k + 1, 64:72, W:]
    columns = lax.broadcasted_iota(jnp.int32, (W, 512), 0)
    own = jnp.broadcast_to(marks[COLUMN : COLUMN + 1], (W, 512)) == columns
    own_root[...] = jnp.sum(jnp.where(own, root.T, F32(0)), 0, keepdims=True)


def chip_offsets(parts):
    return [parts[2 * k, :16] + parts[2 * k + 1, :16] for k in range(4)]


def offset_kernel(marks, parts, gather, ahead, out):
    group = marks[HIGH : HIGH + 1]
    backs = []
    for at in (32, 48):
        order = [2 * x + core for core in range(2) for x in range(4)]
        sides = [parts[k, at : at + 8] for k in order]
        sides += [parts[k, at + 8 : at + 16] for k in order]
        backs.append(jnp.concatenate(sides, 0))
    state = mul3(jnp.concatenate(chip_offsets(parts), 1), gather[...])
    one = mul3(state, ahead[...])
    two = mul3(one, choose(group, 3, backs[1], backs[0]))
    values = [state, one, two, mul3(two, backs[0])]
    for other in range(4):
        value = pick(group - other, *values)
        for k in range(4):
            out[4 * other + k] = value


def carry_kernel(marks, planes, within, parts, spread, out):
    group = marks[HIGH : HIGH + 1]
    apart = jnp.broadcast_to(group[:, :W], (16, W))
    state = jnp.zeros((16, W), F32)
    for k in range(4, 16):
        state = state + jnp.where(apart < k // 4, planes[k], F32(0))
    offsets = [pick(group, *[planes[4 * g + k] for g in range(4)]) for k in range(1, 4)]
    state = mul3(jnp.concatenate([state] + offsets, 1), within[...])
    chips = chip_offsets(parts)
    moved = mul3(chips[3], spread[:, 3 * W : 5 * W])
    plain = [
        chips[1] + mul3(chips[2], spread[:, 5 * W :]) + moved[:, :W],
        chips[2] + moved[:, W:],
        chips[3],
    ]
    moved = mul3(state, spread[:, : 3 * W])
    states = [plain[k] + moved[:, W * k : W * k + W] for k in range(3)] + [state]
    for k in range(4):
        for core in range(2):
            out[2 * k + core, :16] = states[k]
            out[2 * k + core, 16:] = parts[2 * k + 1, 16:32]


def answer_kernel(marks, parts, last, plain, column, out, own_root):
    state = jnp.concatenate([parts[k, :16] for k in range(8)], 0).T
    other = jnp.concatenate([parts[k, 16:] for k in range(8)], 0).T
    made = mul3(last[...], jnp.concatenate([state, other], 0)) + plain[...]
    out[0, 0] = made[:W]
    out[0, 1] = choose(marks[LIVE : LIVE + 1], 2, made[W:], jnp.zeros_like(made[W:]))
    own_root[...] = column[...]


def call(kernel, inputs, shapes, fetched=False):
    vmem = pl.BlockSpec(memory_space=pltpu.VMEM)
    block = pl.BlockSpec(memory_space=pltpu.HBM) if fetched else vmem
    scratch = []
    if fetched:
        scratch = [pltpu.VMEM(a.shape, a.dtype) for a in inputs if a.dtype == BF16]
        scratch.append(pltpu.SemaphoreType.DMA((len(scratch),)))
        inputs = [
            pltpu.with_memory_space_constraint(a, pltpu.HBM) if a.dtype == BF16 else a
            for a in inputs
        ]
    return pl.pallas_call(
        kernel,
        out_shape=[jax.ShapeDtypeStruct(shape, F32) for shape in shapes],
        in_specs=[block if a.dtype == BF16 else vmem for a in inputs],
        out_specs=[vmem] * len(shapes),
        scratch_shapes=scratch,
        compiler_params=pltpu.CompilerParams(vmem_limit_bytes=32 * 1024 * 1024),
    )(*inputs)


def on_device(
    lower_inverse,
    upper_inverse,
    lower_link,
    upper_link,
    lower_root,
    upper_root,
    rhs_blocks,
    rhs_root,
    root_lower_inverse,
    root_upper_inverse,
    live_counts,
):
    places = [lax.axis_index(axes) for axes in ("zh", LOW, "x", "c")]
    column = ((places[0] * 4 + places[1]) * 4 + places[2]) * 2 + places[3]
    odd, piece = lax.axis_index("zb"), 4 * places[3] + places[2]
    marks = jnp.stack(places + [column, live_counts[0, 0], odd, piece]).astype(jnp.int32)
    marks = jnp.broadcast_to(marks[:, None], MARKS)
    square, wide = (W, W), (W, 2 * W)

    keep, send, ahead = call(
        slots_kernel,
        [marks, lower_inverse, lower_link, rhs_blocks, upper_inverse, upper_link, lower_root],
        [(256, 256), (448, 256), (256, 256)],
        fetched=True,
    )
    pair = lax.all_gather(send, "c")
    out, solve, ends, last = call(
        chip_kernel,
        [marks, keep, pair, ahead],
        [(4, 160, 256), (256, 256), square, (256, 256)],
    )
    parts = lax.all_to_all(out, "x", 0, 0, tiled=True)
    pieces = lax.all_gather(parts[:, :96], "c")
    out, before_x, gather, spread = call(
        plane_kernel, [marks, parts, pieces], [(160, 256), wide, (4 * W, W), (W, 6 * W)]
    )
    parts = lax.all_gather(out, LOW)
    pieces = lax.all_gather(parts[:, :96], "c")
    out, before_low, solve, ahead, within = call(
        group_kernel,
        [marks, parts, pieces, solve, before_x],
        [(72 + ROWS, 256), wide, (256, 256), square, (4 * W, W)],
    )
    groups = lax.all_gather(out, "zh")
    pieces = lax.all_gather(groups[:, :64], "c")
    root, carry, solve = call(
        top_kernel,
        [marks, groups, pieces, solve, before_low],
        [(8, ROWS, W), square, (256, 256)],
    )
    parts = lax.all_to_all(root, ("y", "c"), 0, 0, tiled=True)
    (root,) = call(sum_kernel, [parts], [(8, 2 * ROWS, W)])
    sums = lax.all_to_all(root, SHARE + ("x",), 0, 0, tiled=True)
    column, plain, offset = call(
        root_kernel,
        [
            marks, sums, rhs_root, root_lower_inverse, root_upper_inverse, carry, solve, ends,
            groups, upper_inverse, upper_link, upper_root,
        ],
        [(1, 512), (256, W), (8, 64, W)],
    )
    parts = lax.all_to_all(offset, ("x", "c"), 0, 0, tiled=True)
    (offset,) = call(offset_kernel, [marks, parts, gather, ahead], [(16, 16, W)])
    planes = lax.all_to_all(offset, ("zh",) + LOW, 0, 0, tiled=True)
    (states,) = call(carry_kernel, [marks, planes, within, parts, spread], [(8, 32, W)])
    states = lax.all_to_all(states, ("x", "c"), 0, 0, tiled=True)
    answers, own_root = call(
        answer_kernel, [marks, states, last, plain, column], [(1, 2, W, W), (1, 512)]
    )
    return answers, own_root.reshape(512, 1)


def solution(mesh):
    fine = Mesh(mesh.devices.reshape(4, 2, 2, 4, 2, 4), CHAIN + ("y",))
    split = P("y", CHAIN)
    return jax.shard_map(
        on_device,
        mesh=fine,
        in_specs=(split,) * 7 + (P(), P(), P(), split),
        out_specs=(split, P(None, CHAIN)),
        check_vma=False,
    )
```

```python
import jax
import jax.numpy as jnp
from jax import lax
from jax.experimental import pallas as pl
from jax.experimental.pallas import tpu as pltpu
from jax.sharding import Mesh
from jax.sharding import PartitionSpec as P

W = 128
F32 = jnp.float32
BF16 = jnp.bfloat16
CHAIN = ("zh", "za", "zb", "x", "c")
LOW = ("za", "zb")
SHARE = ("zb",)
SHARES = 2
ROWS = 64 // SHARES
HIGH, PLANE, CHIP, CORE, COLUMN, LIVE, ODD, PIECE = range(8)
MARKS = (8, 512)


def dot(left, right):
    return jnp.dot(left, right, preferred_element_type=F32)


def halves(value):
    high = value.astype(BF16)
    return high, (value - high.astype(F32)).astype(BF16)


def mul2(exact, right):
    high, low = halves(right)
    if right.shape[1] == W:
        made = dot(exact, jnp.concatenate([high, low], 1))
        return made[:, :W] + made[:, W:]
    return dot(jnp.concatenate([exact, exact], 1), jnp.concatenate([high, low], 0))


def mul3(left, right):
    left_high, left_low = halves(left)
    right_high, right_low = halves(right)
    both = jnp.concatenate([left_high, left_low], 1)
    if right.shape[1] == W:
        upper = jnp.concatenate([right_high, right_low], 1)
        lower = jnp.concatenate([right_high, jnp.zeros_like(right_low)], 1)
        made = dot(both, jnp.concatenate([upper, lower], 0))
        return made[:, :W] + made[:, W:]
    return dot(both, jnp.concatenate([right_high, right_high], 0)) + dot(left_high, right_low)


def shift(offset):
    return jnp.concatenate([jnp.zeros_like(offset), offset], 1)


def pack(square):
    return jnp.concatenate([square[: W // 2], square[W // 2 :]], 1)


def unpack(packed):
    return jnp.concatenate([packed[:, :W], packed[:, W:]], 0)


def choose(mark, value, one, other):
    return jnp.where(jnp.broadcast_to(mark[:, : one.shape[1]], one.shape) == value, one, other)


def pick(mark, *values):
    chosen = values[-1]
    for k in reversed(range(len(values) - 1)):
        chosen = choose(mark, k, values[k], chosen)
    return chosen


def eye():
    rows = lax.broadcasted_iota(jnp.int32, (W, W), 0)
    cols = lax.broadcasted_iota(jnp.int32, (W, W), 1)
    return jnp.where(rows == cols, F32(1), F32(0))


def slots_kernel(
    marks, linv_in, llink_in, rhs_in, uinv_in, ulink_in, lroot_in, keep, send, ahead,
    linv, llink, rhs, uinv, ulink, lroot, sems,
):
    sources = (linv_in, llink_in, rhs_in, uinv_in, ulink_in, lroot_in)
    targets = (linv, llink, rhs, uinv, ulink, lroot)
    copies = [
        pltpu.make_async_copy(source, target, sems.at[k])
        for k, (source, target) in enumerate(zip(sources, targets))
    ]
    for copy in copies:
        copy.start()
    core, live = marks[CORE : CORE + 1], marks[LIVE : LIVE + 1]
    for copy in copies[:3]:
        copy.wait()
    maps = []
    for slot in range(2):
        made = dot(linv[0, slot], jnp.concatenate([llink[0, slot], rhs[0, slot]], 1))
        maps.append(jnp.concatenate([-made[:, :W], made[:, W:]], 1))
    chain = mul3(maps[1][:, :W], maps[0]) + shift(maps[1][:, W:])
    chain = choose(live, 2, chain, maps[0])
    send[:W] = chain
    for copy in copies[3:]:
        copy.wait()
    links = [-dot(uinv[0, slot], ulink[0, slot]) for slot in range(2)]
    back = choose(live, 2, mul3(links[0], links[1]), links[0])
    send[W : W + W // 2] = pack(back.T)
    ahead[:W] = maps[0]
    ahead[W:] = jnp.concatenate([back, links[1]], 1)
    second = choose(live, 2, chain, jnp.zeros_like(chain))
    ahead_high, ahead_low = halves(jnp.concatenate([maps[0], second], 0))
    blocks = jnp.concatenate([lroot[0, 0], lroot[0, 1]], 1)
    made = dot(blocks, ahead_high) + dot(blocks, ahead_low)
    keep[...] = choose(core, 0, made[:256], made[256:])
    send[W + W // 2 :] = choose(core, 0, made[256:], made[:256])


def half(core, rows):
    middle = rows.shape[0] // 2
    return choose(core, 0, rows[:middle], rows[middle:])


def after(map_rows, ahead):
    return mul3(map_rows[:, :W], ahead) + shift(map_rows[:, W:])


def chip_kernel(marks, keep, pair, ahead, out, solve, ends, last):
    core = marks[CORE : CORE + 1]
    head, tail = pair[0, :W], pair[1, :W]
    root_mine = keep[...]
    root_head = choose(core, 0, root_mine, pair[0, W + W // 2 :])
    root_tail = choose(core, 0, pair[1, W + W // 2 :], root_mine)
    slot = ahead[:W]
    made = after(jnp.concatenate([tail, slot, root_tail], 0), head)
    chain, root = made[:W], root_head + made[2 * W :]
    solve[:W] = choose(core, 0, slot, made[W : 2 * W])
    solve[W:] = choose(core, 0, head, chain)
    back_head, back_tail = [unpack(pair[k, W : W + W // 2]) for k in range(2)]
    chain_half = half(core, chain)
    back_half = half(core, pack(mul3(back_tail, back_head)))
    for other in range(4):
        out[other, :64] = chain_half
        out[other, 64:96] = back_half
        out[other, 96:] = root[64 * other : 64 * other + 64]
    ends[...] = back_head.T
    answer = jnp.concatenate([ahead[W:, :W], ahead[W:, W:]], 0)
    last[:, :W] = choose(core, 0, mul3(answer, back_tail.T), answer)
    last[:, W:] = choose(core, 0, answer, jnp.zeros_like(answer))


def compose(place, maps, roots):
    one = after(jnp.concatenate([maps[1], roots[1]], 0), maps[0])
    two = after(jnp.concatenate([maps[3], roots[3]], 0), maps[2])
    root_one, root_two = roots[0] + one[W:], roots[2] + two[W:]
    one, two = one[:W], two[:W]
    made = after(jnp.concatenate([maps[2], two, root_two], 0), one)
    start = jnp.concatenate([eye(), jnp.zeros((W, W), F32)], 1)
    before = pick(place, start, maps[0], one, made[:W])
    return made[W : 2 * W], root_one + made[2 * W :], before


def products(backs):
    p10, p21, p32 = [mul3(backs[k + 1], backs[k]) for k in range(3)]
    return p10, p21, p32, mul3(backs[2], p10), mul3(backs[3], p21), mul3(p32, p10)


def joined(pieces):
    maps = [jnp.concatenate([pieces[0, k, :64], pieces[1, k, :64]], 0) for k in range(4)]
    backs = [jnp.concatenate([pieces[0, k, 64:], pieces[1, k, 64:]], 0) for k in range(4)]
    return maps, [unpack(packed) for packed in backs]


def plane_kernel(marks, parts, pieces, out, before, gather, spread):
    core = marks[CORE : CORE + 1]
    maps, backs = joined(pieces)
    chain, root, prefix = compose(marks[CHIP : CHIP + 1], maps, [parts[k, 96:] for k in range(4)])
    before[...] = prefix
    p10, p21, p32, p210, p321, total = products(backs)
    out[:64] = half(core, chain)
    out[64:96] = half(core, pack(total))
    out[96:] = root
    for k, value in enumerate((eye(), backs[0], p10, p210)):
        gather[W * k : W * k + W] = value
    for k, value in enumerate((p321, p32, backs[3], p21, backs[2], backs[1])):
        spread[:, W * k : W * k + W] = value


def group_kernel(
    marks, parts, pieces, solve, before_x, out, before, solve_out, ahead, within,
):
    core, place = marks[CORE : CORE + 1], marks[PLANE : PLANE + 1]
    odd = marks[ODD : ODD + 1]
    maps, backs = joined(pieces)
    roots = [choose(odd, 0, parts[k, 96 : 96 + ROWS], parts[k, 96 + ROWS :]) for k in range(4)]
    chain, root, prefix = compose(place, maps, roots)
    before[...] = prefix
    p10, p21, p32, p210, p321, total = products(backs)
    out[:64] = half(core, chain)
    packed = pack(total)
    out[64:72] = pick(marks[PIECE : PIECE + 1], *[packed[8 * k : 8 * k + 8] for k in range(8)])
    out[72:] = root
    solve_out[...] = after(solve[...], before_x[...])
    one, none = eye(), jnp.zeros((W, W), F32)
    ahead[...] = pick(place, one, backs[0], p10, p210)
    within[:W] = pick(place, p321, p32, backs[3], one)
    within[W : 2 * W] = pick(place, one, none)
    within[2 * W : 3 * W] = pick(place, backs[1], one, none)
    within[3 * W :] = pick(place, p21, backs[2], one, none)


def top_kernel(marks, parts, pieces, solve, before_low, root, carry, solve_out):
    place = marks[HIGH : HIGH + 1]
    maps = [jnp.concatenate([pieces[0, k], pieces[1, k]], 0) for k in range(3)]
    roots = [parts[k, 72:] for k in range(4)]
    total = roots[0][:, W:]
    state = maps[0][:, W:]
    states = [jnp.zeros((W, W), F32), state]
    for k in range(1, 3):
        stacked = mul3(jnp.concatenate([maps[k][:, :W], roots[k][:, :W]], 0), state)
        total = total + stacked[W:] + roots[k][:, W:]
        state = stacked[:W] + maps[k][:, W:]
        states.append(state)
    total = total + mul3(roots[3][:, :W], state) + roots[3][:, W:]
    carry[...] = pick(place, *states)
    for other in range(8):
        root[other] = total
    solve_out[...] = after(solve[...], before_low[...])


def sum_kernel(parts, out):
    rows = []
    for core in range(2):
        a, b, c, d = [parts[2 * layer + core] for layer in range(4)]
        rows.append((a + b) + (c + d))
    total = jnp.concatenate(rows, 0)
    for other in range(8):
        out[other] = total


def root_kernel(
    marks, sums, rhs_root, root_lower, root_upper, carry, solve, ends, groups, uinv, ulink,
    uroot, own_root, plain, offset,
):
    order = [(k * 4 + x, c) for c in range(2) for x in range(4) for k in range(SHARES)]
    summed = jnp.concatenate([sums[k, ROWS * c : ROWS * c + ROWS] for k, c in order], 0)
    inner = mul2(root_lower[...], rhs_root[...].astype(F32) - summed)
    root = mul2(root_upper[...], inner)
    solved = mul3(solve[:, :W], carry[...]) + solve[:, W:]
    first, second = uinv[0, 0].astype(F32), uinv[0, 1].astype(F32)
    link = -dot(uinv[0, 0], ulink[0, 0])
    link = choose(marks[LIVE : LIVE + 1], 2, link, jnp.zeros_like(link))
    over = mul3(link, second)
    moved = mul3(ends[...], jnp.concatenate([first, over], 1))
    parts = mul2(jnp.concatenate([uroot[0, 0], uroot[0, 1]], 0), root)
    inner = [(solved - parts)[W * slot : W * slot + W] for slot in range(2)]
    on_first = mul3(jnp.concatenate([first, moved[:, :W]], 0), inner[0])
    on_second = mul3(jnp.concatenate([over, moved[:, W:], second], 0), inner[1])
    whole = on_first + on_second[: 2 * W]
    plain[:W] = whole[:W]
    plain[W:] = on_second[2 * W :]
    turned = whole[:W].T
    carried = choose(marks[CORE : CORE + 1], 0, whole[:W], whole[W:]).T
    for other in range(8):
        rows = slice(16 * other, 16 * other + 16)
        offset[other, :16] = carried[rows]
        offset[other, 16:32] = turned[rows]
        for k in range(2):
            at = 32 + 16 * k
            offset[other, at : at + 8] = groups[k + 1, 64:72, :W]
            offset[other, at + 8 : at + 16] = groups[k + 1, 64:72, W:]
    columns = lax.broadcasted_iota(jnp.int32, (W, 512), 0)
    own = jnp.broadcast_to(marks[COLUMN : COLUMN + 1], (W, 512)) == columns
    own_root[...] = jnp.sum(jnp.where(own, root.T, F32(0)), 0, keepdims=True)


def chip_offsets(parts):
    return [parts[2 * k, :16] + parts[2 * k + 1, :16] for k in range(4)]


def offset_kernel(marks, parts, gather, ahead, out):
    group = marks[HIGH : HIGH + 1]
    backs = []
    for at in (32, 48):
        order = [2 * x + core for core in range(2) for x in range(4)]
        sides = [parts[k, at : at + 8] for k in order]
        sides += [parts[k, at + 8 : at + 16] for k in order]
        backs.append(jnp.concatenate(sides, 0))
    state = mul3(jnp.concatenate(chip_offsets(parts), 1), gather[...])
    one = mul3(state, ahead[...])
    two = mul3(one, choose(group, 3, backs[1], backs[0]))
    values = [state, one, two, mul3(two, backs[0])]
    for other in range(4):
        value = pick(group - other, *values)
        for k in range(4):
            out[4 * k + other] = value


def carry_kernel(marks, planes, within, parts, spread, out):
    group = marks[HIGH : HIGH + 1]
    apart = jnp.broadcast_to(group[:, :W], (16, W))
    state = jnp.zeros((16, W), F32)
    for k in range(16):
        if k % 4:
            state = state + jnp.where(apart < k % 4, planes[k], F32(0))
    offsets = [pick(group, *[planes[4 * k + g] for g in range(4)]) for k in range(1, 4)]
    state = mul3(jnp.concatenate([state] + offsets, 1), within[...])
    chips = chip_offsets(parts)
    moved = mul3(chips[3], spread[:, 3 * W : 5 * W])
    plain = [
        chips[1] + mul3(chips[2], spread[:, 5 * W :]) + moved[:, :W],
        chips[2] + moved[:, W:],
        chips[3],
    ]
    moved = mul3(state, spread[:, : 3 * W])
    states = [plain[k] + moved[:, W * k : W * k + W] for k in range(3)] + [state]
    for k in range(4):
        for core in range(2):
            out[2 * k + core, :16] = states[k]
            out[2 * k + core, 16:] = parts[2 * k + 1, 16:32]


def answer_kernel(marks, parts, last, plain, column, out, own_root):
    state = jnp.concatenate([parts[k, :16] for k in range(8)], 0).T
    other = jnp.concatenate([parts[k, 16:] for k in range(8)], 0).T
    made = mul3(last[...], jnp.concatenate([state, other], 0)) + plain[...]
    out[0, 0] = made[:W]
    out[0, 1] = choose(marks[LIVE : LIVE + 1], 2, made[W:], jnp.zeros_like(made[W:]))
    own_root[...] = column[...]


def call(kernel, inputs, shapes, fetched=False):
    vmem = pl.BlockSpec(memory_space=pltpu.VMEM)
    block = pl.BlockSpec(memory_space=pltpu.HBM) if fetched else vmem
    scratch = []
    if fetched:
        scratch = [pltpu.VMEM(a.shape, a.dtype) for a in inputs if a.dtype == BF16]
        scratch.append(pltpu.SemaphoreType.DMA((len(scratch),)))
        inputs = [
            pltpu.with_memory_space_constraint(a, pltpu.HBM) if a.dtype == BF16 else a
            for a in inputs
        ]
    return pl.pallas_call(
        kernel,
        out_shape=[jax.ShapeDtypeStruct(shape, F32) for shape in shapes],
        in_specs=[block if a.dtype == BF16 else vmem for a in inputs],
        out_specs=[vmem] * len(shapes),
        scratch_shapes=scratch,
        compiler_params=pltpu.CompilerParams(vmem_limit_bytes=32 * 1024 * 1024),
    )(*inputs)


def on_device(
    lower_inverse,
    upper_inverse,
    lower_link,
    upper_link,
    lower_root,
    upper_root,
    rhs_blocks,
    rhs_root,
    root_lower_inverse,
    root_upper_inverse,
    live_counts,
):
    places = [lax.axis_index(axes) for axes in ("zh", LOW, "x", "c")]
    column = ((places[0] * 4 + places[1]) * 4 + places[2]) * 2 + places[3]
    odd, piece = lax.axis_index("zb"), 4 * places[3] + places[2]
    marks = jnp.stack(places + [column, live_counts[0, 0], odd, piece]).astype(jnp.int32)
    marks = jnp.broadcast_to(marks[:, None], MARKS)
    square, wide = (W, W), (W, 2 * W)

    keep, send, ahead = call(
        slots_kernel,
        [marks, lower_inverse, lower_link, rhs_blocks, upper_inverse, upper_link, lower_root],
        [(256, 256), (448, 256), (256, 256)],
        fetched=True,
    )
    pair = lax.all_gather(send, "c")
    out, solve, ends, last = call(
        chip_kernel,
        [marks, keep, pair, ahead],
        [(4, 160, 256), (256, 256), square, (256, 256)],
    )
    parts = lax.all_to_all(out, "x", 0, 0, tiled=True)
    pieces = lax.all_gather(parts[:, :96], "c")
    out, before_x, gather, spread = call(
        plane_kernel, [marks, parts, pieces], [(160, 256), wide, (4 * W, W), (W, 6 * W)]
    )
    parts = lax.all_gather(out, LOW)
    pieces = lax.all_gather(parts[:, :96], "c")
    out, before_low, solve, ahead, within = call(
        group_kernel,
        [marks, parts, pieces, solve, before_x],
        [(72 + ROWS, 256), wide, (256, 256), square, (4 * W, W)],
    )
    groups = lax.all_gather(out, "zh")
    pieces = lax.all_gather(groups[:3, :64], "c")
    root, carry, solve = call(
        top_kernel,
        [marks, groups, pieces, solve, before_low],
        [(8, ROWS, W), square, (256, 256)],
    )
    parts = lax.all_to_all(root, ("y", "c"), 0, 0, tiled=True)
    (root,) = call(sum_kernel, [parts], [(8, 2 * ROWS, W)])
    sums = lax.all_to_all(root, SHARE + ("x",), 0, 0, tiled=True)
    column, plain, offset = call(
        root_kernel,
        [
            marks, sums, rhs_root, root_lower_inverse, root_upper_inverse, carry, solve, ends,
            groups, upper_inverse, upper_link, upper_root,
        ],
        [(1, 512), (256, W), (8, 64, W)],
    )
    parts = lax.all_to_all(offset, ("x", "c"), 0, 0, tiled=True)
    (offset,) = call(offset_kernel, [marks, parts, gather, ahead], [(16, 16, W)])
    planes = lax.all_to_all(offset, LOW + ("zh",), 0, 0, tiled=True)
    (states,) = call(carry_kernel, [marks, planes, within, parts, spread], [(8, 32, W)])
    states = lax.all_to_all(states, ("x", "c"), 0, 0, tiled=True)
    answers, own_root = call(
        answer_kernel, [marks, states, last, plain, column], [(1, 2, W, W), (1, 512)]
    )
    return answers, own_root.reshape(512, 1)


def solution(mesh):
    fine = Mesh(mesh.devices.reshape(4, 2, 2, 4, 2, 4), CHAIN + ("y",))
    split = P("y", CHAIN)
    return jax.shard_map(
        on_device,
        mesh=fine,
        in_specs=(split,) * 7 + (P(), P(), P(), split),
        out_specs=(split, P(None, CHAIN)),
        check_vma=False,
    )
```
